128 devices in a mesh: wide: 32 (over x, y_lo, z), narrow: 4 (over y_hi, core).
Axes of the slice: x: 4, y: 4 (y_hi: 2, y_lo: 2; y = y_hi * 2 + y_lo), z: 4, core: 2. Of those that a mesh axis runs over, the one named last changes fastest.
Arguments:
- sources: float32 [1, 2, 4096, 4096], P(None, None, 'wide', 'narrow'), may hold values from -4 to 4
- incident: float32 [1, 2, 4096, 4096], P(None, None, 'wide', 'narrow'), may hold values from -6 to 6
- contrast: float32 [2, 4096, 4096], P(None, 'wide', 'narrow'), may hold values from -5 to 5
- green: float32 [2, 8192, 8192], P(None, 'narrow', 'wide'), may hold values from -6 to 6
- angles: float32 [1024], replicated, may hold values from -3.140625 to 3.140625
- measured: float32 [1, 2, 1024], replicated, may hold values from -6 to 6
Outputs:
- residual: float32 [1, 2, 4096, 4096], P(None, None, 'wide', 'narrow')
- backprojection: float32 [1, 2, 4096, 4096], P(None, None, 'wide', 'narrow')
- data_residual: float32 [1, 2, 1024], replicated
The draws below stay inside these ranges and needn't reach their ends.
All inputs are finite; a program needn't handle non-finite values.
Results may differ from the reference program's by a relative error of at most 0.0003.
Values sent between devices are 32-bit elements; how exact they have to be, the bound alone decides.
No kernel may reach another device: no remote copies, remote signals or barrier semaphores. Data moves between devices by JAX's collectives and lax.ppermute only.
A program may use at most 128 MiB of HBM per device.

```python
import math
import jax
import jax.numpy as jnp
from jax import lax

N = 4096
R = 1024
TX = 1
M = 8192


def draw_sources(key, part):
    key = jax.random.fold_in(key, 11)
    shape = (TX, 2, N, N)
    return jax.random.truncated_normal(key, -4.0, 4.0, shape, jnp.float32)


def level_of(rng, shape, shards, low, largest):
    factor_of = 1.0
    for dim, parts in shards:
        draws = jax.random.uniform(jax.random.fold_in(jax.random.fold_in(rng, 6), dim), (parts,), jnp.float32, low / len(shards), largest / len(shards))
        factor_of = factor_of * jnp.repeat(jnp.exp(draws), shape[dim] // parts).reshape((-1,) + (1,) * (len(shape) - 1 - dim))
    return factor_of


def noise(own_key, shape, spread, most, pieces=(), kind=jnp.bfloat16):
    entries = jax.random.normal(own_key, shape, jnp.float32) * spread
    if len(pieces) > 0:
        entries = level_of(own_key, shape, pieces, -0.22, 0.18) * entries
    return jnp.clip(entries, min=-most, max=most).astype(kind)


def setup_inputs(seed: int = 0) -> dict:
    key_of = jax.random.split(jax.random.key(seed), 7)
    sources = draw_sources(jax.random.fold_in(key_of[6], 71), 0)
    incident = noise(key_of[1], (TX, 2, N, N), 1.0, 6.0, ((2, 32), (3, 4)), jnp.float32)
    contrast = noise(key_of[2], (2, N, N), 1.0, 5.0, ((1, 32), (2, 4)), jnp.float32)
    green = noise(key_of[3], (2, M, M), 1.0, 6.0, ((1, 4), (2, 32)), jnp.float32)
    angles = jnp.clip(jax.random.uniform(key_of[4], (R,), jnp.float32, -3.140625, 3.140625), -3.140625, 3.140625)
    measured = noise(key_of[5], (TX, 2, R), 1.0, 6.0, (), jnp.float32)
    return {"sources": sources, "incident": incident, "contrast": contrast, "green": green, "angles": angles, "measured": measured}


wave_step = 0.2 * math.pi
highest = lax.Precision.HIGHEST

def phase_table(direction_part):
    position = jnp.arange(N, dtype=jnp.float32) - N // 2 + 0.5
    stepped = wave_step * position
    return stepped[:, None] * direction_part[None, :]

def reference(sources, incident, contrast, green, angles, measured):
    kernel = lax.complex(green[0], green[1]).T

    def convolve(one_source):
        padded = jnp.pad(lax.complex(one_source[0], one_source[1]), ((0, N), (0, N)))
        spectrum = jnp.fft.fft2(padded)
        back = jnp.fft.ifft2(kernel * spectrum)[:N, :N]
        return jnp.stack([jnp.real(back), jnp.imag(back)])
    scattered = lax.map(convolve, sources)
    field = incident + scattered
    residual = jnp.stack([contrast[0] * field[:, 0] - contrast[1] * field[:, 1], contrast[0] * field[:, 1] + contrast[1] * field[:, 0]], 1) - sources
    row_phase = phase_table(jnp.cos(angles))
    col_phase = phase_table(jnp.sin(angles))
    row_cos = jnp.cos(row_phase)
    row_sin = -jnp.sin(row_phase)
    col_cos = jnp.cos(col_phase)
    col_sin = -jnp.sin(col_phase)
    by_real = jnp.einsum('taxy,yr->taxr', sources, col_cos, precision=highest)
    by_imag = jnp.einsum('taxy,yr->taxr', sources, col_sin, precision=highest)
    inner_real = by_real[:, 0] - by_imag[:, 1]
    inner_imag = by_imag[:, 0] + by_real[:, 1]
    total_real = lax.optimization_barrier(jnp.sum(row_cos * inner_real - row_sin * inner_imag, axis=1))
    total_imag = lax.optimization_barrier(jnp.sum(row_cos * inner_imag + row_sin * inner_real, axis=1))
    total = jnp.stack([total_real, total_imag], 1)
    data_residual = measured - total * (1.0 / N)
    rho_real = data_residual[:, 0][:, None, :]
    rho_imag = data_residual[:, 1][:, None, :]
    weight_real = row_cos * rho_real + row_sin * rho_imag
    weight_imag = row_cos * rho_imag - row_sin * rho_real
    weights = jnp.stack([weight_real, weight_imag], 1)
    back_real = jnp.einsum('taxr,yr->taxy', weights, col_cos, precision=highest)
    back_imag = jnp.einsum('taxr,yr->taxy', weights, col_sin, precision=highest)
    scale = 1.0 / math.sqrt(R)
    backprojection = jnp.stack([back_real[:, 0] + back_imag[:, 1], back_real[:, 1] - back_imag[:, 0]], 1) * scale
    return (residual, backprojection, data_residual)
```

```python
import functools
import math

import jax
import jax.numpy as jnp
import ml_dtypes
import numpy as np
from jax import lax
from jax.experimental import pallas as pl
from jax.experimental.pallas import tpu as pltpu
from jax.sharding import PartitionSpec as P

N = 4096
R = 1024
M = 8192
WIDE = 32
NARROW = 4

wave_step = 0.2 * math.pi
f32 = jnp.float32
bf16 = jnp.bfloat16
VMEM_LIMIT = 56 * 1024 * 1024


def complex_block(table):
    return np.block([[table.real, -table.imag], [table.imag, table.real]])


def halves(table):
    high = table.astype(np.float32).astype(ml_dtypes.bfloat16)
    low = (table - high.astype(np.float64)).astype(np.float32).astype(ml_dtypes.bfloat16)
    return high, low


def root(product, length, sign):
    return np.exp(sign * 2j * np.pi * (product % length) / length)


def pair(table):
    return np.stack([table.real, table.imag]).astype(np.float32)


@functools.lru_cache(None)
def tables():
    out = {}
    w = np.arange(32)
    k1 = np.arange(64)
    i = np.arange(128)
    m = np.arange(128)
    high, low = halves(complex_block(root(np.outer(k1, w), 64, -1)))
    out["t1"] = np.concatenate([high, high, low], 1)
    out["tw1"] = pair(root(np.outer(k1, i), M, -1))
    out["t2"] = np.stack(halves(complex_block(root(np.outer(m, i), 128, -1))))
    d = np.arange(128)
    s = 32 * (d % 4) + d // 4
    c1 = np.arange(256)
    out["t3"] = np.stack(halves(complex_block(root(np.outer(c1, s), 256, -1))))
    low_half = np.arange(128) < 64
    first = np.where(low_half[None, :], 1.0, root(c1, M, -1)[:, None])
    out["tw3"] = pair(first)
    out["step3"] = pair(root(2 * c1, M, -1)[:, None] * np.ones((1, 128)))
    lanes = []
    for flip in (0, 1):
        e = (np.arange(16) + 8 * flip) % 16
        lanes.append(pair(np.where(low_half[None, :], 1.0, root(e, 32, -1)[:, None])))
    out["lane3"] = np.stack(lanes)
    out["t4"] = np.stack(halves(complex_block(root(np.outer(s, c1), 256, 1))))
    out["t5"] = np.stack(halves(complex_block(root(np.outer(i, m), 128, 1))))
    lane_k1 = np.arange(128) % 64
    out["tw5"] = pair(root(np.outer(i, lane_k1), M, 1))
    inner = root(np.outer(w, k1), 64, 1) / (M * M)
    block = np.zeros((2, 2, 32, 2, 2, 64))
    for b0 in (0, 1):
        block[b0, 0, :, 0, b0, :] = inner.real
        block[b0, 0, :, 1, b0, :] = -inner.imag
        block[b0, 1, :, 0, b0, :] = inner.imag
        block[b0, 1, :, 1, b0, :] = inner.real
    out["t6"] = np.stack(halves(block.reshape(128, 256)))
    return out


def split(values):
    high = values.astype(bf16)
    low = (values - high.astype(f32)).astype(bf16)
    return high, low


def dot(a, b):
    return lax.dot_general(a, b, (((1,), (0,)), ((), ())), preferred_element_type=f32)


def dot_nt(a, b):
    return lax.dot_general(a, b, (((1,), (1,)), ((), ())), preferred_element_type=f32)


def dot3(table_high, table_low, values, product):
    high, low = split(values)
    return product(table_high, high) + (product(table_high, low) + product(table_low, high))


def times_root(value, numerator, length):
    re, im = value
    numerator %= length
    if numerator == 0:
        return value
    if 4 * numerator == length:
        return im, -re
    if 2 * numerator == length:
        return -re, -im
    if 4 * numerator == 3 * length:
        return -im, re
    if 8 * numerator == length:
        half = math.sqrt(0.5)
        return (re + im) * half, (im - re) * half
    if 8 * numerator == 3 * length:
        half = math.sqrt(0.5)
        return (im - re) * half, (-re - im) * half
    cosine = math.cos(2 * math.pi * numerator / length)
    sine = -math.sin(2 * math.pi * numerator / length)
    return re * cosine - im * sine, re * sine + im * cosine


def transform_list(values):
    count = len(values)
    if count == 1:
        return values
    if count == 2:
        (ar, ai), (br, bi) = values
        return [(ar + br, ai + bi), (ar - br, ai - bi)]
    if count == 4:
        (ar, ai), (br, bi), (cr, ci), (dr, di) = values
        pr, pi_, qr, qi = ar + cr, ai + ci, ar - cr, ai - ci
        sr, si, tr, ti = br + dr, bi + di, br - dr, bi - di
        return [(pr + sr, pi_ + si), (qr + ti, qi - tr), (pr - sr, pi_ - si), (qr - ti, qi + tr)]
    parts = [transform_list(values[start::4]) for start in range(4)]
    quarter = count // 4
    out = [None] * count
    for k in range(quarter):
        column = [times_root(parts[j][k], j * k, count) for j in range(4)]
        for q, value in enumerate(transform_list(column)):
            out[k + q * quarter] = value
    return out


def inverse_list(values):
    swapped = transform_list([(im, re) for re, im in values])
    return [(re, im) for im, re in swapped]


def spec_vmem():
    return pl.BlockSpec(memory_space=pltpu.VMEM)


def params():
    return pltpu.CompilerParams(vmem_limit_bytes=VMEM_LIMIT)


def cost(flops, bytes_accessed):
    return pl.CostEstimate(flops=flops, bytes_accessed=bytes_accessed, transcendentals=0)


def columns_kernel(source_ref, out_ref):
    for part in range(2):
        turned = source_ref[part].T
        for block in range(4):
            out_ref[pl.ds(block * 64 + part * 32, 32), :] = turned[block * 32 : block * 32 + 32]


def columns_major(source):
    return pl.pallas_call(
        columns_kernel,
        grid=(8,),
        in_specs=[pl.BlockSpec((2, 128, 128), lambda t: (0, 0, t))],
        out_specs=pl.BlockSpec((256, 128), lambda t: (t, 0)),
        out_shape=jax.ShapeDtypeStruct((2048, 128), f32),
        cost_estimate=cost(0, 2 << 20),
        name="columns_major",
    )(source)


def x_forward_kernel(a_ref, t1_ref, tw_ref, t2_ref, out_ref):
    @pl.loop(0, 16)
    def _(c):
        columns = []
        for b0 in range(2):
            re = a_ref[pl.ds(2 * c + b0, 32, stride=64), :]
            im = a_ref[pl.ds(2 * c + b0 + 32, 32, stride=64), :]
            columns.append(jnp.concatenate([re, im], 0))
        high, low = split(jnp.concatenate(columns, 1))
        u = dot(t1_ref[...], jnp.concatenate([high, low, high], 0))
        rows = []
        for b0 in range(2):
            ur = u[:64, 128 * b0 : 128 * b0 + 128]
            ui = u[64:, 128 * b0 : 128 * b0 + 128]
            rows.append(
                jnp.concatenate(
                    [ur * tw_ref[0] - ui * tw_ref[1], ur * tw_ref[1] + ui * tw_ref[0]], 1
                )
            )
        z = jnp.concatenate(rows, 0)
        out = dot3(t2_ref[0], t2_ref[1], z, dot_nt)
        out_ref[pl.ds(c, 128, stride=32), :] = out[:128]
        out_ref[pl.ds(c + 16, 128, stride=32), :] = out[128:]


def x_forward(a):
    t = tables()
    return pl.pallas_call(
        x_forward_kernel,
        in_specs=[spec_vmem()] * 4,
        out_specs=spec_vmem(),
        out_shape=jax.ShapeDtypeStruct((4096, 128), f32),
        compiler_params=params(),
        cost_estimate=cost(2 * 2048 * 65536 * 4, 4 << 20),
        name="x_forward",
    )(a, jnp.asarray(t["t1"]), jnp.asarray(t["tw1"]), jnp.asarray(t["t2"]))


def middle_kernel(
    place_ref, a_ref, r0_ref, r1_ref, r2_ref, r3_ref, t3_ref, tw_ref, step_ref, lane_ref, t4_ref,
    out_ref, u_ref, now_ref,
):
    flip = place_ref[0]
    upper = place_ref[1]
    sign = 1.0 - 2.0 * flip.astype(f32)

    def advance():
        sr = step_ref[0] * sign
        si = step_ref[1] * sign
        nr = now_ref[0]
        ni = now_ref[1]
        now_ref[0] = nr * sr - ni * si
        now_ref[1] = nr * si + ni * sr

    now_ref[...] = tw_ref[...]

    @pl.loop(0, 8)
    def _(cc):
        columns = []
        for half in range(2):
            re = a_ref[pl.ds(2 * cc + half, 128, stride=32), :]
            im = a_ref[pl.ds(2 * cc + half + 16, 128, stride=32), :]
            columns.append(jnp.concatenate([re, im], 0))
        u = dot3(t3_ref[0], t3_ref[1], jnp.concatenate(columns, 1), dot)
        for half in range(2):
            ur = u[:256, 128 * half : 128 * half + 128]
            ui = u[256:, 128 * half : 128 * half + 128]
            nr = now_ref[0]
            ni = now_ref[1]
            u_ref[2 * cc + half, 0] = ur * nr - ui * ni
            u_ref[2 * cc + half, 1] = ur * ni + ui * nr
            advance()

    lane = lax.broadcasted_iota(jnp.int32, (8, 128), 1)
    low = lane < 64
    sgn = jnp.where(low, 1.0, -1.0).astype(f32)
    mine = low == (upper == 0)

    @pl.loop(0, 32)
    def _(tile):
        rows = pl.ds(pl.multiple_of(tile * 8, 8), 8)
        values = [(u_ref[c, 0, rows, :], u_ref[c, 1, rows, :]) for c in range(16)]
        spectrum = transform_list(values)
        back = []
        for e in range(16):
            g, q, row_block = e // 8, (e // 4) % 2, e % 4
            own_ref, other_ref = ((r0_ref, r2_ref), (r1_ref, r3_ref))[g]
            grows = pl.ds(pl.multiple_of(tile * 8 + row_block * 256, 8), 8)
            green = []
            for part in range(2):
                own = own_ref[part, grows, :]
                other = other_ref[part, grows, :]
                green.append(jnp.where(mine, own, other) if q == 0 else jnp.where(mine, other, own))
            lr = lane_ref[0, e]
            li = lane_ref[1, e]
            sr, si = spectrum[e]
            vr = sr * lr - si * li
            vi = sr * li + si * lr
            rr = pltpu.roll(vr, 64, 1)
            ri = pltpu.roll(vi, 64, 1)
            if q == 0:
                fr, fi = sgn * vr + rr, sgn * vi + ri
            else:
                fr, fi = vr - sgn * rr, vi - sgn * ri
            pr = green[0] * fr - green[1] * fi
            pi_ = green[0] * fi + green[1] * fr
            rr = pltpu.roll(pr, 64, 1)
            ri = pltpu.roll(pi_, 64, 1)
            if q == 0:
                vr, vi = sgn * pr + rr, sgn * pi_ + ri
            else:
                vr, vi = pr + sgn * rr, pi_ + sgn * ri
            back.append((vr * lr + vi * li, vi * lr - vr * li))
        for c, (re, im) in enumerate(inverse_list(back)):
            u_ref[c, 0, rows, :] = re
            u_ref[c, 1, rows, :] = im

    now_ref[...] = tw_ref[...]

    @pl.loop(0, 8)
    def _(cc):
        columns = []
        for half in range(2):
            ur = u_ref[2 * cc + half, 0]
            ui = u_ref[2 * cc + half, 1]
            nr = now_ref[0]
            ni = now_ref[1]
            columns.append(jnp.concatenate([ur * nr + ui * ni, ui * nr - ur * ni], 0))
            advance()
        out = dot3(t4_ref[0], t4_ref[1], jnp.concatenate(columns, 1), dot)
        for half in range(2):
            lanes = slice(128 * half, 128 * half + 128)
            out_ref[pl.ds(2 * cc + half, 128, stride=32), :] = out[:128, lanes]
            out_ref[pl.ds(2 * cc + half + 16, 128, stride=32), :] = out[128:, lanes]


def middle(a, greens, place):
    t = tables()
    lane = lax.dynamic_index_in_dim(jnp.asarray(t["lane3"]), place[0], 0, keepdims=False)
    lane = jnp.broadcast_to(lane[:, :, None, :], (2, 16, 8, 128))
    return pl.pallas_call(
        middle_kernel,
        in_specs=[pl.BlockSpec(memory_space=pltpu.SMEM)] + [spec_vmem()] * 10,
        out_specs=spec_vmem(),
        out_shape=jax.ShapeDtypeStruct((4096, 128), f32),
        scratch_shapes=[pltpu.VMEM((16, 2, 256, 128), f32), pltpu.VMEM((2, 256, 128), f32)],
        compiler_params=params(),
        cost_estimate=cost(2 * 8 * 2 * 512 * 65536 * 3, 10 << 20),
        name="middle",
    )(
        place, a, *greens, jnp.asarray(t["t3"]), jnp.asarray(t["tw3"]), jnp.asarray(t["step3"]),
        lane, jnp.asarray(t["t4"]),
    )


def x_inverse_kernel(a_ref, t5_ref, tw_ref, t6_ref, out_ref):
    @pl.loop(0, 8)
    def _(cc):
        columns = []
        for half in range(2):
            re = a_ref[pl.ds(2 * cc + half, 128, stride=32), :]
            im = a_ref[pl.ds(2 * cc + half + 16, 128, stride=32), :]
            columns.append(jnp.concatenate([re, im], 0))
        u = dot3(t5_ref[0], t5_ref[1], jnp.concatenate(columns, 1), dot)
        rows = []
        for half in range(2):
            ur = u[:128, 128 * half : 128 * half + 128]
            ui = u[128:, 128 * half : 128 * half + 128]
            rows.append(
                jnp.concatenate(
                    [ur * tw_ref[0] - ui * tw_ref[1], ur * tw_ref[1] + ui * tw_ref[0]], 1
                )
            )
        out = dot3(t6_ref[0], t6_ref[1], jnp.concatenate(rows, 0), dot_nt)
        for half in range(2):
            lanes = slice(128 * half, 128 * half + 128)
            for b0 in range(2):
                b = 2 * (2 * cc + half) + b0
                out_ref[pl.ds(b, 32, stride=64), :] = out[64 * b0 : 64 * b0 + 32, lanes]
                out_ref[pl.ds(b + 32, 32, stride=64), :] = out[64 * b0 + 32 : 64 * b0 + 64, lanes]


def x_inverse(a):
    t = tables()
    return pl.pallas_call(
        x_inverse_kernel,
        in_specs=[spec_vmem()] * 4,
        out_specs=spec_vmem(),
        out_shape=jax.ShapeDtypeStruct((2048, 128), f32),
        compiler_params=params(),
        cost_estimate=cost(2 * 2048 * 65536 * 4, 4 << 20),
        name="x_inverse",
    )(a, jnp.asarray(t["t5"]), jnp.asarray(t["tw5"]), jnp.asarray(t["t6"]))


def residual_kernel(a_ref, incident_ref, contrast_ref, source_ref, out_ref):
    field = []
    for part in range(2):
        rows = [a_ref[pl.ds(block * 64 + part * 32, 32), :] for block in range(4)]
        field.append(incident_ref[part] + jnp.concatenate(rows, 0).T)
    out_ref[0] = contrast_ref[0] * field[0] - contrast_ref[1] * field[1] - source_ref[0]
    out_ref[1] = contrast_ref[0] * field[1] + contrast_ref[1] * field[0] - source_ref[1]


def residual_of(a, incident, contrast, source):
    tile = pl.BlockSpec((2, 128, 128), lambda t: (0, 0, t))
    return pl.pallas_call(
        residual_kernel,
        grid=(8,),
        in_specs=[pl.BlockSpec((256, 128), lambda t: (t, 0)), tile, tile, tile],
        out_specs=tile,
        out_shape=jax.ShapeDtypeStruct((2, 128, 1024), f32),
        cost_estimate=cost(0, 5 << 20),
        name="residual",
    )(a, incident, contrast, source)


def pack_kernel(place_ref, green_ref, out0_ref, out1_ref, out2_ref, out3_ref):
    flip = place_ref[0]
    upper = place_ref[1]
    lane = lax.broadcasted_iota(jnp.int32, (256, 128), 1)
    low = lane < 64
    pick = low == (flip == 0)
    swap = upper == 1
    outs = ((out0_ref, out1_ref), (out2_ref, out3_ref))
    for part in range(2):
        for across in range(2):
            column = jnp.where(swap, 1 - across, across)
            lanes = pl.ds(pl.multiple_of(column * 128, 128), 128)
            first = green_ref[part, 0, :, lanes]
            second = green_ref[part, 1, :, lanes]
            chooses_first = low != swap
            straight = jnp.where(chooses_first, first, second)
            crossed = pltpu.roll(jnp.where(chooses_first, second, first), 64, 1)
            outs[across][0][part] = jnp.where(pick, straight, crossed)
            outs[across][1][part] = jnp.where(pick, crossed, straight)


def pack_green(green, place):
    out = pl.BlockSpec((2, 256, 128), lambda t: (0, t, 0))
    shape = jax.ShapeDtypeStruct((2, 1024, 128), f32)
    return pl.pallas_call(
        pack_kernel,
        grid=(4,),
        in_specs=[
            pl.BlockSpec(memory_space=pltpu.SMEM),
            pl.BlockSpec((2, 2, 256, 256), lambda t: (0, 0, t, 0)),
        ],
        out_specs=[out] * 4,
        out_shape=[shape] * 4,
        compiler_params=params(),
        cost_estimate=cost(0, 8 << 20),
        name="pack_green",
    )(place, green.reshape(2, 2, 1024, 256))


def project_kernel(source_ref, ea_ref, eb_ref, row_ref, out_ref, lhs_ref, rhs_ref):
    @pl.when(pl.program_id(0) == 0)
    def _():
        re = source_ref[0]
        im = source_ref[1]
        for rows, cols, value in (
            (0, 0, re), (0, 1024, -im), (128, 0, im), (128, 1024, re),
        ):
            high, low = split(value)
            lhs_ref[0, rows : rows + 128, cols : cols + 1024] = high
            lhs_ref[1, rows : rows + 128, cols : cols + 1024] = low

    br = eb_ref[0]
    bi = eb_ref[1]
    for a in range(32):
        ar = ea_ref[0, a : a + 1, :]
        ai = ea_ref[1, a : a + 1, :]
        for part, value in ((0, ar * br - ai * bi), (1, ar * bi + ai * br)):
            high, low = split(value)
            rhs_ref[0, part * 1024 + a * 32 : part * 1024 + a * 32 + 32, :] = high
            rhs_ref[1, part * 1024 + a * 32 : part * 1024 + a * 32 + 32, :] = low
    inner = dot(lhs_ref[0], rhs_ref[0]) + (dot(lhs_ref[0], rhs_ref[1]) + dot(lhs_ref[1], rhs_ref[0]))
    ir = inner[:128]
    ii = inner[128:]
    fr = row_ref[0]
    fi = row_ref[1]
    pr = jnp.sum(fr * ir - fi * ii, axis=0, keepdims=True)
    pi_ = jnp.sum(fr * ii + fi * ir, axis=0, keepdims=True)
    out_ref[...] = jnp.concatenate([pr, pi_, jnp.zeros((6, pr.shape[1]), f32)], 0)


def project(source, ea, eb, rows):
    tile = 256
    whole = pl.BlockSpec((2, 128, 1024), lambda t: (0, 0, 0))
    return pl.pallas_call(
        project_kernel,
        grid=(R // tile,),
        in_specs=[
            whole,
            pl.BlockSpec((2, 32, tile), lambda t: (0, 0, t)),
            pl.BlockSpec((2, 32, tile), lambda t: (0, 0, t)),
            pl.BlockSpec((2, 128, tile), lambda t: (0, 0, t)),
        ],
        out_specs=pl.BlockSpec((8, tile), lambda t: (0, t)),
        out_shape=jax.ShapeDtypeStruct((8, R), f32),
        scratch_shapes=[pltpu.VMEM((2, 256, 2048), bf16), pltpu.VMEM((2, 2048, tile), bf16)],
        compiler_params=params(),
        cost_estimate=cost(2 * 256 * 2048 * 1024 * 3, 4 << 20),
        name="project",
    )(source, ea, eb, rows)


def backproject_kernel(weight_ref, ea_ref, eb_ref, out_ref, lhs_ref, rhs_ref):
    @pl.when(pl.program_id(0) == 0)
    def _():
        wr = weight_ref[0]
        wi = weight_ref[1]
        for rows, cols, value in (
            (0, 0, wr), (0, 1024, wi), (128, 0, wi), (128, 1024, -wr),
        ):
            high, low = split(value)
            lhs_ref[0, rows : rows + 128, cols : cols + 1024] = high
            lhs_ref[1, rows : rows + 128, cols : cols + 1024] = low

    br = eb_ref[0]
    bi = eb_ref[1]
    for a in range(8):
        ar = ea_ref[0, a : a + 1, :]
        ai = ea_ref[1, a : a + 1, :]
        for part, value in ((0, ar * br - ai * bi), (1, ar * bi + ai * br)):
            high, low = split(value)
            rhs_ref[0, a * 32 : a * 32 + 32, part * 1024 : part * 1024 + 1024] = high
            rhs_ref[1, a * 32 : a * 32 + 32, part * 1024 : part * 1024 + 1024] = low
    out = dot_nt(lhs_ref[0], rhs_ref[0]) + (
        dot_nt(lhs_ref[0], rhs_ref[1]) + dot_nt(lhs_ref[1], rhs_ref[0])
    )
    out_ref[0] = out[:128]
    out_ref[1] = out[128:]


def backproject(weights, ea, eb):
    whole = pl.BlockSpec((2, 128, 1024), lambda t: (0, 0, 0))
    return pl.pallas_call(
        backproject_kernel,
        grid=(4,),
        in_specs=[
            whole,
            pl.BlockSpec((2, 8, 1024), lambda t: (0, t, 0)),
            pl.BlockSpec((2, 32, 1024), lambda t: (0, 0, 0)),
        ],
        out_specs=pl.BlockSpec((2, 128, 256), lambda t: (0, 0, t)),
        out_shape=jax.ShapeDtypeStruct((2, 128, 1024), f32),
        scratch_shapes=[pltpu.VMEM((2, 256, 2048), bf16), pltpu.VMEM((2, 256, 2048), bf16)],
        compiler_params=params(),
        cost_estimate=cost(2 * 256 * 2048 * 1024 * 3, 4 << 20),
        name="backproject",
    )(weights, ea, eb)


def phase_pair(position, direction):
    phase = (wave_step * position)[:, None] * direction[None, :]
    return jnp.stack([jnp.cos(phase), -jnp.sin(phase)])


def sum_everywhere(value):
    def exchange(value, axis, size, strides):
        parts = [value] + [
            lax.ppermute(value, axis, [(j, j ^ stride) for j in range(size)]) for stride in strides
        ]
        while len(parts) > 1:
            parts = [parts[j] + parts[j + 1] for j in range(0, len(parts), 2)]
        return parts[0]

    value = exchange(value, "narrow", NARROW, (1,))
    value = exchange(value, "narrow", NARROW, (2,))
    value = exchange(value, "wide", WIDE, (4,))
    value = exchange(value, "wide", WIDE, (1, 2, 3))
    return exchange(value, "wide", WIDE, (8, 16, 24))


def local(sources, incident, contrast, green, angles, measured):
    wide = lax.axis_index("wide")
    narrow = lax.axis_index("narrow")
    place = jnp.stack([narrow % 2, narrow // 2]).astype(jnp.int32)
    source = sources[0]

    lines = columns_major(source)
    lines = lax.all_to_all(lines.reshape(WIDE, 64, 128), "wide", 0, 0, tiled=True)

    packed = pack_green(green, place)
    greens = [packed[0]] + [
        lax.ppermute(packed[k], "narrow", [(j, j ^ k) for j in range(NARROW)]) for k in (1, 2, 3)
    ]

    lines = x_forward(lines.reshape(2048, 128))
    lines = lax.all_to_all(lines.reshape(128, 32, 128), ("wide", "narrow"), 0, 0, tiled=True)
    lines = middle(lines.reshape(4096, 128), greens, place)
    lines = lax.all_to_all(lines.reshape(128, 32, 128), ("wide", "narrow"), 0, 0, tiled=True)
    lines = x_inverse(lines.reshape(4096, 128))
    lines = lax.all_to_all(lines.reshape(WIDE, 64, 128), "wide", 0, 0, tiled=True)
    residual = residual_of(lines.reshape(2048, 128), incident[0], contrast, source)

    row_position = (wide * 128 + jnp.arange(128, dtype=jnp.int32)).astype(f32) - N // 2 + 0.5
    block_position = (narrow * 1024 + 32 * jnp.arange(32, dtype=jnp.int32)).astype(f32) - N // 2 + 0.5
    cell_position = jnp.arange(32, dtype=jnp.int32).astype(f32)
    rows = phase_pair(row_position, jnp.cos(angles))
    sine = jnp.sin(angles)
    ea = phase_pair(block_position, sine)
    eb = phase_pair(cell_position, sine)
    partial_value = project(source, ea, eb, rows)
    total = sum_everywhere(partial_value)[:2]
    data_residual = measured - total[None] * (1.0 / N)
    rho_real = data_residual[0, 0][None, :]
    rho_imag = data_residual[0, 1][None, :]
    scale = 1.0 / math.sqrt(R)
    weights = jnp.stack(
        [
            (rows[0] * rho_real + rows[1] * rho_imag) * scale,
            (rows[0] * rho_imag - rows[1] * rho_real) * scale,
        ]
    )
    back = backproject(weights, ea, eb)
    return (residual[None], back[None], data_residual)


def solution(mesh):
    placed = (
        P(None, None, "wide", "narrow"),
        P(None, None, "wide", "narrow"),
        P(None, "wide", "narrow"),
        P(None, "narrow", "wide"),
        P(),
        P(),
    )
    return jax.shard_map(
        local,
        mesh=mesh,
        in_specs=placed,
        out_specs=(P(None, None, "wide", "narrow"), P(None, None, "wide", "narrow"), P()),
        check_vma=False,
    )
```

```python
import functools
import math

import jax
import jax.numpy as jnp
import ml_dtypes
import numpy as np
from jax import lax
from jax.experimental import pallas as pl
from jax.experimental.pallas import tpu as pltpu
from jax.sharding import PartitionSpec as P

N = 4096
R = 1024
M = 8192
WIDE = 32
NARROW = 4

wave_step = 0.2 * math.pi
f32 = jnp.float32
bf16 = jnp.bfloat16
VMEM_LIMIT = 56 * 1024 * 1024


def complex_block(table):
    return np.block([[table.real, -table.imag], [table.imag, table.real]])


def halves(table):
    high = table.astype(np.float32).astype(ml_dtypes.bfloat16)
    low = (table - high.astype(np.float64)).astype(np.float32).astype(ml_dtypes.bfloat16)
    return high, low


def root(product, length, sign):
    return np.exp(sign * 2j * np.pi * (product % length) / length)


def pair(table):
    return np.stack([table.real, table.imag]).astype(np.float32)


@functools.lru_cache(None)
def tables():
    out = {}
    w = np.arange(32)
    k1 = np.arange(64)
    i = np.arange(128)
    m = np.arange(128)
    high, low = halves(complex_block(root(np.outer(k1, w), 64, -1)))
    out["t1"] = np.concatenate([high, high, low], 1)
    out["tw1"] = pair(root(np.outer(k1, i), M, -1))
    out["t2"] = np.stack(halves(complex_block(root(np.outer(m, i), 128, -1))))
    d = np.arange(128)
    s = 32 * (d % 4) + d // 4
    c1 = np.arange(256)
    out["t3"] = np.stack(halves(complex_block(root(np.outer(c1, s), 256, -1))))
    low_half = np.arange(128) < 64
    first = np.where(low_half[None, :], 1.0, root(c1, M, -1)[:, None])
    out["tw3"] = pair(first)
    out["step3"] = pair(root(2 * c1, M, -1)[:, None] * np.ones((1, 128)))
    lanes = []
    for flip in (0, 1):
        e = (np.arange(16) + 8 * flip) % 16
        lanes.append(pair(np.where(low_half[None, :], 1.0, root(e, 32, -1)[:, None])))
    out["lane3"] = np.stack(lanes)
    out["t4"] = np.stack(halves(complex_block(root(np.outer(s, c1), 256, 1))))
    out["t5"] = np.stack(halves(complex_block(root(np.outer(i, m), 128, 1))))
    lane_k1 = np.arange(128) % 64
    out["tw5"] = pair(root(np.outer(i, lane_k1), M, 1))
    inner = root(np.outer(w, k1), 64, 1) / (M * M)
    block = np.zeros((2, 2, 32, 2, 2, 64))
    for b0 in (0, 1):
        block[b0, 0, :, 0, b0, :] = inner.real
        block[b0, 0, :, 1, b0, :] = -inner.imag
        block[b0, 1, :, 0, b0, :] = inner.imag
        block[b0, 1, :, 1, b0, :] = inner.real
    out["t6"] = np.stack(halves(block.reshape(128, 256)))
    return out


def split(values):
    high = values.astype(bf16)
    low = (values - high.astype(f32)).astype(bf16)
    return high, low


def dot(a, b):
    return lax.dot_general(a, b, (((1,), (0,)), ((), ())), preferred_element_type=f32)


def dot_nt(a, b):
    return lax.dot_general(a, b, (((1,), (1,)), ((), ())), preferred_element_type=f32)


def dot3(table_high, table_low, values, product):
    high, low = split(values)
    return product(table_high, high) + (product(table_high, low) + product(table_low, high))


def times_root(value, numerator, length):
    re, im = value
    numerator %= length
    if numerator == 0:
        return value
    if 4 * numerator == length:
        return im, -re
    if 2 * numerator == length:
        return -re, -im
    if 4 * numerator == 3 * length:
        return -im, re
    if 8 * numerator == length:
        half = math.sqrt(0.5)
        return (re + im) * half, (im - re) * half
    if 8 * numerator == 3 * length:
        half = math.sqrt(0.5)
        return (im - re) * half, (-re - im) * half
    cosine = math.cos(2 * math.pi * numerator / length)
    sine = -math.sin(2 * math.pi * numerator / length)
    return re * cosine - im * sine, re * sine + im * cosine


def transform_list(values):
    count = len(values)
    if count == 1:
        return values
    if count == 2:
        (ar, ai), (br, bi) = values
        return [(ar + br, ai + bi), (ar - br, ai - bi)]
    if count == 4:
        (ar, ai), (br, bi), (cr, ci), (dr, di) = values
        pr, pi_, qr, qi = ar + cr, ai + ci, ar - cr, ai - ci
        sr, si, tr, ti = br + dr, bi + di, br - dr, bi - di
        return [(pr + sr, pi_ + si), (qr + ti, qi - tr), (pr - sr, pi_ - si), (qr - ti, qi + tr)]
    parts = [transform_list(values[start::4]) for start in range(4)]
    quarter = count // 4
    out = [None] * count
    for k in range(quarter):
        column = [times_root(parts[j][k], j * k, count) for j in range(4)]
        for q, value in enumerate(transform_list(column)):
            out[k + q * quarter] = value
    return out


def inverse_list(values):
    swapped = transform_list([(im, re) for re, im in values])
    return [(re, im) for im, re in swapped]


def spec_vmem():
    return pl.BlockSpec(memory_space=pltpu.VMEM)


def params():
    return pltpu.CompilerParams(vmem_limit_bytes=VMEM_LIMIT)


def cost(flops, bytes_accessed):
    return pl.CostEstimate(flops=flops, bytes_accessed=bytes_accessed, transcendentals=0)


def columns_kernel(source_ref, out_ref):
    for tile in range(4):
        for part in range(2):
            turned = source_ref[part, :, 128 * tile : 128 * tile + 128].T
            for block in range(4):
                first = 256 * tile + block * 64 + part * 32
                out_ref[first : first + 32, :] = turned[block * 32 : block * 32 + 32]


def columns_major(source):
    return pl.pallas_call(
        columns_kernel,
        grid=(2,),
        in_specs=[pl.BlockSpec((2, 128, 512), lambda t: (0, 0, t))],
        out_specs=pl.BlockSpec((1024, 128), lambda t: (t, 0)),
        out_shape=jax.ShapeDtypeStruct((2048, 128), f32),
        cost_estimate=cost(0, 2 << 20),
        name="columns_major",
    )(source)


def x_forward_kernel(a_ref, t1_ref, tw_ref, t2_ref, out_ref):
    @pl.loop(0, 16, unroll=8)
    def _(c):
        columns = []
        for b0 in range(2):
            re = a_ref[pl.ds(2 * c + b0, 32, stride=64), :]
            im = a_ref[pl.ds(2 * c + b0 + 32, 32, stride=64), :]
            columns.append(jnp.concatenate([re, im], 0))
        high, low = split(jnp.concatenate(columns, 1))
        u = dot(t1_ref[...], jnp.concatenate([high, low, high], 0))
        rows = []
        for b0 in range(2):
            ur = u[:64, 128 * b0 : 128 * b0 + 128]
            ui = u[64:, 128 * b0 : 128 * b0 + 128]
            rows.append(
                jnp.concatenate(
                    [ur * tw_ref[0] - ui * tw_ref[1], ur * tw_ref[1] + ui * tw_ref[0]], 1
                )
            )
        z = jnp.concatenate(rows, 0)
        out = dot3(t2_ref[0], t2_ref[1], z, dot_nt)
        out_ref[pl.ds(c, 128, stride=32), :] = out[:128]
        out_ref[pl.ds(c + 16, 128, stride=32), :] = out[128:]


def x_forward(a):
    t = tables()
    return pl.pallas_call(
        x_forward_kernel,
        in_specs=[spec_vmem()] * 4,
        out_specs=spec_vmem(),
        out_shape=jax.ShapeDtypeStruct((4096, 128), f32),
        compiler_params=params(),
        cost_estimate=cost(2 * 2048 * 65536 * 4, 4 << 20),
        name="x_forward",
    )(a, jnp.asarray(t["t1"]), jnp.asarray(t["tw1"]), jnp.asarray(t["t2"]))


def middle_kernel(
    place_ref, a_ref, r0_ref, r1_ref, r2_ref, r3_ref, t3_ref, tw_ref, step_ref, lane_ref, t4_ref,
    out_ref, u_ref, now_ref, green_ref, late_ref, arrived,
):
    copies = [
        pltpu.make_async_copy(ref, green_ref.at[k], arrived.at[k])
        for k, ref in enumerate((r0_ref, r1_ref, r2_ref.at[0], r3_ref))
    ]
    copies.append(pltpu.make_async_copy(t4_ref, late_ref, arrived.at[4]))
    for copy in copies:
        copy.start()
    flip = place_ref[0]
    upper = place_ref[1]
    sign = 1.0 - 2.0 * flip.astype(f32)

    def advance():
        sr = step_ref[0] * sign
        si = step_ref[1] * sign
        nr = now_ref[0]
        ni = now_ref[1]
        now_ref[0] = nr * sr - ni * si
        now_ref[1] = nr * si + ni * sr

    now_ref[...] = tw_ref[...]

    @pl.loop(0, 8, unroll=2)
    def _(cc):
        columns = []
        for half in range(2):
            re = a_ref[pl.ds(2 * cc + half, 128, stride=32), :]
            im = a_ref[pl.ds(2 * cc + half + 16, 128, stride=32), :]
            columns.append(jnp.concatenate([re, im], 0))
        u = dot3(t3_ref[0], t3_ref[1], jnp.concatenate(columns, 1), dot)
        for half in range(2):
            ur = u[:256, 128 * half : 128 * half + 128]
            ui = u[256:, 128 * half : 128 * half + 128]
            nr = now_ref[0]
            ni = now_ref[1]
            u_ref[2 * cc + half, 0] = ur * nr - ui * ni
            u_ref[2 * cc + half, 1] = ur * ni + ui * nr
            advance()

    for copy in copies:
        copy.wait()

    lane = lax.broadcasted_iota(jnp.int32, (8, 128), 1)
    low = lane < 64
    sgn = jnp.where(low, 1.0, -1.0).astype(f32)
    mine = low == (upper == 0)

    @pl.loop(0, 32, unroll=2)
    def _(tile):
        rows = pl.ds(pl.multiple_of(tile * 8, 8), 8)
        values = [(u_ref[c, 0, rows, :], u_ref[c, 1, rows, :]) for c in range(16)]
        spectrum = transform_list(values)
        back = []
        for e in range(16):
            g, q, row_block = e // 8, (e // 4) % 2, e % 4
            grows = pl.ds(pl.multiple_of(tile * 8 + row_block * 256, 8), 8)
            green = []
            for part in range(2):
                own = green_ref[g, part, grows, :]
                other = green_ref[g + 2, part, grows, :]
                green.append(jnp.where(mine, own, other) if q == 0 else jnp.where(mine, other, own))
            lr = lane_ref[flip, 0, e : e + 1, :]
            li = lane_ref[flip, 1, e : e + 1, :]
            sr, si = spectrum[e]
            vr = sr * lr - si * li
            vi = sr * li + si * lr
            rr = pltpu.roll(vr, 64, 1)
            ri = pltpu.roll(vi, 64, 1)
            if q == 0:
                fr, fi = sgn * vr + rr, sgn * vi + ri
            else:
                fr, fi = vr - sgn * rr, vi - sgn * ri
            pr = green[0] * fr - green[1] * fi
            pi_ = green[0] * fi + green[1] * fr
            rr = pltpu.roll(pr, 64, 1)
            ri = pltpu.roll(pi_, 64, 1)
            if q == 0:
                vr, vi = sgn * pr + rr, sgn * pi_ + ri
            else:
                vr, vi = pr + sgn * rr, pi_ + sgn * ri
            back.append((vr * lr + vi * li, vi * lr - vr * li))
        for c, (re, im) in enumerate(inverse_list(back)):
            u_ref[c, 0, rows, :] = re
            u_ref[c, 1, rows, :] = im

    now_ref[...] = tw_ref[...]

    @pl.loop(0, 8, unroll=2)
    def _(cc):
        columns = []
        for half in range(2):
            ur = u_ref[2 * cc + half, 0]
            ui = u_ref[2 * cc + half, 1]
            nr = now_ref[0]
            ni = now_ref[1]
            columns.append(jnp.concatenate([ur * nr + ui * ni, ui * nr - ur * ni], 0))
            advance()
        out = dot3(late_ref[0], late_ref[1], jnp.concatenate(columns, 1), dot)
        for half in range(2):
            lanes = slice(128 * half, 128 * half + 128)
            out_ref[pl.ds(2 * cc + half, 128, stride=32), :] = out[:128, lanes]
            out_ref[pl.ds(2 * cc + half + 16, 128, stride=32), :] = out[128:, lanes]


def middle(a, greens, place):
    t = tables()
    return pl.pallas_call(
        middle_kernel,
        in_specs=[pl.BlockSpec(memory_space=pltpu.SMEM), spec_vmem()]
        + [pl.BlockSpec(memory_space=pl.ANY)] * 4
        + [spec_vmem()] * 4
        + [pl.BlockSpec(memory_space=pl.ANY)],
        out_specs=spec_vmem(),
        out_shape=jax.ShapeDtypeStruct((4096, 128), f32),
        scratch_shapes=[
            pltpu.VMEM((16, 2, 256, 128), f32),
            pltpu.VMEM((2, 256, 128), f32),
            pltpu.VMEM((4, 2, 1024, 128), f32),
            pltpu.VMEM((2, 256, 512), bf16),
            pltpu.SemaphoreType.DMA((5,)),
        ],
        compiler_params=params(),
        cost_estimate=cost(2 * 8 * 2 * 512 * 65536 * 3, 10 << 20),
        name="middle",
    )(
        place, a, *greens, jnp.asarray(t["t3"]), jnp.asarray(t["tw3"]), jnp.asarray(t["step3"]),
        jnp.asarray(t["lane3"]), jnp.asarray(t["t4"]),
    )


def x_inverse_kernel(a_ref, t5_ref, tw_ref, t6_ref, out_ref):
    @pl.loop(0, 8, unroll=8)
    def _(cc):
        columns = []
        for half in range(2):
            re = a_ref[pl.ds(2 * cc + half, 128, stride=32), :]
            im = a_ref[pl.ds(2 * cc + half + 16, 128, stride=32), :]
            columns.append(jnp.concatenate([re, im], 0))
        u = dot3(t5_ref[0], t5_ref[1], jnp.concatenate(columns, 1), dot)
        rows = []
        for half in range(2):
            ur = u[:128, 128 * half : 128 * half + 128]
            ui = u[128:, 128 * half : 128 * half + 128]
            rows.append(
                jnp.concatenate(
                    [ur * tw_ref[0] - ui * tw_ref[1], ur * tw_ref[1] + ui * tw_ref[0]], 1
                )
            )
        out = dot3(t6_ref[0], t6_ref[1], jnp.concatenate(rows, 0), dot_nt)
        for half in range(2):
            lanes = slice(128 * half, 128 * half + 128)
            for b0 in range(2):
                b = 2 * (2 * cc + half) + b0
                out_ref[pl.ds(b, 32, stride=64), :] = out[64 * b0 : 64 * b0 + 32, lanes]
                out_ref[pl.ds(b + 32, 32, stride=64), :] = out[64 * b0 + 32 : 64 * b0 + 64, lanes]


def x_inverse(a):
    t = tables()
    return pl.pallas_call(
        x_inverse_kernel,
        in_specs=[spec_vmem()] * 4,
        out_specs=spec_vmem(),
        out_shape=jax.ShapeDtypeStruct((2048, 128), f32),
        compiler_params=params(),
        cost_estimate=cost(2 * 2048 * 65536 * 4, 4 << 20),
        name="x_inverse",
    )(a, jnp.asarray(t["t5"]), jnp.asarray(t["tw5"]), jnp.asarray(t["t6"]))


def residual_kernel(a_ref, incident_ref, contrast_ref, source_ref, out_ref):
    for tile in range(4):
        lanes = slice(128 * tile, 128 * tile + 128)
        field = []
        for part in range(2):
            rows = []
            for block in range(4):
                first = 256 * tile + block * 64 + part * 32
                rows.append(a_ref[first : first + 32, :])
            field.append(incident_ref[part, :, lanes] + jnp.concatenate(rows, 0).T)
        cr = contrast_ref[0, :, lanes]
        ci = contrast_ref[1, :, lanes]
        out_ref[0, :, lanes] = cr * field[0] - ci * field[1] - source_ref[0, :, lanes]
        out_ref[1, :, lanes] = cr * field[1] + ci * field[0] - source_ref[1, :, lanes]


def residual_of(a, incident, contrast, source):
    tile = pl.BlockSpec((2, 128, 512), lambda t: (0, 0, t))
    return pl.pallas_call(
        residual_kernel,
        grid=(2,),
        in_specs=[pl.BlockSpec((1024, 128), lambda t: (t, 0)), tile, tile, tile],
        out_specs=tile,
        out_shape=jax.ShapeDtypeStruct((2, 128, 1024), f32),
        compiler_params=params(),
        cost_estimate=cost(0, 5 << 20),
        name="residual",
    )(a, incident, contrast, source)


def pack_kernel(across, place_ref, green_ref, out_ref):
    flip = place_ref[0]
    upper = place_ref[1]
    lane = lax.broadcasted_iota(jnp.int32, (512, 128), 1)
    low = lane < 64
    pick = low == (flip == 0)
    swap = upper == 1
    column = jnp.where(swap, 1 - across, across)
    lanes = pl.ds(pl.multiple_of(column * 128, 128), 128)
    chooses_first = low != swap
    for part in range(2):
        first = green_ref[part, 0, :, lanes]
        second = green_ref[part, 1, :, lanes]
        straight = jnp.where(chooses_first, first, second)
        crossed = pltpu.roll(jnp.where(chooses_first, second, first), 64, 1)
        out_ref[0, part] = jnp.where(pick, straight, crossed)
        out_ref[1, part] = jnp.where(pick, crossed, straight)


def pack_green(green, place, across):
    return pl.pallas_call(
        functools.partial(pack_kernel, across),
        grid=(2,),
        in_specs=[
            pl.BlockSpec(memory_space=pltpu.SMEM),
            pl.BlockSpec((2, 2, 512, 256), lambda t: (0, 0, t, 0)),
        ],
        out_specs=pl.BlockSpec((2, 2, 512, 128), lambda t: (0, 0, t, 0)),
        out_shape=jax.ShapeDtypeStruct((2, 2, 1024, 128), f32),
        compiler_params=params(),
        cost_estimate=cost(0, 6 << 20),
        name="pack_far" if across else "pack_near",
    )(place, green.reshape(2, 2, 1024, 256))


def project_kernel(source_ref, ea_ref, eb_ref, row_ref, out_ref, lhs_ref, rhs_ref):
    @pl.when(pl.program_id(0) == 0)
    def _():
        re = source_ref[0]
        im = source_ref[1]
        for rows, cols, value in (
            (0, 0, re), (0, 1024, -im), (128, 0, im), (128, 1024, re),
        ):
            high, low = split(value)
            lhs_ref[0, rows : rows + 128, cols : cols + 1024] = high
            lhs_ref[1, rows : rows + 128, cols : cols + 1024] = low

    br = eb_ref[0]
    bi = eb_ref[1]
    for a in range(32):
        ar = ea_ref[0, a : a + 1, :]
        ai = ea_ref[1, a : a + 1, :]
        for part, value in ((0, ar * br - ai * bi), (1, ar * bi + ai * br)):
            high, low = split(value)
            rhs_ref[0, part * 1024 + a * 32 : part * 1024 + a * 32 + 32, :] = high
            rhs_ref[1, part * 1024 + a * 32 : part * 1024 + a * 32 + 32, :] = low
    inner = dot(lhs_ref[0], rhs_ref[0]) + (dot(lhs_ref[0], rhs_ref[1]) + dot(lhs_ref[1], rhs_ref[0]))
    ir = inner[:128]
    ii = inner[128:]
    fr = row_ref[0]
    fi = row_ref[1]
    pr = jnp.sum(fr * ir - fi * ii, axis=0, keepdims=True)
    pi_ = jnp.sum(fr * ii + fi * ir, axis=0, keepdims=True)
    out_ref[...] = jnp.concatenate([pr, pi_, jnp.zeros((6, pr.shape[1]), f32)], 0)


def project(source, ea, eb, rows):
    tile = 256
    whole = pl.BlockSpec((2, 128, 1024), lambda t: (0, 0, 0))
    return pl.pallas_call(
        project_kernel,
        grid=(R // tile,),
        in_specs=[
            whole,
            pl.BlockSpec((2, 32, tile), lambda t: (0, 0, t)),
            pl.BlockSpec((2, 32, tile), lambda t: (0, 0, t)),
            pl.BlockSpec((2, 128, tile), lambda t: (0, 0, t)),
        ],
        out_specs=pl.BlockSpec((8, tile), lambda t: (0, t)),
        out_shape=jax.ShapeDtypeStruct((8, R), f32),
        scratch_shapes=[pltpu.VMEM((2, 256, 2048), bf16), pltpu.VMEM((2, 2048, tile), bf16)],
        compiler_params=params(),
        cost_estimate=cost(2 * 256 * 2048 * 1024 * 3, 4 << 20),
        name="project",
    )(source, ea, eb, rows)


def backproject_kernel(weight_ref, ea_ref, eb_ref, out_ref, lhs_ref, rhs_ref):
    @pl.when(pl.program_id(0) == 0)
    def _():
        wr = weight_ref[0]
        wi = weight_ref[1]
        for rows, cols, value in (
            (0, 0, wr), (0, 1024, wi), (128, 0, wi), (128, 1024, -wr),
        ):
            high, low = split(value)
            lhs_ref[0, rows : rows + 128, cols : cols + 1024] = high
            lhs_ref[1, rows : rows + 128, cols : cols + 1024] = low

    br = eb_ref[0]
    bi = eb_ref[1]
    for a in range(8):
        ar = ea_ref[0, a : a + 1, :]
        ai = ea_ref[1, a : a + 1, :]
        for part, value in ((0, ar * br - ai * bi), (1, ar * bi + ai * br)):
            high, low = split(value)
            rhs_ref[0, a * 32 : a * 32 + 32, part * 1024 : part * 1024 + 1024] = high
            rhs_ref[1, a * 32 : a * 32 + 32, part * 1024 : part * 1024 + 1024] = low
    out = dot_nt(lhs_ref[0], rhs_ref[0]) + (
        dot_nt(lhs_ref[0], rhs_ref[1]) + dot_nt(lhs_ref[1], rhs_ref[0])
    )
    out_ref[0] = out[:128]
    out_ref[1] = out[128:]


def backproject(weights, ea, eb):
    whole = pl.BlockSpec((2, 128, 1024), lambda t: (0, 0, 0))
    return pl.pallas_call(
        backproject_kernel,
        grid=(4,),
        in_specs=[
            whole,
            pl.BlockSpec((2, 8, 1024), lambda t: (0, t, 0)),
            pl.BlockSpec((2, 32, 1024), lambda t: (0, 0, 0)),
        ],
        out_specs=pl.BlockSpec((2, 128, 256), lambda t: (0, 0, t)),
        out_shape=jax.ShapeDtypeStruct((2, 128, 1024), f32),
        scratch_shapes=[pltpu.VMEM((2, 256, 2048), bf16), pltpu.VMEM((2, 256, 2048), bf16)],
        compiler_params=params(),
        cost_estimate=cost(2 * 256 * 2048 * 1024 * 3, 4 << 20),
        name="backproject",
    )(weights, ea, eb)


def phase_pair(position, direction):
    phase = (wave_step * position)[:, None] * direction[None, :]
    return jnp.stack([jnp.cos(phase), -jnp.sin(phase)])


def sum_over(value, steps):
    def exchange(value, axis, size, strides):
        parts = [value] + [
            lax.ppermute(value, axis, [(j, j ^ stride) for j in range(size)]) for stride in strides
        ]
        while len(parts) > 1:
            parts = [parts[j] + parts[j + 1] for j in range(0, len(parts), 2)]
        return parts[0]

    for axis, size, strides in steps:
        value = exchange(value, axis, size, strides)
    return value


def local(sources, incident, contrast, green, angles, measured):
    wide = lax.axis_index("wide")
    narrow = lax.axis_index("narrow")
    place = jnp.stack([narrow % 2, narrow // 2]).astype(jnp.int32)
    source = sources[0]

    def partner(value, k):
        return lax.ppermute(value, "narrow", [(j, j ^ k) for j in range(NARROW)])

    far = pack_green(green, place, 1)
    far, source_after, green_after = lax.optimization_barrier((far, source, green))
    far = partner(far, 2)
    lines = columns_major(source_after)
    near = pack_green(green_after, place, 0)
    near_partner = partner(near[1], 1)
    lines = lax.all_to_all(lines.reshape(WIDE, 64, 128), "wide", 0, 0, tiled=True)

    row_position = (wide * 128 + jnp.arange(128, dtype=jnp.int32)).astype(f32) - N // 2 + 0.5
    block_position = (narrow * 1024 + 32 * jnp.arange(32, dtype=jnp.int32)).astype(f32) - N // 2 + 0.5
    cell_position = jnp.arange(32, dtype=jnp.int32).astype(f32)
    rows = phase_pair(row_position, jnp.cos(angles))
    sine = jnp.sin(angles)
    ea = phase_pair(block_position, sine)
    eb = phase_pair(cell_position, sine)
    partial_value = project(source, ea, eb, rows)
    lines, partial_value = lax.optimization_barrier((lines, partial_value))
    lines = x_forward(lines.reshape(2048, 128))
    lines = lax.all_to_all(lines.reshape(128, 32, 128), ("wide", "narrow"), 0, 0, tiled=True)

    total = sum_over(partial_value, [("wide", WIDE, (1, 2, 3)), ("wide", WIDE, (8, 16, 24))])
    total, far, near_partner = lax.optimization_barrier((total, far, near_partner))
    total = sum_over(total, [("narrow", NARROW, (1,))])
    greens = [near[0], near_partner, far, partner(far[1], 1)]
    total, lines = lax.optimization_barrier((total, lines))
    lines = middle(lines.reshape(4096, 128), greens, place)
    total, lines = lax.optimization_barrier((total, lines))
    lines = lax.all_to_all(lines.reshape(128, 32, 128), ("wide", "narrow"), 0, 0, tiled=True)
    total = sum_over(total, [("wide", WIDE, (4,)), ("narrow", NARROW, (2,))])[:2]
    lines = x_inverse(lines.reshape(4096, 128))
    lines = lax.all_to_all(lines.reshape(WIDE, 64, 128), "wide", 0, 0, tiled=True)
    residual = residual_of(lines.reshape(2048, 128), incident[0], contrast, source)

    data_residual = measured - total[None] * (1.0 / N)
    rho_real = data_residual[0, 0][None, :]
    rho_imag = data_residual[0, 1][None, :]
    scale = 1.0 / math.sqrt(R)
    weights = jnp.stack(
        [
            (rows[0] * rho_real + rows[1] * rho_imag) * scale,
            (rows[0] * rho_imag - rows[1] * rho_real) * scale,
        ]
    )
    back = backproject(weights, ea, eb)
    return (residual[None], back[None], data_residual)


def solution(mesh):
    placed = (
        P(None, None, "wide", "narrow"),
        P(None, None, "wide", "narrow"),
        P(None, "wide", "narrow"),
        P(None, "narrow", "wide"),
        P(),
        P(),
    )
    return jax.shard_map(
        local,
        mesh=mesh,
        in_specs=placed,
        out_specs=(P(None, None, "wide", "narrow"), P(None, None, "wide", "narrow"), P()),
        check_vma=False,
    )
```

```python
import functools
import math

import jax
import jax.numpy as jnp
import ml_dtypes
import numpy as np
from jax import lax
from jax.experimental import pallas as pl
from jax.experimental.pallas import tpu as pltpu
from jax.sharding import PartitionSpec as P

N = 4096
R = 1024
M = 8192
WIDE = 32
NARROW = 4

wave_step = 0.2 * math.pi
f32 = jnp.float32
bf16 = jnp.bfloat16


def complex_block(table):
    return np.block([[table.real, -table.imag], [table.imag, table.real]])


def terms(table):
    high = table.astype(np.float32).astype(ml_dtypes.bfloat16)
    low = (table - high.astype(np.float64)).astype(np.float32).astype(ml_dtypes.bfloat16)
    return np.concatenate([high, high, low], 1)


def root(product, length, sign):
    return np.exp(sign * 2j * np.pi * (product % length) / length)


def pair(table):
    return np.stack([table.real, table.imag]).astype(np.float32)


@functools.lru_cache(None)
def tables():
    out = {}
    w = np.arange(32)
    k1 = np.arange(64)
    i = np.arange(128)
    m = np.arange(128)
    out["t1"] = terms(complex_block(root(np.outer(k1, w), 64, -1)))
    out["tw1"] = pair(root(np.outer(k1, i), M, -1))
    out["t2"] = terms(complex_block(root(np.outer(m, i), 128, -1)))
    d = np.arange(128)
    s = 32 * (d % 4) + d // 4
    c1 = np.arange(256)
    out["t3"] = terms(complex_block(root(np.outer(c1, s), 256, -1)))
    low_half = np.arange(128) < 64
    first = np.where(low_half[None, :], 1.0, root(c1, M, -1)[:, None])
    out["tw3"] = pair(first)
    out["step3"] = pair(root(2 * c1, M, -1)[:, None] * np.ones((1, 128)))
    lanes = []
    for flip in (0, 1):
        first_e = (np.array([0, 1, 2, 3, 8, 9, 10, 11]) + 8 * flip) % 16
        e = np.where(low_half[None, :], first_e[:, None], first_e[:, None] + 4)
        lanes.append(pair(root(e, 32, -1)))
    out["lane3"] = np.stack(lanes)
    out["t4"] = terms(complex_block(root(np.outer(s, c1), 256, 1)))
    out["t5"] = terms(complex_block(root(np.outer(i, m), 128, 1)))
    lane_k1 = np.arange(128) % 64
    out["tw5"] = pair(root(np.outer(i, lane_k1), M, 1))
    inner = root(np.outer(w, k1), 64, 1) / (M * M)
    block = np.zeros((2, 2, 32, 2, 2, 64))
    for b0 in (0, 1):
        block[b0, 0, :, 0, b0, :] = inner.real
        block[b0, 0, :, 1, b0, :] = -inner.imag
        block[b0, 1, :, 0, b0, :] = inner.imag
        block[b0, 1, :, 1, b0, :] = inner.real
    out["t6"] = terms(block.reshape(128, 256))
    return out


def split(values):
    high = values.astype(bf16)
    low = (values - high.astype(f32)).astype(bf16)
    return high, low


def dot(a, b):
    return lax.dot_general(a, b, (((1,), (0,)), ((), ())), preferred_element_type=f32)


def dot_nt(a, b):
    return lax.dot_general(a, b, (((1,), (1,)), ((), ())), preferred_element_type=f32)


def dot3(table, values):
    high, low = split(values)
    return dot(table, jnp.concatenate([high, low, high], 0))


def dot3_nt(table, values):
    high, low = split(values)
    return dot_nt(table, jnp.concatenate([high, low, high], 1))


def times_root(value, numerator, length):
    re, im = value
    numerator %= length
    if numerator == 0:
        return value
    if 4 * numerator == length:
        return im, -re
    if 2 * numerator == length:
        return -re, -im
    if 4 * numerator == 3 * length:
        return -im, re
    if 8 * numerator == length:
        half = math.sqrt(0.5)
        return (re + im) * half, (im - re) * half
    if 8 * numerator == 3 * length:
        half = math.sqrt(0.5)
        return (im - re) * half, (-re - im) * half
    cosine = math.cos(2 * math.pi * numerator / length)
    sine = -math.sin(2 * math.pi * numerator / length)
    return re * cosine - im * sine, re * sine + im * cosine


def transform_list(values):
    count = len(values)
    if count == 1:
        return values
    if count == 2:
        (ar, ai), (br, bi) = values
        return [(ar + br, ai + bi), (ar - br, ai - bi)]
    if count == 4:
        (ar, ai), (br, bi), (cr, ci), (dr, di) = values
        pr, pi_, qr, qi = ar + cr, ai + ci, ar - cr, ai - ci
        sr, si, tr, ti = br + dr, bi + di, br - dr, bi - di
        return [(pr + sr, pi_ + si), (qr + ti, qi - tr), (pr - sr, pi_ - si), (qr - ti, qi + tr)]
    parts = [transform_list(values[start::4]) for start in range(4)]
    quarter = count // 4
    out = [None] * count
    for k in range(quarter):
        column = [times_root(parts[j][k], j * k, count) for j in range(4)]
        for q, value in enumerate(transform_list(column)):
            out[k + q * quarter] = value
    return out


def inverse_list(values):
    swapped = transform_list([(im, re) for re, im in values])
    return [(re, im) for im, re in swapped]


def spec_vmem():
    return pl.BlockSpec(memory_space=pltpu.VMEM)


def spec_hbm():
    return pl.BlockSpec(memory_space=pltpu.HBM)


def in_hbm(*values):
    return [pltpu.with_memory_space_constraint(jnp.asarray(value), pltpu.HBM) for value in values]


def fetch(sources, targets, arrived):
    copies = [
        pltpu.make_async_copy(source, target, arrived.at[k])
        for k, (source, target) in enumerate(zip(sources, targets))
    ]
    for copy in copies:
        copy.start()
    return copies


def params(mebibytes=16):
    return pltpu.CompilerParams(vmem_limit_bytes=mebibytes << 20)


def cost(flops, bytes_accessed):
    return pl.CostEstimate(flops=flops, bytes_accessed=bytes_accessed, transcendentals=0)


def columns_kernel(source_ref, out_ref):
    for tile in range(4):
        for part in range(2):
            turned = source_ref[part, :, 128 * tile : 128 * tile + 128].T
            for block in range(4):
                first = 256 * tile + block * 64 + part * 32
                out_ref[first : first + 32, :] = turned[block * 32 : block * 32 + 32]


def columns_major(source):
    return pl.pallas_call(
        columns_kernel,
        grid=(2,),
        in_specs=[pl.BlockSpec((2, 128, 512), lambda t: (0, 0, t))],
        out_specs=pl.BlockSpec((1024, 128), lambda t: (t, 0)),
        out_shape=pltpu.HBM((2048, 128), f32),
        cost_estimate=cost(0, 2 << 20),
        name="columns_major",
    )(source)


def x_forward_kernel(
    a_ref, t1_hbm, tw_hbm, t2_hbm, out_hbm, t1_ref, tw_ref, t2_ref, out_ref, arrived, sent
):
    for copy in fetch((t1_hbm, tw_hbm, t2_hbm), (t1_ref, tw_ref, t2_ref), arrived):
        copy.wait()

    @pl.loop(0, 16, unroll=8)
    def _(c):
        columns = []
        for b0 in range(2):
            re = a_ref[pl.ds(2 * c + b0, 32, stride=64), :]
            im = a_ref[pl.ds(2 * c + b0 + 32, 32, stride=64), :]
            columns.append(jnp.concatenate([re, im], 0))
        u = dot3(t1_ref[...], jnp.concatenate(columns, 1))
        rows = []
        for b0 in range(2):
            ur = u[:64, 128 * b0 : 128 * b0 + 128]
            ui = u[64:, 128 * b0 : 128 * b0 + 128]
            rows.append(
                jnp.concatenate(
                    [ur * tw_ref[0] - ui * tw_ref[1], ur * tw_ref[1] + ui * tw_ref[0]], 1
                )
            )
        z = jnp.concatenate(rows, 0)
        out = dot3_nt(t2_ref[...], z)
        out_ref[pl.ds(c, 128, stride=32), :] = out[:128]
        out_ref[pl.ds(c + 16, 128, stride=32), :] = out[128:]

    last = pltpu.make_async_copy(out_ref, out_hbm, sent)
    last.start()
    last.wait()


def x_forward(a):
    t = tables()
    return pl.pallas_call(
        x_forward_kernel,
        in_specs=[spec_vmem()] + [spec_hbm()] * 3,
        out_specs=spec_hbm(),
        out_shape=pltpu.HBM((4096, 128), f32),
        scratch_shapes=[
            pltpu.VMEM((128, 192), bf16),
            pltpu.VMEM((2, 64, 128), f32),
            pltpu.VMEM((256, 768), bf16),
            pltpu.VMEM((4096, 128), f32),
            pltpu.SemaphoreType.DMA((3,)),
            pltpu.SemaphoreType.DMA,
        ],
        compiler_params=params(8),
        cost_estimate=cost(2 * 2048 * 65536 * 4, 4 << 20),
        name="x_forward",
    )(a, *in_hbm(t["t1"], t["tw1"], t["t2"]))


def middle_kernel(
    place_ref, a_ref, t3_hbm, tw_hbm, step_hbm, r0_hbm, r1_hbm, r2_hbm, r3_hbm, lane_hbm, t4_hbm,
    out_hbm, t3_ref, tw_ref, step_ref, green_ref, lane_ref, t4_ref, u_ref, now_ref, out_ref,
    arrived, sent,
):
    flip = place_ref[0]
    upper = place_ref[1]
    copies = fetch(
        (t3_hbm, tw_hbm, step_hbm, r0_hbm, r1_hbm, r2_hbm.at[0], r3_hbm, lane_hbm, t4_hbm),
        (t3_ref, tw_ref, step_ref)
        + tuple(green_ref.at[g, h] for h in (upper, 1 - upper) for g in range(2))
        + (lane_ref, t4_ref),
        arrived,
    )
    for copy in copies[:3]:
        copy.wait()
    sign = 1.0 - 2.0 * flip.astype(f32)

    def advance():
        sr = step_ref[0] * sign
        si = step_ref[1] * sign
        nr = now_ref[0]
        ni = now_ref[1]
        now_ref[0] = nr * sr - ni * si
        now_ref[1] = nr * si + ni * sr

    now_ref[...] = tw_ref[...]

    @pl.loop(0, 8, unroll=8)
    def _(cc):
        columns = []
        for half in range(2):
            re = a_ref[pl.ds(2 * cc + half, 128, stride=32), :]
            im = a_ref[pl.ds(2 * cc + half + 16, 128, stride=32), :]
            columns.append(jnp.concatenate([re, im], 0))
        u = dot3(t3_ref[...], jnp.concatenate(columns, 1))
        for half in range(2):
            ur = u[:256, 128 * half : 128 * half + 128]
            ui = u[256:, 128 * half : 128 * half + 128]
            nr = now_ref[0]
            ni = now_ref[1]
            u_ref[2 * cc + half, 0] = ur * nr - ui * ni
            u_ref[2 * cc + half, 1] = ur * ni + ui * nr
            advance()

    for copy in copies[3:]:
        copy.wait()

    lane = lax.broadcasted_iota(jnp.int32, (8, 128), 1)
    low = lane < 64

    def trade(first, second):
        middle_part = pltpu.roll(jnp.where(low, second, first), 64, 1)
        return jnp.where(low, first, middle_part), jnp.where(low, middle_part, second)

    @pl.loop(0, 32, unroll=4)
    def _(tile):
        rows = pl.ds(pl.multiple_of(tile * 8, 8), 8)
        values = [(u_ref[c, 0, rows, :], u_ref[c, 1, rows, :]) for c in range(16)]
        spectrum = transform_list(values)
        back = [None] * 16
        for index in range(8):
            g, r = index // 4, index % 4
            e = 8 * g + r
            grows = pl.ds(pl.multiple_of(tile * 8 + r * 256, 8), 8)
            lr = lane_ref[flip, 0, index : index + 1, :]
            li = lane_ref[flip, 1, index : index + 1, :]
            even_r, odd_r = trade(spectrum[e][0], spectrum[e + 4][0])
            even_i, odd_i = trade(spectrum[e][1], spectrum[e + 4][1])
            odd_r, odd_i = odd_r * lr - odd_i * li, odd_r * li + odd_i * lr
            products = []
            for h, (fr, fi) in enumerate(
                ((even_r + odd_r, even_i + odd_i), (even_r - odd_r, even_i - odd_i))
            ):
                gr = green_ref[g, h, 0, grows, :]
                gi = green_ref[g, h, 1, grows, :]
                products.append((gr * fr - gi * fi, gr * fi + gi * fr))
            (ar, ai), (br, bi) = products
            odd_r, odd_i = ar - br, ai - bi
            odd_r, odd_i = odd_r * lr + odd_i * li, odd_i * lr - odd_r * li
            first_r, second_r = trade(ar + br, odd_r)
            first_i, second_i = trade(ai + bi, odd_i)
            back[e] = (first_r, first_i)
            back[e + 4] = (second_r, second_i)
        for c, (re, im) in enumerate(inverse_list(back)):
            u_ref[c, 0, rows, :] = re
            u_ref[c, 1, rows, :] = im

    now_ref[...] = tw_ref[...]

    @pl.loop(0, 8, unroll=8)
    def _(cc):
        columns = []
        for half in range(2):
            ur = u_ref[2 * cc + half, 0]
            ui = u_ref[2 * cc + half, 1]
            nr = now_ref[0]
            ni = now_ref[1]
            columns.append(jnp.concatenate([ur * nr + ui * ni, ui * nr - ur * ni], 0))
            advance()
        out = dot3(t4_ref[...], jnp.concatenate(columns, 1))
        for half in range(2):
            lanes = slice(128 * half, 128 * half + 128)
            out_ref[pl.ds(2 * cc + half, 128, stride=32), :] = out[:128, lanes]
            out_ref[pl.ds(2 * cc + half + 16, 128, stride=32), :] = out[128:, lanes]

    last = pltpu.make_async_copy(out_ref, out_hbm, sent)
    last.start()
    last.wait()


def middle(a, greens, place):
    t = tables()
    return pl.pallas_call(
        middle_kernel,
        in_specs=[pl.BlockSpec(memory_space=pltpu.SMEM), spec_vmem()] + [spec_hbm()] * 9,
        out_specs=spec_hbm(),
        out_shape=pltpu.HBM((4096, 128), f32),
        scratch_shapes=[
            pltpu.VMEM((512, 768), bf16),
            pltpu.VMEM((2, 256, 128), f32),
            pltpu.VMEM((2, 256, 128), f32),
            pltpu.VMEM((2, 2, 2, 1024, 128), f32),
            pltpu.VMEM((2, 2, 8, 128), f32),
            pltpu.VMEM((256, 1536), bf16),
            pltpu.VMEM((16, 2, 256, 128), f32),
            pltpu.VMEM((2, 256, 128), f32),
            pltpu.VMEM((4096, 128), f32),
            pltpu.SemaphoreType.DMA((9,)),
            pltpu.SemaphoreType.DMA,
        ],
        compiler_params=params(24),
        cost_estimate=cost(2 * 8 * 2 * 512 * 65536 * 3, 10 << 20),
        name="middle",
    )(
        place, a, *in_hbm(t["t3"], t["tw3"], t["step3"], *greens, t["lane3"], t["t4"])
    )


def x_inverse_kernel(
    a_ref, t5_hbm, tw_hbm, t6_hbm, out_hbm, t5_ref, tw_ref, t6_ref, out_ref, arrived, sent
):
    for copy in fetch((t5_hbm, tw_hbm, t6_hbm), (t5_ref, tw_ref, t6_ref), arrived):
        copy.wait()

    @pl.loop(0, 8, unroll=8)
    def _(cc):
        columns = []
        for half in range(2):
            re = a_ref[pl.ds(2 * cc + half, 128, stride=32), :]
            im = a_ref[pl.ds(2 * cc + half + 16, 128, stride=32), :]
            columns.append(jnp.concatenate([re, im], 0))
        u = dot3(t5_ref[...], jnp.concatenate(columns, 1))
        rows = []
        for half in range(2):
            ur = u[:128, 128 * half : 128 * half + 128]
            ui = u[128:, 128 * half : 128 * half + 128]
            rows.append(
                jnp.concatenate(
                    [ur * tw_ref[0] - ui * tw_ref[1], ur * tw_ref[1] + ui * tw_ref[0]], 1
                )
            )
        out = dot3_nt(t6_ref[...], jnp.concatenate(rows, 0))
        for half in range(2):
            lanes = slice(128 * half, 128 * half + 128)
            for b0 in range(2):
                b = 2 * (2 * cc + half) + b0
                out_ref[pl.ds(b, 32, stride=64), :] = out[64 * b0 : 64 * b0 + 32, lanes]
                out_ref[pl.ds(b + 32, 32, stride=64), :] = out[64 * b0 + 32 : 64 * b0 + 64, lanes]

    last = pltpu.make_async_copy(out_ref, out_hbm, sent)
    last.start()
    last.wait()


def x_inverse(a):
    t = tables()
    return pl.pallas_call(
        x_inverse_kernel,
        in_specs=[spec_vmem()] + [spec_hbm()] * 3,
        out_specs=spec_hbm(),
        out_shape=pltpu.HBM((2048, 128), f32),
        scratch_shapes=[
            pltpu.VMEM((256, 768), bf16),
            pltpu.VMEM((2, 128, 128), f32),
            pltpu.VMEM((128, 768), bf16),
            pltpu.VMEM((2048, 128), f32),
            pltpu.SemaphoreType.DMA((3,)),
            pltpu.SemaphoreType.DMA,
        ],
        compiler_params=params(8),
        cost_estimate=cost(2 * 2048 * 65536 * 4, 4 << 20),
        name="x_inverse",
    )(a, *in_hbm(t["t5"], t["tw5"], t["t6"]))


def residual_kernel(a_ref, incident_ref, contrast_ref, source_ref, out_ref):
    for tile in range(4):
        lanes = slice(128 * tile, 128 * tile + 128)
        field = []
        for part in range(2):
            rows = []
            for block in range(4):
                first = 256 * tile + block * 64 + part * 32
                rows.append(a_ref[first : first + 32, :])
            field.append(incident_ref[part, :, lanes] + jnp.concatenate(rows, 0).T)
        cr = contrast_ref[0, :, lanes]
        ci = contrast_ref[1, :, lanes]
        out_ref[0, :, lanes] = cr * field[0] - ci * field[1] - source_ref[0, :, lanes]
        out_ref[1, :, lanes] = cr * field[1] + ci * field[0] - source_ref[1, :, lanes]


def residual_of(a, incident, contrast, source):
    tile = pl.BlockSpec((2, 128, 512), lambda t: (0, 0, t))
    return pl.pallas_call(
        residual_kernel,
        grid=(2,),
        in_specs=[pl.BlockSpec((1024, 128), lambda t: (t, 0)), tile, tile, tile],
        out_specs=tile,
        out_shape=jax.ShapeDtypeStruct((2, 128, 1024), f32),
        compiler_params=params(),
        cost_estimate=cost(0, 5 << 20),
        name="residual",
    )(a, incident, contrast, source)


def pack_kernel(across, place_ref, green_ref, *out_refs):
    flip = place_ref[0]
    lane = lax.broadcasted_iota(jnp.int32, (512, 128), 1)
    low = lane < 64
    pick = low == (flip == 0)
    for part in range(2):
        first = green_ref[part, 0]
        second = green_ref[part, 1]
        straight = jnp.where(low, first, second)
        crossed = pltpu.roll(jnp.where(low, second, first), 64, 1)
        for core, value in enumerate(
            (jnp.where(pick, straight, crossed), jnp.where(pick, crossed, straight))
        ):
            if across:
                out_refs[0][core, part] = value
            else:
                out_refs[core][part] = value


def pack_green(green, place, across):
    if across:
        out_specs = pl.BlockSpec((2, 2, 512, 128), lambda t, place_ref: (0, 0, t, 0))
        out_shape = pltpu.HBM((2, 2, 1024, 128), f32)
    else:
        out_specs = [pl.BlockSpec((2, 512, 128), lambda t, place_ref: (0, t, 0))] * 2
        out_shape = [pltpu.HBM((2, 1024, 128), f32)] * 2

    def column(t, place_ref):
        return 0, 0, t, jnp.where(place_ref[1] == 1, 1 - across, across)

    return pl.pallas_call(
        functools.partial(pack_kernel, across),
        grid_spec=pltpu.PrefetchScalarGridSpec(
            num_scalar_prefetch=1,
            grid=(2,),
            in_specs=[pl.BlockSpec((2, 2, 512, 128), column)],
            out_specs=out_specs,
        ),
        out_shape=out_shape,
        compiler_params=params(),
        cost_estimate=cost(0, 4 << 20),
        name="pack_far" if across else "pack_near",
    )(place, *in_hbm(green.reshape(2, 2, 1024, 256)))


def project_kernel(source_ref, ea_ref, eb_ref, row_ref, out_ref, lhs_ref, rhs_ref):
    @pl.when(pl.program_id(0) == 0)
    def _():
        re = source_ref[0]
        im = source_ref[1]
        for rows, cols, value in (
            (0, 0, re), (0, 1024, -im), (128, 0, im), (128, 1024, re),
        ):
            high, low = split(value)
            lhs_ref[0, rows : rows + 128, cols : cols + 1024] = high
            lhs_ref[1, rows : rows + 128, cols : cols + 1024] = low

    br = eb_ref[0]
    bi = eb_ref[1]
    for a in range(32):
        ar = ea_ref[0, a : a + 1, :]
        ai = ea_ref[1, a : a + 1, :]
        for part, value in ((0, ar * br - ai * bi), (1, ar * bi + ai * br)):
            high, low = split(value)
            rhs_ref[0, part * 1024 + a * 32 : part * 1024 + a * 32 + 32, :] = high
            rhs_ref[1, part * 1024 + a * 32 : part * 1024 + a * 32 + 32, :] = low
    inner = dot(lhs_ref[0], rhs_ref[0]) + (dot(lhs_ref[0], rhs_ref[1]) + dot(lhs_ref[1], rhs_ref[0]))
    ir = inner[:128]
    ii = inner[128:]
    fr = row_ref[0]
    fi = row_ref[1]
    pr = jnp.sum(fr * ir - fi * ii, axis=0, keepdims=True)
    pi_ = jnp.sum(fr * ii + fi * ir, axis=0, keepdims=True)
    out_ref[...] = jnp.concatenate([pr, pi_, jnp.zeros((6, pr.shape[1]), f32)], 0)


def project(source, ea, eb, rows):
    tile = 256
    whole = pl.BlockSpec((2, 128, 1024), lambda t: (0, 0, 0))
    return pl.pallas_call(
        project_kernel,
        grid=(R // tile,),
        in_specs=[
            whole,
            pl.BlockSpec((2, 32, tile), lambda t: (0, 0, t)),
            pl.BlockSpec((2, 32, tile), lambda t: (0, 0, t)),
            pl.BlockSpec((2, 128, tile), lambda t: (0, 0, t)),
        ],
        out_specs=pl.BlockSpec((8, tile), lambda t: (0, t)),
        out_shape=jax.ShapeDtypeStruct((8, R), f32),
        scratch_shapes=[pltpu.VMEM((2, 256, 2048), bf16), pltpu.VMEM((2, 2048, tile), bf16)],
        compiler_params=params(),
        cost_estimate=cost(2 * 256 * 2048 * 1024 * 3, 4 << 20),
        name="project",
    )(source, ea, eb, rows)


def backproject_kernel(weight_ref, ea_ref, eb_ref, out_ref, lhs_ref, rhs_ref):
    @pl.when(pl.program_id(0) == 0)
    def _():
        wr = weight_ref[0]
        wi = weight_ref[1]
        for rows, cols, value in (
            (0, 0, wr), (0, 1024, wi), (128, 0, wi), (128, 1024, -wr),
        ):
            high, low = split(value)
            lhs_ref[0, rows : rows + 128, cols : cols + 1024] = high
            lhs_ref[1, rows : rows + 128, cols : cols + 1024] = low

    br = eb_ref[0]
    bi = eb_ref[1]
    for a in range(8):
        ar = ea_ref[0, a : a + 1, :]
        ai = ea_ref[1, a : a + 1, :]
        for part, value in ((0, ar * br - ai * bi), (1, ar * bi + ai * br)):
            high, low = split(value)
            rhs_ref[0, a * 32 : a * 32 + 32, part * 1024 : part * 1024 + 1024] = high
            rhs_ref[1, a * 32 : a * 32 + 32, part * 1024 : part * 1024 + 1024] = low
    out = dot_nt(lhs_ref[0], rhs_ref[0]) + (
        dot_nt(lhs_ref[0], rhs_ref[1]) + dot_nt(lhs_ref[1], rhs_ref[0])
    )
    out_ref[0] = out[:128]
    out_ref[1] = out[128:]


def backproject(weights, ea, eb):
    whole = pl.BlockSpec((2, 128, 1024), lambda t: (0, 0, 0))
    return pl.pallas_call(
        backproject_kernel,
        grid=(4,),
        in_specs=[
            whole,
            pl.BlockSpec((2, 8, 1024), lambda t: (0, t, 0)),
            pl.BlockSpec((2, 32, 1024), lambda t: (0, 0, 0)),
        ],
        out_specs=pl.BlockSpec((2, 128, 256), lambda t: (0, 0, t)),
        out_shape=jax.ShapeDtypeStruct((2, 128, 1024), f32),
        scratch_shapes=[pltpu.VMEM((2, 256, 2048), bf16), pltpu.VMEM((2, 256, 2048), bf16)],
        compiler_params=params(),
        cost_estimate=cost(2 * 256 * 2048 * 1024 * 3, 4 << 20),
        name="backproject",
    )(weights, ea, eb)


def phase_pair(position, direction):
    phase = (wave_step * position)[:, None] * direction[None, :]
    return jnp.stack([jnp.cos(phase), -jnp.sin(phase)])


def sum_over(value, steps):
    def exchange(value, axis, size, strides):
        parts = [value] + [
            lax.ppermute(value, axis, [(j, j ^ stride) for j in range(size)]) for stride in strides
        ]
        while len(parts) > 1:
            parts = [parts[j] + parts[j + 1] for j in range(0, len(parts), 2)]
        return parts[0]

    for axis, size, strides in steps:
        value = exchange(value, axis, size, strides)
    return value


def local(sources, incident, contrast, green, angles, measured):
    wide = lax.axis_index("wide")
    narrow = lax.axis_index("narrow")
    place = jnp.stack([narrow % 2, narrow // 2]).astype(jnp.int32)
    source = sources[0]

    def partner(value, k):
        return lax.ppermute(value, "narrow", [(j, j ^ k) for j in range(NARROW)])

    lines = columns_major(source)
    lines, green = lax.optimization_barrier((lines, green))
    far = partner(pack_green(green, place, 1), 2)
    lines = lax.all_to_all(lines.reshape(WIDE, 64, 128), "wide", 0, 0, tiled=True)

    row_position = (wide * 128 + jnp.arange(128, dtype=jnp.int32)).astype(f32) - N // 2 + 0.5
    block_position = (narrow * 1024 + 32 * jnp.arange(32, dtype=jnp.int32)).astype(f32) - N // 2 + 0.5
    cell_position = jnp.arange(32, dtype=jnp.int32).astype(f32)
    rows = phase_pair(row_position, jnp.cos(angles))
    sine = jnp.sin(angles)
    ea = phase_pair(block_position, sine)
    eb = phase_pair(cell_position, sine)
    partial_value = project(source, ea, eb, rows)
    lines, partial_value = lax.optimization_barrier((lines, partial_value))
    lines = x_forward(lines.reshape(2048, 128))
    lines, partial_value = lax.optimization_barrier((lines, partial_value))
    lines = lax.all_to_all(lines.reshape(128, 32, 128), ("wide", "narrow"), 0, 0, tiled=True)

    total = sum_over(partial_value, [("wide", WIDE, (1, 2, 3))])
    total, green = lax.optimization_barrier((total, green))
    near = pack_green(green, place, 0)
    near_partner = partner(near[1], 1)
    total = sum_over(total, [("wide", WIDE, (8, 16, 24))])
    total, far, near_partner = lax.optimization_barrier((total, far, near_partner))
    total = sum_over(total, [("narrow", NARROW, (1,))])
    greens = [near[0], near_partner, far, partner(far[1], 1)]
    total, lines = lax.optimization_barrier((total, lines))
    lines = middle(lines.reshape(4096, 128), greens, place)
    total, lines = lax.optimization_barrier((total, lines))
    lines = lax.all_to_all(lines.reshape(128, 32, 128), ("wide", "narrow"), 0, 0, tiled=True)
    total = sum_over(total, [("wide", WIDE, (4,)), ("narrow", NARROW, (2,))])[:2]
    lines = x_inverse(lines.reshape(4096, 128))
    lines = lax.all_to_all(lines.reshape(WIDE, 64, 128), "wide", 0, 0, tiled=True)
    residual = residual_of(lines.reshape(2048, 128), incident[0], contrast, source)

    data_residual = measured - total[None] * (1.0 / N)
    rho_real = data_residual[0, 0][None, :]
    rho_imag = data_residual[0, 1][None, :]
    scale = 1.0 / math.sqrt(R)
    weights = jnp.stack(
        [
            (rows[0] * rho_real + rows[1] * rho_imag) * scale,
            (rows[0] * rho_imag - rows[1] * rho_real) * scale,
        ]
    )
    back = backproject(weights, ea, eb)
    return (residual[None], back[None], data_residual)


def solution(mesh):
    placed = (
        P(None, None, "wide", "narrow"),
        P(None, None, "wide", "narrow"),
        P(None, "wide", "narrow"),
        P(None, "narrow", "wide"),
        P(),
        P(),
    )
    return jax.shard_map(
        local,
        mesh=mesh,
        in_specs=placed,
        out_specs=(P(None, None, "wide", "narrow"), P(None, None, "wide", "narrow"), P()),
        check_vma=False,
    )
```

```python
import functools
import math

import jax
import jax.numpy as jnp
import ml_dtypes
import numpy as np
from jax import lax
from jax.experimental import pallas as pl
from jax.experimental.pallas import tpu as pltpu
from jax.sharding import PartitionSpec as P

N = 4096
R = 1024
M = 8192
WIDE = 32
NARROW = 4

wave_step = 0.2 * math.pi
f32 = jnp.float32
bf16 = jnp.bfloat16


def complex_block(table):
    return np.block([[table.real, -table.imag], [table.imag, table.real]])


def terms(table):
    high = table.astype(np.float32).astype(ml_dtypes.bfloat16)
    low = (table - high.astype(np.float64)).astype(np.float32).astype(ml_dtypes.bfloat16)
    return np.concatenate([high, high, low], 1)


def root(product, length, sign):
    return np.exp(sign * 2j * np.pi * (product % length) / length)


def pair(table):
    return np.stack([table.real, table.imag]).astype(np.float32)


@functools.lru_cache(None)
def tables():
    out = {}
    w = np.arange(32)
    k1 = np.arange(64)
    i = np.arange(128)
    m = np.arange(128)
    out["t1"] = terms(complex_block(root(np.outer(k1, w), 64, -1)))
    out["tw1"] = pair(root(np.outer(k1, i), M, -1))
    out["t2"] = terms(complex_block(root(np.outer(m, i), 128, -1)))
    d = np.arange(128)
    s = 32 * (d % 4) + d // 4
    c1 = np.arange(256)
    out["t3"] = terms(complex_block(root(np.outer(c1, s), 256, -1)))
    low_half = np.arange(128) < 64
    first = np.where(low_half[None, :], 1.0, root(c1, M, -1)[:, None])
    out["tw3"] = pair(first)
    out["step3"] = pair(root(2 * c1, M, -1)[:, None] * np.ones((1, 128)))
    lanes = []
    for flip in (0, 1):
        first_e = (np.array([0, 1, 2, 3, 8, 9, 10, 11]) + 8 * flip) % 16
        e = np.where(low_half[None, :], first_e[:, None], first_e[:, None] + 4)
        lanes.append(pair(root(e, 32, -1)))
    out["lane3"] = np.stack(lanes)
    out["t4"] = terms(complex_block(root(np.outer(s, c1), 256, 1)))
    out["t5"] = terms(complex_block(root(np.outer(i, m), 128, 1)))
    lane_k1 = np.arange(128) % 64
    out["tw5"] = pair(root(np.outer(i, lane_k1), M, 1))
    inner = root(np.outer(w, k1), 64, 1) / (M * M)
    block = np.zeros((2, 2, 32, 2, 2, 64))
    for b0 in (0, 1):
        block[b0, 0, :, 0, b0, :] = inner.real
        block[b0, 0, :, 1, b0, :] = -inner.imag
        block[b0, 1, :, 0, b0, :] = inner.imag
        block[b0, 1, :, 1, b0, :] = inner.real
    out["t6"] = terms(block.reshape(128, 256))
    return out


def split(values):
    high = values.astype(bf16)
    low = (values - high.astype(f32)).astype(bf16)
    return high, low


def dot(a, b):
    return lax.dot_general(a, b, (((1,), (0,)), ((), ())), preferred_element_type=f32)


def dot_nt(a, b):
    return lax.dot_general(a, b, (((1,), (1,)), ((), ())), preferred_element_type=f32)


def dot3(table, values):
    high, low = split(values)
    return dot(table, jnp.concatenate([high, low, high], 0))


def dot3_nt(table, values):
    high, low = split(values)
    return dot_nt(table, jnp.concatenate([high, low, high], 1))


def times_root(value, numerator, length):
    re, im = value
    numerator %= length
    if numerator == 0:
        return value
    if 4 * numerator == length:
        return im, -re
    if 2 * numerator == length:
        return -re, -im
    if 4 * numerator == 3 * length:
        return -im, re
    if 8 * numerator == length:
        half = math.sqrt(0.5)
        return (re + im) * half, (im - re) * half
    if 8 * numerator == 3 * length:
        half = math.sqrt(0.5)
        return (im - re) * half, (-re - im) * half
    cosine = math.cos(2 * math.pi * numerator / length)
    sine = -math.sin(2 * math.pi * numerator / length)
    return re * cosine - im * sine, re * sine + im * cosine


def transform_list(values):
    count = len(values)
    if count == 1:
        return values
    if count == 2:
        (ar, ai), (br, bi) = values
        return [(ar + br, ai + bi), (ar - br, ai - bi)]
    if count == 4:
        (ar, ai), (br, bi), (cr, ci), (dr, di) = values
        pr, pi_, qr, qi = ar + cr, ai + ci, ar - cr, ai - ci
        sr, si, tr, ti = br + dr, bi + di, br - dr, bi - di
        return [(pr + sr, pi_ + si), (qr + ti, qi - tr), (pr - sr, pi_ - si), (qr - ti, qi + tr)]
    parts = [transform_list(values[start::4]) for start in range(4)]
    quarter = count // 4
    out = [None] * count
    for k in range(quarter):
        column = [times_root(parts[j][k], j * k, count) for j in range(4)]
        for q, value in enumerate(transform_list(column)):
            out[k + q * quarter] = value
    return out


def inverse_list(values):
    swapped = transform_list([(im, re) for re, im in values])
    return [(re, im) for im, re in swapped]


def spec_vmem():
    return pl.BlockSpec(memory_space=pltpu.VMEM)


def spec_hbm():
    return pl.BlockSpec(memory_space=pltpu.HBM)


def in_hbm(*values):
    return [pltpu.with_memory_space_constraint(jnp.asarray(value), pltpu.HBM) for value in values]


def fetch(sources, targets, arrived):
    copies = [
        pltpu.make_async_copy(source, target, arrived.at[k])
        for k, (source, target) in enumerate(zip(sources, targets))
    ]
    for copy in copies:
        copy.start()
    return copies


def params(mebibytes=16):
    return pltpu.CompilerParams(vmem_limit_bytes=mebibytes << 20)


def cost(flops, bytes_accessed):
    return pl.CostEstimate(flops=flops, bytes_accessed=bytes_accessed, transcendentals=0)


def columns_kernel(source_ref, out_ref):
    for tile in range(4):
        for part in range(2):
            turned = source_ref[part, :, 128 * tile : 128 * tile + 128].T
            for block in range(4):
                first = 256 * tile + block * 64 + part * 32
                out_ref[first : first + 32, :] = turned[block * 32 : block * 32 + 32]


def columns_major(source):
    return pl.pallas_call(
        columns_kernel,
        grid=(2,),
        in_specs=[pl.BlockSpec((2, 128, 512), lambda t: (0, 0, t))],
        out_specs=pl.BlockSpec((1024, 128), lambda t: (t, 0)),
        out_shape=pltpu.HBM((2048, 128), f32),
        cost_estimate=cost(0, 2 << 20),
        name="columns_major",
    )(source)


def x_forward_kernel(
    a_ref, t1_hbm, tw_hbm, t2_hbm, out_hbm, t1_ref, tw_ref, t2_ref, out_ref, arrived, sent
):
    for copy in fetch((t1_hbm, tw_hbm, t2_hbm), (t1_ref, tw_ref, t2_ref), arrived):
        copy.wait()

    @pl.loop(0, 16, unroll=8)
    def _(c):
        columns = []
        for b0 in range(2):
            re = a_ref[pl.ds(2 * c + b0, 32, stride=64), :]
            im = a_ref[pl.ds(2 * c + b0 + 32, 32, stride=64), :]
            columns.append(jnp.concatenate([re, im], 0))
        u = dot3(t1_ref[...], jnp.concatenate(columns, 1))
        rows = []
        for b0 in range(2):
            ur = u[:64, 128 * b0 : 128 * b0 + 128]
            ui = u[64:, 128 * b0 : 128 * b0 + 128]
            rows.append(
                jnp.concatenate(
                    [ur * tw_ref[0] - ui * tw_ref[1], ur * tw_ref[1] + ui * tw_ref[0]], 1
                )
            )
        z = jnp.concatenate(rows, 0)
        out = dot3_nt(t2_ref[...], z)
        out_ref[pl.ds(c, 128, stride=32), :] = out[:128]
        out_ref[pl.ds(c + 16, 128, stride=32), :] = out[128:]

    last = pltpu.make_async_copy(out_ref, out_hbm, sent)
    last.start()
    last.wait()


def x_forward(a):
    t = tables()
    return pl.pallas_call(
        x_forward_kernel,
        in_specs=[spec_vmem()] + [spec_hbm()] * 3,
        out_specs=spec_hbm(),
        out_shape=pltpu.HBM((4096, 128), f32),
        scratch_shapes=[
            pltpu.VMEM((128, 192), bf16),
            pltpu.VMEM((2, 64, 128), f32),
            pltpu.VMEM((256, 768), bf16),
            pltpu.VMEM((4096, 128), f32),
            pltpu.SemaphoreType.DMA((3,)),
            pltpu.SemaphoreType.DMA,
        ],
        compiler_params=params(8),
        cost_estimate=cost(2 * 2048 * 65536 * 4, 4 << 20),
        name="x_forward",
    )(a, *in_hbm(t["t1"], t["tw1"], t["t2"]))


def line_row(c):
    return c // 8 * 16 + c % 8


def middle_kernel(
    place_ref, a_ref, t3_hbm, tw_hbm, step_hbm, r0_hbm, r1_hbm, r2_hbm, r3_hbm, lane_hbm, t4_hbm,
    out_hbm, t3_ref, tw_ref, step_ref, green_ref, lane_ref, t4_ref, u_ref, now_ref, out_ref,
    arrived, sent,
):
    flip = place_ref[0]
    upper = place_ref[1]
    copies = fetch(
        (t3_hbm, tw_hbm, step_hbm, r0_hbm, r1_hbm, r2_hbm.at[0], r3_hbm, lane_hbm, t4_hbm),
        (t3_ref, tw_ref, step_ref)
        + tuple(green_ref.at[g, h] for h in (upper, 1 - upper) for g in range(2))
        + (lane_ref, t4_ref),
        arrived,
    )
    for copy in copies[:3]:
        copy.wait()
    sign = 1.0 - 2.0 * flip.astype(f32)

    def advance():
        sr = step_ref[0] * sign
        si = step_ref[1] * sign
        nr = now_ref[0]
        ni = now_ref[1]
        now_ref[0] = nr * sr - ni * si
        now_ref[1] = nr * si + ni * sr

    now_ref[...] = tw_ref[...]

    @pl.loop(0, 8, unroll=8)
    def _(cc):
        columns = []
        for half in range(2):
            re = a_ref[pl.ds(2 * cc + half, 128, stride=32), :]
            im = a_ref[pl.ds(2 * cc + half + 16, 128, stride=32), :]
            columns.append(jnp.concatenate([re, im], 0))
        u = dot3(t3_ref[...], jnp.concatenate(columns, 1))
        for half in range(2):
            ur = u[:256, 128 * half : 128 * half + 128]
            ui = u[256:, 128 * half : 128 * half + 128]
            nr = now_ref[0]
            ni = now_ref[1]
            u_ref[2 * cc + half, 0] = ur * nr - ui * ni
            u_ref[2 * cc + half, 1] = ur * ni + ui * nr
            advance()

    for copy in copies[3:]:
        copy.wait()

    lane = lax.broadcasted_iota(jnp.int32, (8, 128), 1)
    low = lane < 64

    def trade(first, second):
        middle_part = pltpu.roll(jnp.where(low, second, first), 64, 1)
        return jnp.where(low, first, middle_part), jnp.where(low, middle_part, second)

    @pl.loop(0, 32, unroll=4)
    def _(tile):
        rows = pl.ds(pl.multiple_of(tile * 8, 8), 8)
        values = [(u_ref[c, 0, rows, :], u_ref[c, 1, rows, :]) for c in range(16)]
        spectrum = transform_list(values)
        back = [None] * 16
        for index in range(8):
            g, r = index // 4, index % 4
            e = 8 * g + r
            grows = pl.ds(pl.multiple_of(tile * 8 + r * 256, 8), 8)
            lr = lane_ref[flip, 0, index : index + 1, :]
            li = lane_ref[flip, 1, index : index + 1, :]
            even_r, odd_r = trade(spectrum[e][0], spectrum[e + 4][0])
            even_i, odd_i = trade(spectrum[e][1], spectrum[e + 4][1])
            odd_r, odd_i = odd_r * lr - odd_i * li, odd_r * li + odd_i * lr
            products = []
            for h, (fr, fi) in enumerate(
                ((even_r + odd_r, even_i + odd_i), (even_r - odd_r, even_i - odd_i))
            ):
                gr = green_ref[g, h, 0, grows, :]
                gi = green_ref[g, h, 1, grows, :]
                products.append((gr * fr - gi * fi, gr * fi + gi * fr))
            (ar, ai), (br, bi) = products
            odd_r, odd_i = ar - br, ai - bi
            odd_r, odd_i = odd_r * lr + odd_i * li, odd_i * lr - odd_r * li
            first_r, second_r = trade(ar + br, odd_r)
            first_i, second_i = trade(ai + bi, odd_i)
            back[e] = (first_r, first_i)
            back[e + 4] = (second_r, second_i)
        for c, (re, im) in enumerate(inverse_list(back)):
            u_ref[c, 0, rows, :] = re
            u_ref[c, 1, rows, :] = im

    now_ref[...] = tw_ref[...]

    halves = []
    for cc in range(8):
        columns = []
        for half in range(2):
            ur = u_ref[2 * cc + half, 0]
            ui = u_ref[2 * cc + half, 1]
            nr = now_ref[0]
            ni = now_ref[1]
            columns.append(jnp.concatenate([ur * nr + ui * ni, ui * nr - ur * ni], 0))
            advance()
        out = dot3(t4_ref[...], jnp.concatenate(columns, 1))
        for half in range(2):
            lanes = slice(128 * half, 128 * half + 128)
            row = line_row(2 * cc + half)
            out_ref[pl.ds(row, 128, stride=32), :] = out[:128, lanes]
            out_ref[pl.ds(row + 8, 128, stride=32), :] = out[128:, lanes]
        if cc % 4 == 3:
            rows = pl.ds(cc // 4 * 16, 16)
            halves.append(
                pltpu.make_async_copy(
                    out_ref.reshape(128, 32, 128).at[:, rows], out_hbm.at[:, rows], sent.at[cc // 4]
                )
            )
            halves[-1].start()
    for copy in halves:
        copy.wait()


def middle(a, greens, place):
    t = tables()
    return pl.pallas_call(
        middle_kernel,
        in_specs=[pl.BlockSpec(memory_space=pltpu.SMEM), spec_vmem()] + [spec_hbm()] * 9,
        out_specs=spec_hbm(),
        out_shape=pltpu.HBM((128, 32, 128), f32),
        scratch_shapes=[
            pltpu.VMEM((512, 768), bf16),
            pltpu.VMEM((2, 256, 128), f32),
            pltpu.VMEM((2, 256, 128), f32),
            pltpu.VMEM((2, 2, 2, 1024, 128), f32),
            pltpu.VMEM((2, 2, 8, 128), f32),
            pltpu.VMEM((256, 1536), bf16),
            pltpu.VMEM((16, 2, 256, 128), f32),
            pltpu.VMEM((2, 256, 128), f32),
            pltpu.VMEM((4096, 128), f32),
            pltpu.SemaphoreType.DMA((9,)),
            pltpu.SemaphoreType.DMA((2,)),
        ],
        compiler_params=params(24),
        cost_estimate=cost(2 * 8 * 2 * 512 * 65536 * 3, 10 << 20),
        name="middle",
    )(
        place, a, *in_hbm(t["t3"], t["tw3"], t["step3"], *greens, t["lane3"], t["t4"])
    )


def x_inverse_kernel(
    a_ref, t5_hbm, tw_hbm, t6_hbm, out_hbm, t5_ref, tw_ref, t6_ref, out_ref, arrived, sent
):
    for copy in fetch((t5_hbm, tw_hbm, t6_hbm), (t5_ref, tw_ref, t6_ref), arrived):
        copy.wait()

    blocks = []
    for cc in range(8):
        columns = []
        for half in range(2):
            row = line_row(2 * cc + half)
            re = a_ref[pl.ds(row, 128, stride=32), :]
            im = a_ref[pl.ds(row + 8, 128, stride=32), :]
            columns.append(jnp.concatenate([re, im], 0))
        u = dot3(t5_ref[...], jnp.concatenate(columns, 1))
        rows = []
        for half in range(2):
            ur = u[:128, 128 * half : 128 * half + 128]
            ui = u[128:, 128 * half : 128 * half + 128]
            rows.append(
                jnp.concatenate(
                    [ur * tw_ref[0] - ui * tw_ref[1], ur * tw_ref[1] + ui * tw_ref[0]], 1
                )
            )
        out = dot3_nt(t6_ref[...], jnp.concatenate(rows, 0))
        for half in range(2):
            lanes = slice(128 * half, 128 * half + 128)
            for b0 in range(2):
                row = line_row(4 * cc + 2 * half + b0)
                out_ref[pl.ds(row, 32, stride=64), :] = out[64 * b0 : 64 * b0 + 32, lanes]
                out_ref[pl.ds(row + 8, 32, stride=64), :] = out[64 * b0 + 32 : 64 * b0 + 64, lanes]
        if cc % 2 == 1:
            rows = pl.ds(cc // 2 * 16, 16)
            blocks.append(
                pltpu.make_async_copy(
                    out_ref.reshape(32, 64, 128).at[:, rows], out_hbm.at[:, rows], sent.at[cc // 2]
                )
            )
            blocks[-1].start()
    for copy in blocks:
        copy.wait()


def x_inverse(a):
    t = tables()
    return pl.pallas_call(
        x_inverse_kernel,
        in_specs=[spec_vmem()] + [spec_hbm()] * 3,
        out_specs=spec_hbm(),
        out_shape=pltpu.HBM((32, 64, 128), f32),
        scratch_shapes=[
            pltpu.VMEM((256, 768), bf16),
            pltpu.VMEM((2, 128, 128), f32),
            pltpu.VMEM((128, 768), bf16),
            pltpu.VMEM((2048, 128), f32),
            pltpu.SemaphoreType.DMA((3,)),
            pltpu.SemaphoreType.DMA((4,)),
        ],
        compiler_params=params(8),
        cost_estimate=cost(2 * 2048 * 65536 * 4, 4 << 20),
        name="x_inverse",
    )(a, *in_hbm(t["t5"], t["tw5"], t["t6"]))


def residual_kernel(a_ref, contrast_ref, known_ref, out_ref):
    for tile in range(4):
        lanes = slice(128 * tile, 128 * tile + 128)
        scattered = []
        for part in range(2):
            rows = []
            for block in range(16):
                first = 256 * tile + block * 16 + part * 8
                rows.append(a_ref[first : first + 8, :])
            scattered.append(jnp.concatenate(rows, 0).T)
        cr = contrast_ref[0, :, lanes]
        ci = contrast_ref[1, :, lanes]
        out_ref[0, :, lanes] = cr * scattered[0] - ci * scattered[1] + known_ref[0, :, lanes]
        out_ref[1, :, lanes] = cr * scattered[1] + ci * scattered[0] + known_ref[1, :, lanes]


def residual_of(a, contrast, known):
    tile = pl.BlockSpec((2, 128, 512), lambda t: (0, 0, t))
    return pl.pallas_call(
        residual_kernel,
        grid=(2,),
        in_specs=[pl.BlockSpec((1024, 128), lambda t: (t, 0)), tile, tile],
        out_specs=tile,
        out_shape=jax.ShapeDtypeStruct((2, 128, 1024), f32),
        compiler_params=params(),
        cost_estimate=cost(0, 4 << 20),
        name="residual",
    )(a, contrast, known)


def pack_kernel(across, place_ref, green_ref, *out_refs):
    flip = place_ref[0]
    lane = lax.broadcasted_iota(jnp.int32, (512, 128), 1)
    low = lane < 64
    pick = low == (flip == 0)
    for part in range(2):
        first = green_ref[part, 0]
        second = green_ref[part, 1]
        straight = jnp.where(low, first, second)
        crossed = pltpu.roll(jnp.where(low, second, first), 64, 1)
        for core, value in enumerate(
            (jnp.where(pick, straight, crossed), jnp.where(pick, crossed, straight))
        ):
            if across:
                out_refs[0][core, part] = value
            else:
                out_refs[core][part] = value


def pack_green(green, place, across):
    if across:
        out_specs = pl.BlockSpec((2, 2, 512, 128), lambda t, place_ref: (0, 0, t, 0))
        out_shape = pltpu.HBM((2, 2, 1024, 128), f32)
    else:
        out_specs = [pl.BlockSpec((2, 512, 128), lambda t, place_ref: (0, t, 0))] * 2
        out_shape = [pltpu.HBM((2, 1024, 128), f32)] * 2

    def column(t, place_ref):
        return 0, 0, t, jnp.where(place_ref[1] == 1, 1 - across, across)

    return pl.pallas_call(
        functools.partial(pack_kernel, across),
        grid_spec=pltpu.PrefetchScalarGridSpec(
            num_scalar_prefetch=1,
            grid=(2,),
            in_specs=[pl.BlockSpec((2, 2, 512, 128), column)],
            out_specs=out_specs,
        ),
        out_shape=out_shape,
        compiler_params=params(),
        cost_estimate=cost(0, 4 << 20),
        name="pack_far" if across else "pack_near",
    )(place, *in_hbm(green.reshape(2, 2, 1024, 256)))


def second_kernel(in_ref, out_ref):
    out_ref[...] = in_ref[0]


def second_of(values):
    return pl.pallas_call(
        second_kernel,
        grid=(2,),
        in_specs=[pl.BlockSpec((1, 1, 1024, 128), lambda t: (1, t, 0, 0))],
        out_specs=pl.BlockSpec((1, 1024, 128), lambda t: (t, 0, 0)),
        out_shape=pltpu.HBM(values.shape[1:], f32),
        compiler_params=params(8),
        cost_estimate=cost(0, 2 << 20),
        name="second",
    )(*in_hbm(values))


def project_kernel(source_ref, ea_ref, eb_ref, row_ref, out_ref, lhs_ref, rhs_ref):
    @pl.when(pl.program_id(0) == 0)
    def _():
        re = source_ref[0]
        im = source_ref[1]
        for rows, cols, value in (
            (0, 0, re), (0, 1024, -im), (128, 0, im), (128, 1024, re),
        ):
            high, low = split(value)
            lhs_ref[0, rows : rows + 128, cols : cols + 1024] = high
            lhs_ref[1, rows : rows + 128, cols : cols + 1024] = low

    br = eb_ref[0]
    bi = eb_ref[1]
    for a in range(32):
        ar = ea_ref[0, a : a + 1, :]
        ai = ea_ref[1, a : a + 1, :]
        for part, value in ((0, ar * br - ai * bi), (1, ar * bi + ai * br)):
            high, low = split(value)
            rhs_ref[0, part * 1024 + a * 32 : part * 1024 + a * 32 + 32, :] = high
            rhs_ref[1, part * 1024 + a * 32 : part * 1024 + a * 32 + 32, :] = low
    inner = dot(lhs_ref[0], rhs_ref[0]) + (dot(lhs_ref[0], rhs_ref[1]) + dot(lhs_ref[1], rhs_ref[0]))
    ir = inner[:128]
    ii = inner[128:]
    fr = row_ref[0]
    fi = row_ref[1]
    pr = jnp.sum(fr * ir - fi * ii, axis=0, keepdims=True)
    pi_ = jnp.sum(fr * ii + fi * ir, axis=0, keepdims=True)
    out_ref[...] = jnp.concatenate([pr, pi_, jnp.zeros((6, pr.shape[1]), f32)], 0)


def project(source, ea, eb, rows):
    tile = 256
    whole = pl.BlockSpec((2, 128, 1024), lambda t: (0, 0, 0))
    return pl.pallas_call(
        project_kernel,
        grid=(R // tile,),
        in_specs=[
            whole,
            pl.BlockSpec((2, 32, tile), lambda t: (0, 0, t)),
            pl.BlockSpec((2, 32, tile), lambda t: (0, 0, t)),
            pl.BlockSpec((2, 128, tile), lambda t: (0, 0, t)),
        ],
        out_specs=pl.BlockSpec((8, tile), lambda t: (0, t)),
        out_shape=jax.ShapeDtypeStruct((8, R), f32),
        scratch_shapes=[pltpu.VMEM((2, 256, 2048), bf16), pltpu.VMEM((2, 2048, tile), bf16)],
        compiler_params=params(),
        cost_estimate=cost(2 * 256 * 2048 * 1024 * 3, 4 << 20),
        name="project",
    )(source, ea, eb, rows)


def backproject_kernel(weight_ref, ea_ref, eb_ref, out_ref, lhs_ref, rhs_ref):
    @pl.when(pl.program_id(0) == 0)
    def _():
        wr = weight_ref[0]
        wi = weight_ref[1]
        for rows, cols, value in (
            (0, 0, wr), (0, 1024, wi), (128, 0, wi), (128, 1024, -wr),
        ):
            high, low = split(value)
            lhs_ref[0, rows : rows + 128, cols : cols + 1024] = high
            lhs_ref[1, rows : rows + 128, cols : cols + 1024] = low

    br = eb_ref[0]
    bi = eb_ref[1]
    for a in range(8):
        ar = ea_ref[0, a : a + 1, :]
        ai = ea_ref[1, a : a + 1, :]
        for part, value in ((0, ar * br - ai * bi), (1, ar * bi + ai * br)):
            high, low = split(value)
            rhs_ref[0, a * 32 : a * 32 + 32, part * 1024 : part * 1024 + 1024] = high
            rhs_ref[1, a * 32 : a * 32 + 32, part * 1024 : part * 1024 + 1024] = low
    out = dot_nt(lhs_ref[0], rhs_ref[0]) + (
        dot_nt(lhs_ref[0], rhs_ref[1]) + dot_nt(lhs_ref[1], rhs_ref[0])
    )
    out_ref[0] = out[:128]
    out_ref[1] = out[128:]


def backproject(weights, ea, eb):
    whole = pl.BlockSpec((2, 128, 1024), lambda t: (0, 0, 0))
    return pl.pallas_call(
        backproject_kernel,
        grid=(4,),
        in_specs=[
            whole,
            pl.BlockSpec((2, 8, 1024), lambda t: (0, t, 0)),
            pl.BlockSpec((2, 32, 1024), lambda t: (0, 0, 0)),
        ],
        out_specs=pl.BlockSpec((2, 128, 256), lambda t: (0, 0, t)),
        out_shape=jax.ShapeDtypeStruct((2, 128, 1024), f32),
        scratch_shapes=[pltpu.VMEM((2, 256, 2048), bf16), pltpu.VMEM((2, 256, 2048), bf16)],
        compiler_params=params(),
        cost_estimate=cost(2 * 256 * 2048 * 1024 * 3, 4 << 20),
        name="backproject",
    )(weights, ea, eb)


def phase_pair(position, direction):
    phase = (wave_step * position)[:, None] * direction[None, :]
    return jnp.stack([jnp.cos(phase), -jnp.sin(phase)])


def sum_over(value, steps):
    def exchange(value, axis, size, strides):
        parts = [value] + [
            lax.ppermute(value, axis, [(j, j ^ stride) for j in range(size)]) for stride in strides
        ]
        while len(parts) > 1:
            parts = [parts[j] + parts[j + 1] for j in range(0, len(parts), 2)]
        return parts[0]

    for axis, size, strides in steps:
        value = exchange(value, axis, size, strides)
    return value


def local(sources, incident, contrast, green, angles, measured):
    wide = lax.axis_index("wide")
    narrow = lax.axis_index("narrow")
    place = jnp.stack([narrow % 2, narrow // 2]).astype(jnp.int32)
    source = sources[0]

    def partner(value, k):
        return lax.ppermute(value, "narrow", [(j, j ^ k) for j in range(NARROW)])

    lines = columns_major(source)
    lines, green = lax.optimization_barrier((lines, green))
    far = partner(pack_green(green, place, 1), 2)
    lines = lax.all_to_all(lines.reshape(WIDE, 64, 128), "wide", 0, 0, tiled=True)

    row_position = (wide * 128 + jnp.arange(128, dtype=jnp.int32)).astype(f32) - N // 2 + 0.5
    block_position = (narrow * 1024 + 32 * jnp.arange(32, dtype=jnp.int32)).astype(f32) - N // 2 + 0.5
    cell_position = jnp.arange(32, dtype=jnp.int32).astype(f32)
    rows = phase_pair(row_position, jnp.cos(angles))
    sine = jnp.sin(angles)
    ea = phase_pair(block_position, sine)
    eb = phase_pair(cell_position, sine)
    partial_value = project(source, ea, eb, rows)
    lines, partial_value = lax.optimization_barrier((lines, partial_value))
    lines = x_forward(lines.reshape(2048, 128))
    lines, partial_value = lax.optimization_barrier((lines, partial_value))
    lines = lax.all_to_all(lines.reshape(128, 32, 128), ("wide", "narrow"), 0, 0, tiled=True)

    total = sum_over(partial_value, [("wide", WIDE, (1, 2, 3))])
    total, green = lax.optimization_barrier((total, green))
    near = pack_green(green, place, 0)
    near_partner = partner(near[1], 1)
    total = sum_over(total, [("wide", WIDE, (8, 16, 24))])
    total, far, near_partner = lax.optimization_barrier((total, far, near_partner))
    total = sum_over(total, [("narrow", NARROW, (1,))])
    greens = [near[0], near_partner, far, partner(second_of(far), 1)]
    total, lines = lax.optimization_barrier((total, lines))
    lines = middle(lines.reshape(4096, 128), greens, place)
    total, lines = lax.optimization_barrier((total, lines))
    lines = lax.all_to_all(lines.reshape(128, 32, 128), ("wide", "narrow"), 0, 0, tiled=True)
    total = sum_over(
        total, [(("wide", "narrow"), WIDE * NARROW, (2, 4 * NARROW, 4 * NARROW + 2))]
    )[:2]
    lines = x_inverse(lines.reshape(4096, 128))
    lines, contrast = lax.optimization_barrier((lines, contrast))
    known = jnp.stack(
        [
            contrast[0] * incident[0, 0] - contrast[1] * incident[0, 1] - source[0],
            contrast[0] * incident[0, 1] + contrast[1] * incident[0, 0] - source[1],
        ]
    )
    lines = lax.all_to_all(lines.reshape(WIDE, 64, 128), "wide", 0, 0, tiled=True)
    residual = residual_of(lines.reshape(2048, 128), contrast, known)

    data_residual = measured - total[None] * (1.0 / N)
    rho_real = data_residual[0, 0][None, :]
    rho_imag = data_residual[0, 1][None, :]
    scale = 1.0 / math.sqrt(R)
    weights = jnp.stack(
        [
            (rows[0] * rho_real + rows[1] * rho_imag) * scale,
            (rows[0] * rho_imag - rows[1] * rho_real) * scale,
        ]
    )
    back = backproject(weights, ea, eb)
    return (residual[None], back[None], data_residual)


def solution(mesh):
    placed = (
        P(None, None, "wide", "narrow"),
        P(None, None, "wide", "narrow"),
        P(None, "wide", "narrow"),
        P(None, "narrow", "wide"),
        P(),
        P(),
    )
    return jax.shard_map(
        local,
        mesh=mesh,
        in_specs=placed,
        out_specs=(P(None, None, "wide", "narrow"), P(None, None, "wide", "narrow"), P()),
        check_vma=False,
    )
```

```python
import functools
import math

import jax
import jax.numpy as jnp
import ml_dtypes
import numpy as np
from jax import lax
from jax.experimental import pallas as pl
from jax.experimental.pallas import tpu as pltpu
from jax.sharding import PartitionSpec as P

N = 4096
R = 1024
M = 8192
WIDE = 32
NARROW = 4

wave_step = 0.2 * math.pi
f32 = jnp.float32
bf16 = jnp.bfloat16


def complex_block(table):
    return np.block([[table.real, -table.imag], [table.imag, table.real]])


def terms(table):
    high = table.astype(np.float32).astype(ml_dtypes.bfloat16)
    low = (table - high.astype(np.float64)).astype(np.float32).astype(ml_dtypes.bfloat16)
    return np.concatenate([high, high, low], 1)


def root(product, length, sign):
    return np.exp(sign * 2j * np.pi * (product % length) / length)


def pair(table):
    return np.stack([table.real, table.imag]).astype(np.float32)


@functools.lru_cache(None)
def tables():
    out = {}
    w = np.arange(32)
    k1 = np.arange(64)
    i = np.arange(128)
    m = np.arange(128)
    out["t1"] = terms(complex_block(root(np.outer(k1, w), 64, -1)))
    out["tw1"] = pair(root(np.outer(k1, i), M, -1))
    out["t2"] = terms(complex_block(root(np.outer(m, i), 128, -1)))
    d = np.arange(128)
    s = 32 * (d % 4) + d // 4
    c1 = np.arange(256)
    out["t3"] = terms(complex_block(root(np.outer(c1, s), 256, -1)))
    low_half = np.arange(128) < 64
    first = np.where(low_half[None, :], 1.0, root(c1, M, -1)[:, None])
    out["tw3"] = pair(first)
    out["step3"] = pair(root(2 * c1, M, -1)[:, None] * np.ones((1, 128)))
    lanes = []
    for flip in (0, 1):
        first_e = (np.array([0, 1, 2, 3, 8, 9, 10, 11]) + 8 * flip) % 16
        e = np.where(low_half[None, :], first_e[:, None], first_e[:, None] + 4)
        lanes.append(pair(root(e, 32, -1)))
    out["lane3"] = np.stack(lanes)
    out["t4"] = terms(complex_block(root(np.outer(s, c1), 256, 1)))
    out["t5"] = terms(complex_block(root(np.outer(i, m), 128, 1)))
    lane_k1 = np.arange(128) % 64
    out["tw5"] = pair(root(np.outer(i, lane_k1), M, 1))
    inner = root(np.outer(w, k1), 64, 1) / (M * M)
    block = np.zeros((2, 2, 32, 2, 2, 64))
    for b0 in (0, 1):
        block[b0, 0, :, 0, b0, :] = inner.real
        block[b0, 0, :, 1, b0, :] = -inner.imag
        block[b0, 1, :, 0, b0, :] = inner.imag
        block[b0, 1, :, 1, b0, :] = inner.real
    out["t6"] = terms(block.reshape(128, 256))
    return out


def split(values):
    high = values.astype(bf16)
    low = (values - high.astype(f32)).astype(bf16)
    return high, low


def dot(a, b):
    return lax.dot_general(a, b, (((1,), (0,)), ((), ())), preferred_element_type=f32)


def dot_nt(a, b):
    return lax.dot_general(a, b, (((1,), (1,)), ((), ())), preferred_element_type=f32)


def dot3(table, values):
    high, low = split(values)
    return dot(table, jnp.concatenate([high, low, high], 0))


def dot3_nt(table, values):
    high, low = split(values)
    return dot_nt(table, jnp.concatenate([high, low, high], 1))


def times_root(value, numerator, length):
    re, im = value
    numerator %= length
    if numerator == 0:
        return value
    if 4 * numerator == length:
        return im, -re
    if 2 * numerator == length:
        return -re, -im
    if 4 * numerator == 3 * length:
        return -im, re
    if 8 * numerator == length:
        half = math.sqrt(0.5)
        return (re + im) * half, (im - re) * half
    if 8 * numerator == 3 * length:
        half = math.sqrt(0.5)
        return (im - re) * half, (-re - im) * half
    cosine = math.cos(2 * math.pi * numerator / length)
    sine = -math.sin(2 * math.pi * numerator / length)
    return re * cosine - im * sine, re * sine + im * cosine


def transform_list(values):
    count = len(values)
    if count == 1:
        return values
    if count == 2:
        (ar, ai), (br, bi) = values
        return [(ar + br, ai + bi), (ar - br, ai - bi)]
    if count == 4:
        (ar, ai), (br, bi), (cr, ci), (dr, di) = values
        pr, pi_, qr, qi = ar + cr, ai + ci, ar - cr, ai - ci
        sr, si, tr, ti = br + dr, bi + di, br - dr, bi - di
        return [(pr + sr, pi_ + si), (qr + ti, qi - tr), (pr - sr, pi_ - si), (qr - ti, qi + tr)]
    parts = [transform_list(values[start::4]) for start in range(4)]
    quarter = count // 4
    out = [None] * count
    for k in range(quarter):
        column = [times_root(parts[j][k], j * k, count) for j in range(4)]
        for q, value in enumerate(transform_list(column)):
            out[k + q * quarter] = value
    return out


def inverse_list(values):
    swapped = transform_list([(im, re) for re, im in values])
    return [(re, im) for im, re in swapped]


def spec_vmem():
    return pl.BlockSpec(memory_space=pltpu.VMEM)


def spec_hbm():
    return pl.BlockSpec(memory_space=pltpu.HBM)


def in_hbm(*values):
    return [pltpu.with_memory_space_constraint(jnp.asarray(value), pltpu.HBM) for value in values]


def fetch(sources, targets, arrived):
    copies = [
        pltpu.make_async_copy(source, target, arrived.at[k])
        for k, (source, target) in enumerate(zip(sources, targets))
    ]
    for copy in copies:
        copy.start()
    return copies


def params(mebibytes=16):
    return pltpu.CompilerParams(vmem_limit_bytes=mebibytes << 20)


def cost(flops, bytes_accessed):
    return pl.CostEstimate(flops=flops, bytes_accessed=bytes_accessed, transcendentals=0)


def columns_kernel(source_ref, out_ref):
    for tile in range(4):
        for part in range(2):
            turned = source_ref[part, :, 128 * tile : 128 * tile + 128].T
            for block in range(4):
                first = 256 * tile + block * 64 + part * 32
                out_ref[first : first + 32, :] = turned[block * 32 : block * 32 + 32]


def columns_major(source):
    return pl.pallas_call(
        columns_kernel,
        grid=(2,),
        in_specs=[pl.BlockSpec((2, 128, 512), lambda t: (0, 0, t))],
        out_specs=pl.BlockSpec((1024, 128), lambda t: (t, 0)),
        out_shape=pltpu.HBM((2048, 128), f32),
        cost_estimate=cost(0, 2 << 20),
        name="columns_major",
    )(source)


def x_forward_kernel(
    a_ref, t1_hbm, tw_hbm, t2_hbm, out_hbm, t1_ref, tw_ref, t2_ref, out_ref, arrived, sent
):
    for copy in fetch((t1_hbm, tw_hbm, t2_hbm), (t1_ref, tw_ref, t2_ref), arrived):
        copy.wait()

    @pl.loop(0, 16, unroll=8)
    def _(c):
        columns = []
        for b0 in range(2):
            re = a_ref[pl.ds(2 * c + b0, 32, stride=64), :]
            im = a_ref[pl.ds(2 * c + b0 + 32, 32, stride=64), :]
            columns.append(jnp.concatenate([re, im], 0))
        u = dot3(t1_ref[...], jnp.concatenate(columns, 1))
        rows = []
        for b0 in range(2):
            ur = u[:64, 128 * b0 : 128 * b0 + 128]
            ui = u[64:, 128 * b0 : 128 * b0 + 128]
            rows.append(
                jnp.concatenate(
                    [ur * tw_ref[0] - ui * tw_ref[1], ur * tw_ref[1] + ui * tw_ref[0]], 1
                )
            )
        z = jnp.concatenate(rows, 0)
        out = dot3_nt(t2_ref[...], z)
        out_ref[pl.ds(c, 128, stride=32), :] = out[:128]
        out_ref[pl.ds(c + 16, 128, stride=32), :] = out[128:]

    last = pltpu.make_async_copy(out_ref, out_hbm, sent)
    last.start()
    last.wait()


def x_forward(a):
    t = tables()
    return pl.pallas_call(
        x_forward_kernel,
        in_specs=[spec_vmem()] + [spec_hbm()] * 3,
        out_specs=spec_hbm(),
        out_shape=pltpu.HBM((4096, 128), f32),
        scratch_shapes=[
            pltpu.VMEM((128, 192), bf16),
            pltpu.VMEM((2, 64, 128), f32),
            pltpu.VMEM((256, 768), bf16),
            pltpu.VMEM((4096, 128), f32),
            pltpu.SemaphoreType.DMA((3,)),
            pltpu.SemaphoreType.DMA,
        ],
        compiler_params=params(8),
        cost_estimate=cost(2 * 2048 * 65536 * 4, 4 << 20),
        name="x_forward",
    )(a, *in_hbm(t["t1"], t["tw1"], t["t2"]))


def line_row(c):
    return c // 8 * 16 + c % 8


def middle_kernel(
    place_ref, a_ref, t3_hbm, tw_hbm, step_hbm, r0_hbm, r1_hbm, r2_hbm, r3_hbm, lane_hbm, t4_hbm,
    out_hbm, t3_ref, tw_ref, step_ref, green_ref, lane_ref, t4_ref, u_ref, now_ref, out_ref,
    arrived, sent,
):
    flip = place_ref[0]
    upper = place_ref[1]
    copies = fetch(
        (t3_hbm, tw_hbm, step_hbm, r0_hbm, r1_hbm, r2_hbm.at[0], r3_hbm, lane_hbm, t4_hbm),
        (t3_ref, tw_ref, step_ref)
        + tuple(green_ref.at[g, h] for h in (upper, 1 - upper) for g in range(2))
        + (lane_ref, t4_ref),
        arrived,
    )
    for copy in copies[:3]:
        copy.wait()
    sign = 1.0 - 2.0 * flip.astype(f32)
    step_ref[...] = step_ref[...] * sign
    now_ref[0] = tw_ref[...]

    for cc in range(8):
        columns = []
        for half in range(2):
            re = a_ref[pl.ds(2 * cc + half, 128, stride=32), :]
            im = a_ref[pl.ds(2 * cc + half + 16, 128, stride=32), :]
            columns.append(jnp.concatenate([re, im], 0))
        u = dot3(t3_ref[...], jnp.concatenate(columns, 1))
        for half in range(2):
            ur = u[:256, 128 * half : 128 * half + 128]
            ui = u[256:, 128 * half : 128 * half + 128]
            c = 2 * cc + half
            nr = now_ref[c, 0]
            ni = now_ref[c, 1]
            u_ref[c, 0, :256, :] = ur * nr - ui * ni
            u_ref[c, 1, :256, :] = ur * ni + ui * nr
            if c < 15:
                now_ref[c + 1, 0] = nr * step_ref[0] - ni * step_ref[1]
                now_ref[c + 1, 1] = nr * step_ref[1] + ni * step_ref[0]

    for copy in copies[3:]:
        copy.wait()

    lane = lax.broadcasted_iota(jnp.int32, (8, 128), 1)
    low = lane < 64

    def trade(first, second):
        middle_part = pltpu.roll(jnp.where(low, second, first), 64, 1)
        return jnp.where(low, first, middle_part), jnp.where(low, middle_part, second)

    @pl.loop(0, 32, unroll=4)
    def _(tile):
        rows = pl.ds(pl.multiple_of(tile * 8, 8), 8)
        values = [(u_ref[c, 0, rows, :], u_ref[c, 1, rows, :]) for c in range(16)]
        spectrum = transform_list(values)
        back = [None] * 16
        for index in range(8):
            g, r = index // 4, index % 4
            e = 8 * g + r
            grows = pl.ds(pl.multiple_of(tile * 8 + r * 256, 8), 8)
            lr = lane_ref[flip, 0, index : index + 1, :]
            li = lane_ref[flip, 1, index : index + 1, :]
            even_r, odd_r = trade(spectrum[e][0], spectrum[e + 4][0])
            even_i, odd_i = trade(spectrum[e][1], spectrum[e + 4][1])
            odd_r, odd_i = odd_r * lr - odd_i * li, odd_r * li + odd_i * lr
            products = []
            for h, (fr, fi) in enumerate(
                ((even_r + odd_r, even_i + odd_i), (even_r - odd_r, even_i - odd_i))
            ):
                gr = green_ref[g, h, 0, grows, :]
                gi = green_ref[g, h, 1, grows, :]
                products.append((gr * fr - gi * fi, gr * fi + gi * fr))
            (ar, ai), (br, bi) = products
            odd_r, odd_i = ar - br, ai - bi
            odd_r, odd_i = odd_r * lr + odd_i * li, odd_i * lr - odd_r * li
            first_r, second_r = trade(ar + br, odd_r)
            first_i, second_i = trade(ai + bi, odd_i)
            back[e] = (first_r, first_i)
            back[e + 4] = (second_r, second_i)
        for c, (re, im) in enumerate(inverse_list(back)):
            u_ref[c, 0, rows, :] = re
            u_ref[c, 1, rows, :] = im

    halves = []
    for cc in range(8):
        columns = []
        for half in range(2):
            ur = u_ref[2 * cc + half, 0, :256, :]
            ui = u_ref[2 * cc + half, 1, :256, :]
            nr = now_ref[2 * cc + half, 0]
            ni = now_ref[2 * cc + half, 1]
            columns.append(jnp.concatenate([ur * nr + ui * ni, ui * nr - ur * ni], 0))
        out = dot3(t4_ref[...], jnp.concatenate(columns, 1))
        for half in range(2):
            lanes = slice(128 * half, 128 * half + 128)
            row = line_row(2 * cc + half)
            out_ref[pl.ds(row, 128, stride=40), :] = out[:128, lanes]
            out_ref[pl.ds(row + 8, 128, stride=40), :] = out[128:, lanes]
        if cc % 4 == 3:
            rows = pl.ds(cc // 4 * 16, 16)
            halves.append(
                pltpu.make_async_copy(
                    out_ref.reshape(128, 40, 128).at[:, rows], out_hbm.at[:, rows], sent.at[cc // 4]
                )
            )
            halves[-1].start()
    for copy in halves:
        copy.wait()


def middle(a, greens, place):
    t = tables()
    return pl.pallas_call(
        middle_kernel,
        in_specs=[pl.BlockSpec(memory_space=pltpu.SMEM), spec_vmem()] + [spec_hbm()] * 9,
        out_specs=spec_hbm(),
        out_shape=pltpu.HBM((128, 32, 128), f32),
        scratch_shapes=[
            pltpu.VMEM((512, 768), bf16),
            pltpu.VMEM((2, 256, 128), f32),
            pltpu.VMEM((2, 256, 128), f32),
            pltpu.VMEM((2, 2, 2, 1024, 128), f32),
            pltpu.VMEM((2, 2, 8, 128), f32),
            pltpu.VMEM((256, 1536), bf16),
            pltpu.VMEM((16, 2, 264, 128), f32),
            pltpu.VMEM((16, 2, 256, 128), f32),
            pltpu.VMEM((5120, 128), f32),
            pltpu.SemaphoreType.DMA((9,)),
            pltpu.SemaphoreType.DMA((2,)),
        ],
        compiler_params=params(28),
        cost_estimate=cost(2 * 8 * 2 * 512 * 65536 * 3, 10 << 20),
        name="middle",
    )(
        place, a, *in_hbm(t["t3"], t["tw3"], t["step3"], *greens, t["lane3"], t["t4"])
    )


def x_inverse_kernel(
    a_ref, t5_hbm, tw_hbm, t6_hbm, out_hbm, t5_ref, tw_ref, t6_ref, out_ref, arrived, sent
):
    for copy in fetch((t5_hbm, tw_hbm, t6_hbm), (t5_ref, tw_ref, t6_ref), arrived):
        copy.wait()

    blocks = []
    for cc in range(8):
        columns = []
        for half in range(2):
            row = line_row(2 * cc + half)
            re = a_ref[pl.ds(row, 128, stride=32), :]
            im = a_ref[pl.ds(row + 8, 128, stride=32), :]
            columns.append(jnp.concatenate([re, im], 0))
        u = dot3(t5_ref[...], jnp.concatenate(columns, 1))
        rows = []
        for half in range(2):
            ur = u[:128, 128 * half : 128 * half + 128]
            ui = u[128:, 128 * half : 128 * half + 128]
            rows.append(
                jnp.concatenate(
                    [ur * tw_ref[0] - ui * tw_ref[1], ur * tw_ref[1] + ui * tw_ref[0]], 1
                )
            )
        out = dot3_nt(t6_ref[...], jnp.concatenate(rows, 0))
        for half in range(2):
            lanes = slice(128 * half, 128 * half + 128)
            for b0 in range(2):
                row = line_row(4 * cc + 2 * half + b0)
                out_ref[pl.ds(row, 32, stride=72), :] = out[64 * b0 : 64 * b0 + 32, lanes]
                out_ref[pl.ds(row + 8, 32, stride=72), :] = out[64 * b0 + 32 : 64 * b0 + 64, lanes]
        if cc % 2 == 1:
            rows = pl.ds(cc // 2 * 16, 16)
            blocks.append(
                pltpu.make_async_copy(
                    out_ref.reshape(32, 72, 128).at[:, rows], out_hbm.at[:, rows], sent.at[cc // 2]
                )
            )
            blocks[-1].start()
    for copy in blocks:
        copy.wait()


def x_inverse(a):
    t = tables()
    return pl.pallas_call(
        x_inverse_kernel,
        in_specs=[spec_vmem()] + [spec_hbm()] * 3,
        out_specs=spec_hbm(),
        out_shape=pltpu.HBM((32, 64, 128), f32),
        scratch_shapes=[
            pltpu.VMEM((256, 768), bf16),
            pltpu.VMEM((2, 128, 128), f32),
            pltpu.VMEM((128, 768), bf16),
            pltpu.VMEM((2304, 128), f32),
            pltpu.SemaphoreType.DMA((3,)),
            pltpu.SemaphoreType.DMA((4,)),
        ],
        compiler_params=params(8),
        cost_estimate=cost(2 * 2048 * 65536 * 4, 4 << 20),
        name="x_inverse",
    )(a, *in_hbm(t["t5"], t["tw5"], t["t6"]))


def residual_kernel(a_ref, contrast_ref, known_ref, out_ref):
    for tile in range(4):
        lanes = slice(128 * tile, 128 * tile + 128)
        scattered = []
        for part in range(2):
            rows = []
            for block in range(16):
                first = 256 * tile + block * 16 + part * 8
                rows.append(a_ref[first : first + 8, :])
            scattered.append(jnp.concatenate(rows, 0).T)
        cr = contrast_ref[0, :, lanes]
        ci = contrast_ref[1, :, lanes]
        out_ref[0, :, lanes] = cr * scattered[0] - ci * scattered[1] + known_ref[0, :, lanes]
        out_ref[1, :, lanes] = cr * scattered[1] + ci * scattered[0] + known_ref[1, :, lanes]


def residual_of(a, contrast, known):
    tile = pl.BlockSpec((2, 128, 512), lambda t: (0, 0, t))
    return pl.pallas_call(
        residual_kernel,
        grid=(2,),
        in_specs=[pl.BlockSpec((1024, 128), lambda t: (t, 0)), tile, tile],
        out_specs=tile,
        out_shape=jax.ShapeDtypeStruct((2, 128, 1024), f32),
        compiler_params=params(),
        cost_estimate=cost(0, 4 << 20),
        name="residual",
    )(a, contrast, known)


def pack_kernel(across, place_ref, green_ref, *out_refs):
    flip = place_ref[0]
    lane = lax.broadcasted_iota(jnp.int32, (512, 128), 1)
    low = lane < 64
    pick = low == (flip == 0)
    for part in range(2):
        first = green_ref[part, 0]
        second = green_ref[part, 1]
        straight = jnp.where(low, first, second)
        crossed = pltpu.roll(jnp.where(low, second, first), 64, 1)
        for core, value in enumerate(
            (jnp.where(pick, straight, crossed), jnp.where(pick, crossed, straight))
        ):
            if across:
                out_refs[0][core, part] = value
            else:
                out_refs[core][part] = value


def pack_green(green, place, across):
    if across:
        out_specs = pl.BlockSpec((2, 2, 512, 128), lambda t, place_ref: (0, 0, t, 0))
        out_shape = pltpu.HBM((2, 2, 1024, 128), f32)
    else:
        out_specs = [pl.BlockSpec((2, 512, 128), lambda t, place_ref: (0, t, 0))] * 2
        out_shape = [pltpu.HBM((2, 1024, 128), f32)] * 2

    def column(t, place_ref):
        return 0, 0, t, jnp.where(place_ref[1] == 1, 1 - across, across)

    return pl.pallas_call(
        functools.partial(pack_kernel, across),
        grid_spec=pltpu.PrefetchScalarGridSpec(
            num_scalar_prefetch=1,
            grid=(2,),
            in_specs=[pl.BlockSpec((2, 2, 512, 128), column)],
            out_specs=out_specs,
        ),
        out_shape=out_shape,
        compiler_params=params(),
        cost_estimate=cost(0, 4 << 20),
        name="pack_far" if across else "pack_near",
    )(place, *in_hbm(green.reshape(2, 2, 1024, 256)))


def second_kernel(in_ref, out_ref):
    out_ref[...] = in_ref[0]


def second_of(values):
    return pl.pallas_call(
        second_kernel,
        grid=(2,),
        in_specs=[pl.BlockSpec((1, 1, 1024, 128), lambda t: (1, t, 0, 0))],
        out_specs=pl.BlockSpec((1, 1024, 128), lambda t: (t, 0, 0)),
        out_shape=pltpu.HBM(values.shape[1:], f32),
        compiler_params=params(8),
        cost_estimate=cost(0, 2 << 20),
        name="second",
    )(*in_hbm(values))


def project_kernel(source_ref, ea_ref, eb_ref, row_ref, out_ref, lhs_ref, rhs_ref):
    @pl.when(pl.program_id(0) == 0)
    def _():
        re = source_ref[0]
        im = source_ref[1]
        for rows, cols, value in (
            (0, 0, re), (0, 1024, -im), (128, 0, im), (128, 1024, re),
        ):
            high, low = split(value)
            lhs_ref[0, rows : rows + 128, cols : cols + 1024] = high
            lhs_ref[1, rows : rows + 128, cols : cols + 1024] = low

    br = eb_ref[0]
    bi = eb_ref[1]
    for a in range(32):
        ar = ea_ref[0, a : a + 1, :]
        ai = ea_ref[1, a : a + 1, :]
        for part, value in ((0, ar * br - ai * bi), (1, ar * bi + ai * br)):
            high, low = split(value)
            rhs_ref[0, part * 1024 + a * 32 : part * 1024 + a * 32 + 32, :] = high
            rhs_ref[1, part * 1024 + a * 32 : part * 1024 + a * 32 + 32, :] = low
    inner = dot(lhs_ref[0], rhs_ref[0]) + (dot(lhs_ref[0], rhs_ref[1]) + dot(lhs_ref[1], rhs_ref[0]))
    ir = inner[:128]
    ii = inner[128:]
    fr = row_ref[0]
    fi = row_ref[1]
    pr = jnp.sum(fr * ir - fi * ii, axis=0, keepdims=True)
    pi_ = jnp.sum(fr * ii + fi * ir, axis=0, keepdims=True)
    out_ref[...] = jnp.concatenate([pr, pi_, jnp.zeros((6, pr.shape[1]), f32)], 0)


def project(source, ea, eb, rows):
    tile = 256
    whole = pl.BlockSpec((2, 128, 1024), lambda t: (0, 0, 0))
    return pl.pallas_call(
        project_kernel,
        grid=(R // tile,),
        in_specs=[
            whole,
            pl.BlockSpec((2, 32, tile), lambda t: (0, 0, t)),
            pl.BlockSpec((2, 32, tile), lambda t: (0, 0, t)),
            pl.BlockSpec((2, 128, tile), lambda t: (0, 0, t)),
        ],
        out_specs=pl.BlockSpec((8, tile), lambda t: (0, t)),
        out_shape=jax.ShapeDtypeStruct((8, R), f32),
        scratch_shapes=[pltpu.VMEM((2, 256, 2048), bf16), pltpu.VMEM((2, 2048, tile), bf16)],
        compiler_params=params(),
        cost_estimate=cost(2 * 256 * 2048 * 1024 * 3, 4 << 20),
        name="project",
    )(source, ea, eb, rows)


def backproject_kernel(weight_ref, ea_ref, eb_ref, out_ref, lhs_ref, rhs_ref):
    @pl.when(pl.program_id(0) == 0)
    def _():
        wr = weight_ref[0]
        wi = weight_ref[1]
        for rows, cols, value in (
            (0, 0, wr), (0, 1024, wi), (128, 0, wi), (128, 1024, -wr),
        ):
            high, low = split(value)
            lhs_ref[0, rows : rows + 128, cols : cols + 1024] = high
            lhs_ref[1, rows : rows + 128, cols : cols + 1024] = low

    br = eb_ref[0]
    bi = eb_ref[1]
    for a in range(8):
        ar = ea_ref[0, a : a + 1, :]
        ai = ea_ref[1, a : a + 1, :]
        for part, value in ((0, ar * br - ai * bi), (1, ar * bi + ai * br)):
            high, low = split(value)
            rhs_ref[0, a * 32 : a * 32 + 32, part * 1024 : part * 1024 + 1024] = high
            rhs_ref[1, a * 32 : a * 32 + 32, part * 1024 : part * 1024 + 1024] = low
    out = dot_nt(lhs_ref[0], rhs_ref[0]) + (
        dot_nt(lhs_ref[0], rhs_ref[1]) + dot_nt(lhs_ref[1], rhs_ref[0])
    )
    out_ref[0] = out[:128]
    out_ref[1] = out[128:]


def backproject(weights, ea, eb):
    whole = pl.BlockSpec((2, 128, 1024), lambda t: (0, 0, 0))
    return pl.pallas_call(
        backproject_kernel,
        grid=(4,),
        in_specs=[
            whole,
            pl.BlockSpec((2, 8, 1024), lambda t: (0, t, 0)),
            pl.BlockSpec((2, 32, 1024), lambda t: (0, 0, 0)),
        ],
        out_specs=pl.BlockSpec((2, 128, 256), lambda t: (0, 0, t)),
        out_shape=jax.ShapeDtypeStruct((2, 128, 1024), f32),
        scratch_shapes=[pltpu.VMEM((2, 256, 2048), bf16), pltpu.VMEM((2, 256, 2048), bf16)],
        compiler_params=params(),
        cost_estimate=cost(2 * 256 * 2048 * 1024 * 3, 4 << 20),
        name="backproject",
    )(weights, ea, eb)


def phase_pair(position, direction):
    phase = (wave_step * position)[:, None] * direction[None, :]
    return jnp.stack([jnp.cos(phase), -jnp.sin(phase)])


def sum_over(value, steps):
    def exchange(value, axis, size, strides):
        parts = [value] + [
            lax.ppermute(value, axis, [(j, j ^ stride) for j in range(size)]) for stride in strides
        ]
        while len(parts) > 1:
            parts = [parts[j] + parts[j + 1] for j in range(0, len(parts), 2)]
        return parts[0]

    for axis, size, strides in steps:
        value = exchange(value, axis, size, strides)
    return value


def local(sources, incident, contrast, green, angles, measured):
    wide = lax.axis_index("wide")
    narrow = lax.axis_index("narrow")
    place = jnp.stack([narrow % 2, narrow // 2]).astype(jnp.int32)
    source = sources[0]

    def partner(value, k):
        return lax.ppermute(value, "narrow", [(j, j ^ k) for j in range(NARROW)])

    lines = columns_major(source)
    lines, green = lax.optimization_barrier((lines, green))
    far = partner(pack_green(green, place, 1), 2)
    lines = lax.all_to_all(lines.reshape(WIDE, 64, 128), "wide", 0, 0, tiled=True)

    row_position = (wide * 128 + jnp.arange(128, dtype=jnp.int32)).astype(f32) - N // 2 + 0.5
    block_position = (narrow * 1024 + 32 * jnp.arange(32, dtype=jnp.int32)).astype(f32) - N // 2 + 0.5
    cell_position = jnp.arange(32, dtype=jnp.int32).astype(f32)
    rows = phase_pair(row_position, jnp.cos(angles))
    sine = jnp.sin(angles)
    ea = phase_pair(block_position, sine)
    eb = phase_pair(cell_position, sine)
    partial_value = project(source, ea, eb, rows)
    lines, partial_value = lax.optimization_barrier((lines, partial_value))
    lines = x_forward(lines.reshape(2048, 128))
    lines, partial_value = lax.optimization_barrier((lines, partial_value))
    lines = lax.all_to_all(lines.reshape(128, 32, 128), ("wide", "narrow"), 0, 0, tiled=True)

    total = sum_over(partial_value, [("wide", WIDE, (1, 2, 3))])
    total, green = lax.optimization_barrier((total, green))
    near = pack_green(green, place, 0)
    near_partner = partner(near[1], 1)
    total = sum_over(total, [("wide", WIDE, (8, 16, 24))])
    total, far, near_partner = lax.optimization_barrier((total, far, near_partner))
    total = sum_over(total, [("narrow", NARROW, (1,))])
    greens = [near[0], near_partner, far, partner(second_of(far), 1)]
    total, lines = lax.optimization_barrier((total, lines))
    lines = middle(lines.reshape(4096, 128), greens, place)
    total, lines = lax.optimization_barrier((total, lines))
    lines = lax.all_to_all(lines.reshape(128, 32, 128), ("wide", "narrow"), 0, 0, tiled=True)
    total = sum_over(
        total, [(("wide", "narrow"), WIDE * NARROW, (2, 4 * NARROW, 4 * NARROW + 2))]
    )[:2]
    lines = x_inverse(lines.reshape(4096, 128))
    lines, contrast = lax.optimization_barrier((lines, contrast))
    known = jnp.stack(
        [
            contrast[0] * incident[0, 0] - contrast[1] * incident[0, 1] - source[0],
            contrast[0] * incident[0, 1] + contrast[1] * incident[0, 0] - source[1],
        ]
    )
    lines = lax.all_to_all(lines.reshape(WIDE, 64, 128), "wide", 0, 0, tiled=True)
    residual = residual_of(lines.reshape(2048, 128), contrast, known)

    data_residual = measured - total[None] * (1.0 / N)
    rho_real = data_residual[0, 0][None, :]
    rho_imag = data_residual[0, 1][None, :]
    scale = 1.0 / math.sqrt(R)
    weights = jnp.stack(
        [
            (rows[0] * rho_real + rows[1] * rho_imag) * scale,
            (rows[0] * rho_imag - rows[1] * rho_real) * scale,
        ]
    )
    back = backproject(weights, ea, eb)
    return (residual[None], back[None], data_residual)


def solution(mesh):
    placed = (
        P(None, None, "wide", "narrow"),
        P(None, None, "wide", "narrow"),
        P(None, "wide", "narrow"),
        P(None, "narrow", "wide"),
        P(),
        P(),
    )
    return jax.shard_map(
        local,
        mesh=mesh,
        in_specs=placed,
        out_specs=(P(None, None, "wide", "narrow"), P(None, None, "wide", "narrow"), P()),
        check_vma=False,
    )
```

```python
import functools
import math

import jax
import jax.numpy as jnp
import ml_dtypes
import numpy as np
from jax import lax
from jax.experimental import pallas as pl
from jax.experimental.pallas import tpu as pltpu
from jax.sharding import PartitionSpec as P

N = 4096
R = 1024
M = 8192
WIDE = 32
NARROW = 4

wave_step = 0.2 * math.pi
f32 = jnp.float32
bf16 = jnp.bfloat16


def complex_block(table):
    return np.block([[table.real, -table.imag], [table.imag, table.real]])


def terms(table):
    high = table.astype(np.float32).astype(ml_dtypes.bfloat16)
    low = (table - high.astype(np.float64)).astype(np.float32).astype(ml_dtypes.bfloat16)
    return np.concatenate([high, high, low], 1)


def root(product, length, sign):
    return np.exp(sign * 2j * np.pi * (product % length) / length)


def pair(table):
    return np.stack([table.real, table.imag]).astype(np.float32)


@functools.lru_cache(None)
def tables():
    out = {}
    w = np.arange(32)
    k1 = np.arange(64)
    i = np.arange(128)
    m = np.arange(128)
    out["t1"] = terms(complex_block(root(np.outer(k1, w), 64, -1)))
    out["tw1"] = pair(root(np.outer(k1, i), M, -1))
    out["t2"] = terms(complex_block(root(np.outer(m, i), 128, -1)))
    d = np.arange(128)
    s = 32 * (d % 4) + d // 4
    c1 = np.arange(256)
    out["t3"] = terms(complex_block(root(np.outer(c1, s), 256, -1)))
    low_half = np.arange(128) < 64
    first = np.where(low_half[None, :], 1.0, root(c1, M, -1)[:, None])
    out["tw3"] = pair(first)
    out["step3"] = pair(root(2 * c1, M, -1)[:, None] * np.ones((1, 128)))
    lanes = []
    for flip in (0, 1):
        first_e = (np.array([0, 1, 2, 3, 8, 9, 10, 11]) + 8 * flip) % 16
        e = np.where(low_half[None, :], first_e[:, None], first_e[:, None] + 4)
        lanes.append(pair(root(e, 32, -1)))
    out["lane3"] = np.stack(lanes)
    out["t4"] = terms(complex_block(root(np.outer(s, c1), 256, 1)))
    out["t5"] = terms(complex_block(root(np.outer(i, m), 128, 1)))
    lane_k1 = np.arange(128) % 64
    out["tw5"] = pair(root(np.outer(i, lane_k1), M, 1))
    inner = root(np.outer(w, k1), 64, 1) / (M * M)
    block = np.zeros((2, 2, 32, 2, 2, 64))
    for b0 in (0, 1):
        block[b0, 0, :, 0, b0, :] = inner.real
        block[b0, 0, :, 1, b0, :] = -inner.imag
        block[b0, 1, :, 0, b0, :] = inner.imag
        block[b0, 1, :, 1, b0, :] = inner.real
    out["t6"] = terms(block.reshape(128, 256))
    return out


def split(values):
    high = values.astype(bf16)
    low = (values - high.astype(f32)).astype(bf16)
    return high, low


def dot(a, b):
    return lax.dot_general(a, b, (((1,), (0,)), ((), ())), preferred_element_type=f32)


def dot_nt(a, b):
    return lax.dot_general(a, b, (((1,), (1,)), ((), ())), preferred_element_type=f32)


def dot3(table, values):
    high, low = split(values)
    return dot(table, jnp.concatenate([high, low, high], 0))


def dot3_nt(table, values):
    high, low = split(values)
    return dot_nt(table, jnp.concatenate([high, low, high], 1))


def times_root(value, numerator, length):
    re, im = value
    numerator %= length
    if numerator == 0:
        return value
    if 4 * numerator == length:
        return im, -re
    if 2 * numerator == length:
        return -re, -im
    if 4 * numerator == 3 * length:
        return -im, re
    if 8 * numerator == length:
        half = math.sqrt(0.5)
        return (re + im) * half, (im - re) * half
    if 8 * numerator == 3 * length:
        half = math.sqrt(0.5)
        return (im - re) * half, (-re - im) * half
    cosine = math.cos(2 * math.pi * numerator / length)
    sine = -math.sin(2 * math.pi * numerator / length)
    return re * cosine - im * sine, re * sine + im * cosine


def transform_list(values):
    count = len(values)
    if count == 1:
        return values
    if count == 2:
        (ar, ai), (br, bi) = values
        return [(ar + br, ai + bi), (ar - br, ai - bi)]
    if count == 4:
        (ar, ai), (br, bi), (cr, ci), (dr, di) = values
        pr, pi_, qr, qi = ar + cr, ai + ci, ar - cr, ai - ci
        sr, si, tr, ti = br + dr, bi + di, br - dr, bi - di
        return [(pr + sr, pi_ + si), (qr + ti, qi - tr), (pr - sr, pi_ - si), (qr - ti, qi + tr)]
    parts = [transform_list(values[start::4]) for start in range(4)]
    quarter = count // 4
    out = [None] * count
    for k in range(quarter):
        column = [times_root(parts[j][k], j * k, count) for j in range(4)]
        for q, value in enumerate(transform_list(column)):
            out[k + q * quarter] = value
    return out


def inverse_list(values):
    swapped = transform_list([(im, re) for re, im in values])
    return [(re, im) for im, re in swapped]


def spec_vmem():
    return pl.BlockSpec(memory_space=pltpu.VMEM)


def spec_hbm():
    return pl.BlockSpec(memory_space=pltpu.HBM)


def in_hbm(*values):
    return [pltpu.with_memory_space_constraint(jnp.asarray(value), pltpu.HBM) for value in values]


def fetch(sources, targets, arrived):
    copies = [
        pltpu.make_async_copy(source, target, arrived.at[k])
        for k, (source, target) in enumerate(zip(sources, targets))
    ]
    for copy in copies:
        copy.start()
    return copies


def params(mebibytes=16):
    return pltpu.CompilerParams(vmem_limit_bytes=mebibytes << 20)


def cost(flops, bytes_accessed):
    return pl.CostEstimate(flops=flops, bytes_accessed=bytes_accessed, transcendentals=0)


def columns_kernel(source_ref, out_ref):
    for tile in range(4):
        for part in range(2):
            turned = source_ref[part, :, 128 * tile : 128 * tile + 128].T
            for block in range(4):
                first = 256 * tile + block * 64 + part * 32
                out_ref[first : first + 32, :] = turned[block * 32 : block * 32 + 32]


def columns_major(source):
    return pl.pallas_call(
        columns_kernel,
        grid=(2,),
        in_specs=[pl.BlockSpec((2, 128, 512), lambda t: (0, 0, t))],
        out_specs=pl.BlockSpec((1024, 128), lambda t: (t, 0)),
        out_shape=pltpu.HBM((2048, 128), f32),
        cost_estimate=cost(0, 2 << 20),
        name="columns_major",
    )(source)


def x_forward_kernel(
    a_ref, t1_hbm, tw_hbm, t2_hbm, out_hbm, t1_ref, tw_ref, t2_ref, out_ref, arrived, sent
):
    for copy in fetch((t1_hbm, tw_hbm, t2_hbm), (t1_ref, tw_ref, t2_ref), arrived):
        copy.wait()

    @pl.loop(0, 16, unroll=8)
    def _(c):
        columns = []
        for b0 in range(2):
            re = a_ref[pl.ds(2 * c + b0, 32, stride=64), :]
            im = a_ref[pl.ds(2 * c + b0 + 32, 32, stride=64), :]
            columns.append(jnp.concatenate([re, im], 0))
        u = dot3(t1_ref[...], jnp.concatenate(columns, 1))
        rows = []
        for b0 in range(2):
            ur = u[:64, 128 * b0 : 128 * b0 + 128]
            ui = u[64:, 128 * b0 : 128 * b0 + 128]
            rows.append(
                jnp.concatenate(
                    [ur * tw_ref[0] - ui * tw_ref[1], ur * tw_ref[1] + ui * tw_ref[0]], 1
                )
            )
        z = jnp.concatenate(rows, 0)
        out = dot3_nt(t2_ref[...], z)
        out_ref[pl.ds(c, 128, stride=32), :] = out[:128]
        out_ref[pl.ds(c + 16, 128, stride=32), :] = out[128:]

    last = pltpu.make_async_copy(out_ref, out_hbm, sent)
    last.start()
    last.wait()


def x_forward(a):
    t = tables()
    return pl.pallas_call(
        x_forward_kernel,
        in_specs=[spec_vmem()] + [spec_hbm()] * 3,
        out_specs=spec_hbm(),
        out_shape=pltpu.HBM((4096, 128), f32),
        scratch_shapes=[
            pltpu.VMEM((128, 192), bf16),
            pltpu.VMEM((2, 64, 128), f32),
            pltpu.VMEM((256, 768), bf16),
            pltpu.VMEM((4096, 128), f32),
            pltpu.SemaphoreType.DMA((3,)),
            pltpu.SemaphoreType.DMA,
        ],
        compiler_params=params(8),
        cost_estimate=cost(2 * 2048 * 65536 * 4, 4 << 20),
        name="x_forward",
    )(a, *in_hbm(t["t1"], t["tw1"], t["t2"]))


def line_row(c):
    return c // 8 * 16 + c % 8


def middle_kernel(
    place_ref, a_ref, t3_hbm, tw_hbm, step_hbm, r0_hbm, r1_hbm, r2_hbm, r3_hbm, lane_hbm, t4_hbm,
    out_hbm, t3_ref, tw_ref, step_ref, green_ref, lane_ref, t4_ref, u_ref, now_ref, out_ref,
    spread_ref, arrived, sent, moved,
):
    flip = place_ref[0]
    upper = place_ref[1]
    spread = pltpu.make_async_copy(
        a_ref.reshape(128, 32, 128), spread_ref.reshape(128, 40, 128).at[:, pl.ds(0, 32)], moved
    )
    spread.start()
    copies = fetch(
        (t3_hbm, tw_hbm, step_hbm, r0_hbm, r1_hbm, r2_hbm.at[0], r3_hbm, lane_hbm, t4_hbm),
        (t3_ref, tw_ref, step_ref)
        + tuple(green_ref.at[g, h] for h in (upper, 1 - upper) for g in range(2))
        + (lane_ref, t4_ref),
        arrived,
    )
    for copy in copies[:3]:
        copy.wait()
    spread.wait()
    sign = 1.0 - 2.0 * flip.astype(f32)
    step_ref[...] = step_ref[...] * sign
    now_ref[0] = tw_ref[...]

    for cc in range(8):
        columns = []
        for half in range(2):
            re = spread_ref[pl.ds(2 * cc + half, 128, stride=40), :]
            im = spread_ref[pl.ds(2 * cc + half + 16, 128, stride=40), :]
            columns.append(jnp.concatenate([re, im], 0))
        u = dot3(t3_ref[...], jnp.concatenate(columns, 1))
        for half in range(2):
            ur = u[:256, 128 * half : 128 * half + 128]
            ui = u[256:, 128 * half : 128 * half + 128]
            c = 2 * cc + half
            nr = now_ref[c, 0]
            ni = now_ref[c, 1]
            u_ref[c, 0, :256, :] = ur * nr - ui * ni
            u_ref[c, 1, :256, :] = ur * ni + ui * nr
            if c < 15:
                now_ref[c + 1, 0] = nr * step_ref[0] - ni * step_ref[1]
                now_ref[c + 1, 1] = nr * step_ref[1] + ni * step_ref[0]

    for copy in copies[3:]:
        copy.wait()

    lane = lax.broadcasted_iota(jnp.int32, (8, 128), 1)
    low = lane < 64

    def trade(first, second):
        middle_part = pltpu.roll(jnp.where(low, second, first), 64, 1)
        return jnp.where(low, first, middle_part), jnp.where(low, middle_part, second)

    @pl.loop(0, 32, unroll=4)
    def _(tile):
        rows = pl.ds(pl.multiple_of(tile * 8, 8), 8)
        values = [(u_ref[c, 0, rows, :], u_ref[c, 1, rows, :]) for c in range(16)]
        spectrum = transform_list(values)
        back = [None] * 16
        for index in range(8):
            g, r = index // 4, index % 4
            e = 8 * g + r
            grows = pl.ds(pl.multiple_of(tile * 8 + r * 256, 8), 8)
            lr = lane_ref[flip, 0, index : index + 1, :]
            li = lane_ref[flip, 1, index : index + 1, :]
            even_r, odd_r = trade(spectrum[e][0], spectrum[e + 4][0])
            even_i, odd_i = trade(spectrum[e][1], spectrum[e + 4][1])
            odd_r, odd_i = odd_r * lr - odd_i * li, odd_r * li + odd_i * lr
            products = []
            for h, (fr, fi) in enumerate(
                ((even_r + odd_r, even_i + odd_i), (even_r - odd_r, even_i - odd_i))
            ):
                gr = green_ref[g, h, 0, grows, :]
                gi = green_ref[g, h, 1, grows, :]
                products.append((gr * fr - gi * fi, gr * fi + gi * fr))
            (ar, ai), (br, bi) = products
            odd_r, odd_i = ar - br, ai - bi
            odd_r, odd_i = odd_r * lr + odd_i * li, odd_i * lr - odd_r * li
            first_r, second_r = trade(ar + br, odd_r)
            first_i, second_i = trade(ai + bi, odd_i)
            back[e] = (first_r, first_i)
            back[e + 4] = (second_r, second_i)
        for c, (re, im) in enumerate(inverse_list(back)):
            u_ref[c, 0, rows, :] = re
            u_ref[c, 1, rows, :] = im

    halves = []
    for cc in range(8):
        columns = []
        for half in range(2):
            ur = u_ref[2 * cc + half, 0, :256, :]
            ui = u_ref[2 * cc + half, 1, :256, :]
            nr = now_ref[2 * cc + half, 0]
            ni = now_ref[2 * cc + half, 1]
            columns.append(jnp.concatenate([ur * nr + ui * ni, ui * nr - ur * ni], 0))
        out = dot3(t4_ref[...], jnp.concatenate(columns, 1))
        for half in range(2):
            lanes = slice(128 * half, 128 * half + 128)
            row = line_row(2 * cc + half)
            out_ref[pl.ds(row, 128, stride=40), :] = out[:128, lanes]
            out_ref[pl.ds(row + 8, 128, stride=40), :] = out[128:, lanes]
        if cc % 4 == 3:
            rows = pl.ds(cc // 4 * 16, 16)
            halves.append(
                pltpu.make_async_copy(
                    out_ref.reshape(128, 40, 128).at[:, rows], out_hbm.at[:, rows], sent.at[cc // 4]
                )
            )
            halves[-1].start()
    for copy in halves:
        copy.wait()


def middle(a, greens, place):
    t = tables()
    return pl.pallas_call(
        middle_kernel,
        in_specs=[pl.BlockSpec(memory_space=pltpu.SMEM), spec_vmem()] + [spec_hbm()] * 9,
        out_specs=spec_hbm(),
        out_shape=pltpu.HBM((128, 32, 128), f32),
        scratch_shapes=[
            pltpu.VMEM((512, 768), bf16),
            pltpu.VMEM((2, 256, 128), f32),
            pltpu.VMEM((2, 256, 128), f32),
            pltpu.VMEM((2, 2, 2, 1024, 128), f32),
            pltpu.VMEM((2, 2, 8, 128), f32),
            pltpu.VMEM((256, 1536), bf16),
            pltpu.VMEM((16, 2, 264, 128), f32),
            pltpu.VMEM((16, 2, 256, 128), f32),
            pltpu.VMEM((5120, 128), f32),
            pltpu.VMEM((5120, 128), f32),
            pltpu.SemaphoreType.DMA((9,)),
            pltpu.SemaphoreType.DMA((2,)),
            pltpu.SemaphoreType.DMA,
        ],
        compiler_params=params(32),
        cost_estimate=cost(2 * 8 * 2 * 512 * 65536 * 3, 10 << 20),
        name="middle",
    )(
        place, a, *in_hbm(t["t3"], t["tw3"], t["step3"], *greens, t["lane3"], t["t4"])
    )


def x_inverse_kernel(
    a_ref, t5_hbm, tw_hbm, t6_hbm, out_hbm, t5_ref, tw_ref, t6_ref, spread_ref, out_ref, arrived,
    sent, moved,
):
    spread = pltpu.make_async_copy(
        a_ref.reshape(128, 32, 128), spread_ref.reshape(128, 40, 128).at[:, pl.ds(0, 32)], moved
    )
    spread.start()
    for copy in fetch((t5_hbm, tw_hbm, t6_hbm), (t5_ref, tw_ref, t6_ref), arrived):
        copy.wait()
    spread.wait()

    blocks = []
    for cc in range(8):
        columns = []
        for half in range(2):
            row = line_row(2 * cc + half)
            re = spread_ref[pl.ds(row, 128, stride=40), :]
            im = spread_ref[pl.ds(row + 8, 128, stride=40), :]
            columns.append(jnp.concatenate([re, im], 0))
        u = dot3(t5_ref[...], jnp.concatenate(columns, 1))
        rows = []
        for half in range(2):
            ur = u[:128, 128 * half : 128 * half + 128]
            ui = u[128:, 128 * half : 128 * half + 128]
            rows.append(
                jnp.concatenate(
                    [ur * tw_ref[0] - ui * tw_ref[1], ur * tw_ref[1] + ui * tw_ref[0]], 1
                )
            )
        out = dot3_nt(t6_ref[...], jnp.concatenate(rows, 0))
        for half in range(2):
            lanes = slice(128 * half, 128 * half + 128)
            for b0 in range(2):
                row = line_row(4 * cc + 2 * half + b0)
                out_ref[pl.ds(row, 32, stride=72), :] = out[64 * b0 : 64 * b0 + 32, lanes]
                out_ref[pl.ds(row + 8, 32, stride=72), :] = out[64 * b0 + 32 : 64 * b0 + 64, lanes]
        if cc % 2 == 1:
            rows = pl.ds(cc // 2 * 16, 16)
            blocks.append(
                pltpu.make_async_copy(
                    out_ref.reshape(32, 72, 128).at[:, rows], out_hbm.at[:, rows], sent.at[cc // 2]
                )
            )
            blocks[-1].start()
    for copy in blocks:
        copy.wait()


def x_inverse(a):
    t = tables()
    return pl.pallas_call(
        x_inverse_kernel,
        in_specs=[spec_vmem()] + [spec_hbm()] * 3,
        out_specs=spec_hbm(),
        out_shape=pltpu.HBM((32, 64, 128), f32),
        scratch_shapes=[
            pltpu.VMEM((256, 768), bf16),
            pltpu.VMEM((2, 128, 128), f32),
            pltpu.VMEM((128, 768), bf16),
            pltpu.VMEM((5120, 128), f32),
            pltpu.VMEM((2304, 128), f32),
            pltpu.SemaphoreType.DMA((3,)),
            pltpu.SemaphoreType.DMA((4,)),
            pltpu.SemaphoreType.DMA,
        ],
        compiler_params=params(12),
        cost_estimate=cost(2 * 2048 * 65536 * 4, 4 << 20),
        name="x_inverse",
    )(a, *in_hbm(t["t5"], t["tw5"], t["t6"]))


def residual_kernel(a_ref, contrast_ref, known_ref, out_ref):
    for tile in range(4):
        lanes = slice(128 * tile, 128 * tile + 128)
        scattered = []
        for part in range(2):
            rows = []
            for block in range(16):
                first = 256 * tile + block * 16 + part * 8
                rows.append(a_ref[first : first + 8, :])
            scattered.append(jnp.concatenate(rows, 0).T)
        cr = contrast_ref[0, :, lanes]
        ci = contrast_ref[1, :, lanes]
        out_ref[0, :, lanes] = cr * scattered[0] - ci * scattered[1] + known_ref[0, :, lanes]
        out_ref[1, :, lanes] = cr * scattered[1] + ci * scattered[0] + known_ref[1, :, lanes]


def residual_of(a, contrast, known):
    tile = pl.BlockSpec((2, 128, 512), lambda t: (0, 0, t))
    return pl.pallas_call(
        residual_kernel,
        grid=(2,),
        in_specs=[pl.BlockSpec((1024, 128), lambda t: (t, 0)), tile, tile],
        out_specs=tile,
        out_shape=jax.ShapeDtypeStruct((2, 128, 1024), f32),
        compiler_params=params(),
        cost_estimate=cost(0, 4 << 20),
        name="residual",
    )(a, contrast, known)


def pack_kernel(across, place_ref, green_ref, *out_refs):
    flip = place_ref[0]
    lane = lax.broadcasted_iota(jnp.int32, (512, 128), 1)
    low = lane < 64
    pick = low == (flip == 0)
    for part in range(2):
        first = green_ref[part, 0]
        second = green_ref[part, 1]
        straight = jnp.where(low, first, second)
        crossed = pltpu.roll(jnp.where(low, second, first), 64, 1)
        for core, value in enumerate(
            (jnp.where(pick, straight, crossed), jnp.where(pick, crossed, straight))
        ):
            if across:
                out_refs[0][core, part] = value
            else:
                out_refs[core][part] = value


def pack_green(green, place, across):
    if across:
        out_specs = pl.BlockSpec((2, 2, 512, 128), lambda t, place_ref: (0, 0, t, 0))
        out_shape = pltpu.HBM((2, 2, 1024, 128), f32)
    else:
        out_specs = [pl.BlockSpec((2, 512, 128), lambda t, place_ref: (0, t, 0))] * 2
        out_shape = [pltpu.HBM((2, 1024, 128), f32)] * 2

    def column(t, place_ref):
        return 0, 0, t, jnp.where(place_ref[1] == 1, 1 - across, across)

    return pl.pallas_call(
        functools.partial(pack_kernel, across),
        grid_spec=pltpu.PrefetchScalarGridSpec(
            num_scalar_prefetch=1,
            grid=(2,),
            in_specs=[pl.BlockSpec((2, 2, 512, 128), column)],
            out_specs=out_specs,
        ),
        out_shape=out_shape,
        compiler_params=params(),
        cost_estimate=cost(0, 4 << 20),
        name="pack_far" if across else "pack_near",
    )(place, *in_hbm(green.reshape(2, 2, 1024, 256)))


def second_kernel(in_ref, out_ref):
    out_ref[...] = in_ref[0]


def second_of(values):
    return pl.pallas_call(
        second_kernel,
        grid=(2,),
        in_specs=[pl.BlockSpec((1, 1, 1024, 128), lambda t: (1, t, 0, 0))],
        out_specs=pl.BlockSpec((1, 1024, 128), lambda t: (t, 0, 0)),
        out_shape=pltpu.HBM(values.shape[1:], f32),
        compiler_params=params(8),
        cost_estimate=cost(0, 2 << 20),
        name="second",
    )(*in_hbm(values))


def project_kernel(source_ref, ea_ref, eb_ref, row_ref, out_ref, lhs_ref, rhs_ref):
    @pl.when(pl.program_id(0) == 0)
    def _():
        re = source_ref[0]
        im = source_ref[1]
        for rows, cols, value in (
            (0, 0, re), (0, 1024, -im), (128, 0, im), (128, 1024, re),
        ):
            high, low = split(value)
            lhs_ref[0, rows : rows + 128, cols : cols + 1024] = high
            lhs_ref[1, rows : rows + 128, cols : cols + 1024] = low

    br = eb_ref[0]
    bi = eb_ref[1]
    for a in range(32):
        ar = ea_ref[0, a : a + 1, :]
        ai = ea_ref[1, a : a + 1, :]
        for part, value in ((0, ar * br - ai * bi), (1, ar * bi + ai * br)):
            high, low = split(value)
            rhs_ref[0, part * 1024 + a * 32 : part * 1024 + a * 32 + 32, :] = high
            rhs_ref[1, part * 1024 + a * 32 : part * 1024 + a * 32 + 32, :] = low
    inner = dot(lhs_ref[0], rhs_ref[0]) + (dot(lhs_ref[0], rhs_ref[1]) + dot(lhs_ref[1], rhs_ref[0]))
    ir = inner[:128]
    ii = inner[128:]
    fr = row_ref[0]
    fi = row_ref[1]
    pr = jnp.sum(fr * ir - fi * ii, axis=0, keepdims=True)
    pi_ = jnp.sum(fr * ii + fi * ir, axis=0, keepdims=True)
    out_ref[...] = jnp.concatenate([pr, pi_, jnp.zeros((6, pr.shape[1]), f32)], 0)


def project(source, ea, eb, rows):
    tile = 256
    whole = pl.BlockSpec((2, 128, 1024), lambda t: (0, 0, 0))
    return pl.pallas_call(
        project_kernel,
        grid=(R // tile,),
        in_specs=[
            whole,
            pl.BlockSpec((2, 32, tile), lambda t: (0, 0, t)),
            pl.BlockSpec((2, 32, tile), lambda t: (0, 0, t)),
            pl.BlockSpec((2, 128, tile), lambda t: (0, 0, t)),
        ],
        out_specs=pl.BlockSpec((8, tile), lambda t: (0, t)),
        out_shape=jax.ShapeDtypeStruct((8, R), f32),
        scratch_shapes=[pltpu.VMEM((2, 256, 2048), bf16), pltpu.VMEM((2, 2048, tile), bf16)],
        compiler_params=params(),
        cost_estimate=cost(2 * 256 * 2048 * 1024 * 3, 4 << 20),
        name="project",
    )(source, ea, eb, rows)


def backproject_kernel(weight_ref, ea_ref, eb_ref, out_ref, lhs_ref, rhs_ref):
    @pl.when(pl.program_id(0) == 0)
    def _():
        wr = weight_ref[0]
        wi = weight_ref[1]
        for rows, cols, value in (
            (0, 0, wr), (0, 1024, wi), (128, 0, wi), (128, 1024, -wr),
        ):
            high, low = split(value)
            lhs_ref[0, rows : rows + 128, cols : cols + 1024] = high
            lhs_ref[1, rows : rows + 128, cols : cols + 1024] = low

    br = eb_ref[0]
    bi = eb_ref[1]
    for a in range(8):
        ar = ea_ref[0, a : a + 1, :]
        ai = ea_ref[1, a : a + 1, :]
        for part, value in ((0, ar * br - ai * bi), (1, ar * bi + ai * br)):
            high, low = split(value)
            rhs_ref[0, a * 32 : a * 32 + 32, part * 1024 : part * 1024 + 1024] = high
            rhs_ref[1, a * 32 : a * 32 + 32, part * 1024 : part * 1024 + 1024] = low
    out = dot_nt(lhs_ref[0], rhs_ref[0]) + (
        dot_nt(lhs_ref[0], rhs_ref[1]) + dot_nt(lhs_ref[1], rhs_ref[0])
    )
    out_ref[0] = out[:128]
    out_ref[1] = out[128:]


def backproject(weights, ea, eb):
    whole = pl.BlockSpec((2, 128, 1024), lambda t: (0, 0, 0))
    return pl.pallas_call(
        backproject_kernel,
        grid=(4,),
        in_specs=[
            whole,
            pl.BlockSpec((2, 8, 1024), lambda t: (0, t, 0)),
            pl.BlockSpec((2, 32, 1024), lambda t: (0, 0, 0)),
        ],
        out_specs=pl.BlockSpec((2, 128, 256), lambda t: (0, 0, t)),
        out_shape=jax.ShapeDtypeStruct((2, 128, 1024), f32),
        scratch_shapes=[pltpu.VMEM((2, 256, 2048), bf16), pltpu.VMEM((2, 256, 2048), bf16)],
        compiler_params=params(),
        cost_estimate=cost(2 * 256 * 2048 * 1024 * 3, 4 << 20),
        name="backproject",
    )(weights, ea, eb)


def phase_pair(position, direction):
    phase = (wave_step * position)[:, None] * direction[None, :]
    return jnp.stack([jnp.cos(phase), -jnp.sin(phase)])


def sum_over(value, steps):
    def exchange(value, axis, size, strides):
        parts = [value] + [
            lax.ppermute(value, axis, [(j, j ^ stride) for j in range(size)]) for stride in strides
        ]
        while len(parts) > 1:
            parts = [parts[j] + parts[j + 1] for j in range(0, len(parts), 2)]
        return parts[0]

    for axis, size, strides in steps:
        value = exchange(value, axis, size, strides)
    return value


def local(sources, incident, contrast, green, angles, measured):
    wide = lax.axis_index("wide")
    narrow = lax.axis_index("narrow")
    place = jnp.stack([narrow % 2, narrow // 2]).astype(jnp.int32)
    source = sources[0]

    def partner(value, k):
        return lax.ppermute(value, "narrow", [(j, j ^ k) for j in range(NARROW)])

    lines = columns_major(source)
    lines, green = lax.optimization_barrier((lines, green))
    far = partner(pack_green(green, place, 1), 2)
    lines = lax.all_to_all(lines.reshape(WIDE, 64, 128), "wide", 0, 0, tiled=True)

    row_position = (wide * 128 + jnp.arange(128, dtype=jnp.int32)).astype(f32) - N // 2 + 0.5
    block_position = (narrow * 1024 + 32 * jnp.arange(32, dtype=jnp.int32)).astype(f32) - N // 2 + 0.5
    cell_position = jnp.arange(32, dtype=jnp.int32).astype(f32)
    rows = phase_pair(row_position, jnp.cos(angles))
    sine = jnp.sin(angles)
    ea = phase_pair(block_position, sine)
    eb = phase_pair(cell_position, sine)
    partial_value = project(source, ea, eb, rows)
    lines, partial_value = lax.optimization_barrier((lines, partial_value))
    lines = x_forward(lines.reshape(2048, 128))
    lines, partial_value = lax.optimization_barrier((lines, partial_value))
    lines = lax.all_to_all(lines.reshape(128, 32, 128), ("wide", "narrow"), 0, 0, tiled=True)

    total = sum_over(partial_value, [("wide", WIDE, (1, 2, 3)), ("wide", WIDE, (8, 16, 24))])
    total, green = lax.optimization_barrier((total, green))
    near = pack_green(green, place, 0)
    near_partner = partner(near[1], 1)
    total, far, near_partner = lax.optimization_barrier((total, far, near_partner))
    total = sum_over(total, [("narrow", NARROW, (1,))])
    greens = [near[0], near_partner, far, partner(second_of(far), 1)]
    total, lines = lax.optimization_barrier((total, lines))
    lines = middle(lines.reshape(4096, 128), greens, place)
    total, lines = lax.optimization_barrier((total, lines))
    lines = lax.all_to_all(lines.reshape(128, 32, 128), ("wide", "narrow"), 0, 0, tiled=True)
    total = sum_over(
        total, [(("wide", "narrow"), WIDE * NARROW, (2, 4 * NARROW, 4 * NARROW + 2))]
    )[:2]
    lines = x_inverse(lines.reshape(4096, 128))
    lines, contrast = lax.optimization_barrier((lines, contrast))
    known = jnp.stack(
        [
            contrast[0] * incident[0, 0] - contrast[1] * incident[0, 1] - source[0],
            contrast[0] * incident[0, 1] + contrast[1] * incident[0, 0] - source[1],
        ]
    )
    lines = lax.all_to_all(lines.reshape(WIDE, 64, 128), "wide", 0, 0, tiled=True)
    residual = residual_of(lines.reshape(2048, 128), contrast, known)

    data_residual = measured - total[None] * (1.0 / N)
    rho_real = data_residual[0, 0][None, :]
    rho_imag = data_residual[0, 1][None, :]
    scale = 1.0 / math.sqrt(R)
    weights = jnp.stack(
        [
            (rows[0] * rho_real + rows[1] * rho_imag) * scale,
            (rows[0] * rho_imag - rows[1] * rho_real) * scale,
        ]
    )
    back = backproject(weights, ea, eb)
    return (residual[None], back[None], data_residual)


def solution(mesh):
    placed = (
        P(None, None, "wide", "narrow"),
        P(None, None, "wide", "narrow"),
        P(None, "wide", "narrow"),
        P(None, "narrow", "wide"),
        P(),
        P(),
    )
    return jax.shard_map(
        local,
        mesh=mesh,
        in_specs=placed,
        out_specs=(P(None, None, "wide", "narrow"), P(None, None, "wide", "narrow"), P()),
        check_vma=False,
    )
```

```python
import functools
import math

import jax
import jax.numpy as jnp
import ml_dtypes
import numpy as np
from jax import lax
from jax.experimental import pallas as pl
from jax.experimental.pallas import tpu as pltpu
from jax.sharding import PartitionSpec as P

N = 4096
R = 1024
M = 8192
WIDE = 32
NARROW = 4

wave_step = 0.2 * math.pi
f32 = jnp.float32
bf16 = jnp.bfloat16


def complex_block(table):
    return np.block([[table.real, -table.imag], [table.imag, table.real]])


def terms(table):
    high = table.astype(np.float32).astype(ml_dtypes.bfloat16)
    low = (table - high.astype(np.float64)).astype(np.float32).astype(ml_dtypes.bfloat16)
    return np.concatenate([high, high, low], 1)


def root(product, length, sign):
    return np.exp(sign * 2j * np.pi * (product % length) / length)


def pair(table):
    return np.stack([table.real, table.imag]).astype(np.float32)


@functools.lru_cache(None)
def tables():
    out = {}
    w = np.arange(32)
    k1 = np.arange(64)
    i = np.arange(128)
    m = np.arange(128)
    out["t1"] = terms(complex_block(root(np.outer(k1, w), 64, -1)))
    out["tw1"] = pair(root(np.outer(k1, i), M, -1))
    out["t2"] = terms(complex_block(root(np.outer(m, i), 128, -1)))
    d = np.arange(128)
    s = 32 * (d % 4) + d // 4
    c1 = np.arange(256)
    out["t3"] = terms(complex_block(root(np.outer(c1, s), 256, -1)))
    low_half = np.arange(128) < 64
    first = np.where(low_half[None, :], 1.0, root(c1, M, -1)[:, None])
    out["tw3"] = pair(first)
    out["step3"] = pair(root(2 * c1, M, -1)[:, None] * np.ones((1, 128)))
    lanes = []
    for flip in (0, 1):
        first_e = (np.array([0, 1, 2, 3, 8, 9, 10, 11]) + 8 * flip) % 16
        e = np.where(low_half[None, :], first_e[:, None], first_e[:, None] + 4)
        lanes.append(pair(root(e, 32, -1)))
    out["lane3"] = np.stack(lanes)
    out["t4"] = terms(complex_block(root(np.outer(s, c1), 256, 1)))
    out["t5"] = terms(complex_block(root(np.outer(i, m), 128, 1)))
    lane_k1 = np.arange(128) % 64
    out["tw5"] = pair(root(np.outer(i, lane_k1), M, 1))
    inner = root(np.outer(w, k1), 64, 1) / (M * M)
    block = np.zeros((2, 2, 32, 2, 2, 64))
    for b0 in (0, 1):
        block[b0, 0, :, 0, b0, :] = inner.real
        block[b0, 0, :, 1, b0, :] = -inner.imag
        block[b0, 1, :, 0, b0, :] = inner.imag
        block[b0, 1, :, 1, b0, :] = inner.real
    out["t6"] = terms(block.reshape(128, 256))
    return out


def split(values):
    high = values.astype(bf16)
    low = (values - high.astype(f32)).astype(bf16)
    return high, low


def dot(a, b):
    return lax.dot_general(a, b, (((1,), (0,)), ((), ())), preferred_element_type=f32)


def dot_nt(a, b):
    return lax.dot_general(a, b, (((1,), (1,)), ((), ())), preferred_element_type=f32)


def dot3(table, values):
    high, low = split(values)
    return dot(table, jnp.concatenate([high, low, high], 0))


def dot3_nt(table, values):
    high, low = split(values)
    return dot_nt(table, jnp.concatenate([high, low, high], 1))


def times_root(value, numerator, length):
    re, im = value
    numerator %= length
    if numerator == 0:
        return value
    if 4 * numerator == length:
        return im, -re
    if 2 * numerator == length:
        return -re, -im
    if 4 * numerator == 3 * length:
        return -im, re
    if 8 * numerator == length:
        half = math.sqrt(0.5)
        return (re + im) * half, (im - re) * half
    if 8 * numerator == 3 * length:
        half = math.sqrt(0.5)
        return (im - re) * half, (-re - im) * half
    cosine = math.cos(2 * math.pi * numerator / length)
    sine = -math.sin(2 * math.pi * numerator / length)
    return re * cosine - im * sine, re * sine + im * cosine


def transform_list(values):
    count = len(values)
    if count == 1:
        return values
    if count == 2:
        (ar, ai), (br, bi) = values
        return [(ar + br, ai + bi), (ar - br, ai - bi)]
    if count == 4:
        (ar, ai), (br, bi), (cr, ci), (dr, di) = values
        pr, pi_, qr, qi = ar + cr, ai + ci, ar - cr, ai - ci
        sr, si, tr, ti = br + dr, bi + di, br - dr, bi - di
        return [(pr + sr, pi_ + si), (qr + ti, qi - tr), (pr - sr, pi_ - si), (qr - ti, qi + tr)]
    parts = [transform_list(values[start::4]) for start in range(4)]
    quarter = count // 4
    out = [None] * count
    for k in range(quarter):
        column = [times_root(parts[j][k], j * k, count) for j in range(4)]
        for q, value in enumerate(transform_list(column)):
            out[k + q * quarter] = value
    return out


def inverse_list(values):
    swapped = transform_list([(im, re) for re, im in values])
    return [(re, im) for im, re in swapped]


def place():
    narrow = lax.axis_index("narrow")
    return lax.rem(narrow, 2), lax.div(narrow, 2)


def spec_vmem():
    return pl.BlockSpec(memory_space=pltpu.VMEM)


def spec_hbm():
    return pl.BlockSpec(memory_space=pltpu.HBM)


def in_hbm(*values):
    return [pltpu.with_memory_space_constraint(jnp.asarray(value), pltpu.HBM) for value in values]


def fetch(sources, targets, arrived):
    copies = [
        pltpu.make_async_copy(source, target, arrived.at[k])
        for k, (source, target) in enumerate(zip(sources, targets))
    ]
    for copy in copies:
        copy.start()
    return copies


def params(mebibytes=16):
    return pltpu.CompilerParams(vmem_limit_bytes=mebibytes << 20)


def cost(flops, bytes_accessed):
    return pl.CostEstimate(flops=flops, bytes_accessed=bytes_accessed, transcendentals=0)


def columns_kernel(source_ref, out_ref):
    for tile in range(4):
        for part in range(2):
            turned = source_ref[part, :, 128 * tile : 128 * tile + 128].T
            for block in range(4):
                first = 256 * tile + block * 64 + part * 32
                out_ref[first : first + 32, :] = turned[block * 32 : block * 32 + 32]


def columns_major(source):
    return pl.pallas_call(
        columns_kernel,
        grid=(2,),
        in_specs=[pl.BlockSpec((2, 128, 512), lambda t: (0, 0, t))],
        out_specs=pl.BlockSpec((1024, 128), lambda t: (t, 0)),
        out_shape=pltpu.HBM((2048, 128), f32),
        cost_estimate=cost(0, 2 << 20),
        name="columns_major",
    )(source)


def x_forward_kernel(
    a_ref, t1_hbm, tw_hbm, t2_hbm, out_hbm, t1_ref, tw_ref, t2_ref, out_ref, arrived, sent
):
    for copy in fetch((t1_hbm, tw_hbm, t2_hbm), (t1_ref, tw_ref, t2_ref), arrived):
        copy.wait()

    @pl.loop(0, 16, unroll=8)
    def _(c):
        columns = []
        for b0 in range(2):
            re = a_ref[pl.ds(2 * c + b0, 32, stride=64), :]
            im = a_ref[pl.ds(2 * c + b0 + 32, 32, stride=64), :]
            columns.append(jnp.concatenate([re, im], 0))
        u = dot3(t1_ref[...], jnp.concatenate(columns, 1))
        rows = []
        for b0 in range(2):
            ur = u[:64, 128 * b0 : 128 * b0 + 128]
            ui = u[64:, 128 * b0 : 128 * b0 + 128]
            rows.append(
                jnp.concatenate(
                    [ur * tw_ref[0] - ui * tw_ref[1], ur * tw_ref[1] + ui * tw_ref[0]], 1
                )
            )
        z = jnp.concatenate(rows, 0)
        out = dot3_nt(t2_ref[...], z)
        out_ref[pl.ds(c, 128, stride=32), :] = out[:128]
        out_ref[pl.ds(c + 16, 128, stride=32), :] = out[128:]

    last = pltpu.make_async_copy(out_ref, out_hbm, sent)
    last.start()
    last.wait()


def x_forward(a):
    t = tables()
    return pl.pallas_call(
        x_forward_kernel,
        in_specs=[spec_vmem()] + [spec_hbm()] * 3,
        out_specs=spec_hbm(),
        out_shape=pltpu.HBM((4096, 128), f32),
        scratch_shapes=[
            pltpu.VMEM((128, 192), bf16),
            pltpu.VMEM((2, 64, 128), f32),
            pltpu.VMEM((256, 768), bf16),
            pltpu.VMEM((4096, 128), f32),
            pltpu.SemaphoreType.DMA((3,)),
            pltpu.SemaphoreType.DMA,
        ],
        compiler_params=params(8),
        cost_estimate=cost(2 * 2048 * 65536 * 4, 4 << 20),
        name="x_forward",
    )(a, *in_hbm(t["t1"], t["tw1"], t["t2"]))


def line_row(c):
    return c // 8 * 16 + c % 8


def middle_kernel(
    a_ref, t3_hbm, tw_hbm, step_hbm, r0_hbm, r1_hbm, r2_hbm, r3_hbm, lane_hbm, t4_hbm,
    out_hbm, t3_ref, tw_ref, step_ref, green_ref, lane_ref, t4_ref, u_ref, now_ref, out_ref,
    spread_ref, arrived, sent, moved,
):
    flip, upper = place()
    spread = pltpu.make_async_copy(
        a_ref.reshape(128, 32, 128), spread_ref.reshape(128, 40, 128).at[:, pl.ds(0, 32)], moved
    )
    spread.start()
    copies = fetch(
        (t3_hbm, tw_hbm, step_hbm, r0_hbm, r1_hbm, r2_hbm.at[0], r3_hbm, lane_hbm, t4_hbm),
        (t3_ref, tw_ref, step_ref)
        + tuple(green_ref.at[g, h] for h in (upper, 1 - upper) for g in range(2))
        + (lane_ref, t4_ref),
        arrived,
    )
    for copy in copies[:3]:
        copy.wait()
    spread.wait()
    sign = 1.0 - 2.0 * flip.astype(f32)
    step_ref[...] = step_ref[...] * sign
    now_ref[0] = tw_ref[...]

    for cc in range(8):
        columns = []
        for half in range(2):
            re = spread_ref[pl.ds(2 * cc + half, 128, stride=40), :]
            im = spread_ref[pl.ds(2 * cc + half + 16, 128, stride=40), :]
            columns.append(jnp.concatenate([re, im], 0))
        u = dot3(t3_ref[...], jnp.concatenate(columns, 1))
        for half in range(2):
            ur = u[:256, 128 * half : 128 * half + 128]
            ui = u[256:, 128 * half : 128 * half + 128]
            c = 2 * cc + half
            nr = now_ref[c, 0]
            ni = now_ref[c, 1]
            u_ref[c, 0, :256, :] = ur * nr - ui * ni
            u_ref[c, 1, :256, :] = ur * ni + ui * nr
            if c < 15:
                now_ref[c + 1, 0] = nr * step_ref[0] - ni * step_ref[1]
                now_ref[c + 1, 1] = nr * step_ref[1] + ni * step_ref[0]

    for copy in copies[3:]:
        copy.wait()

    lane = lax.broadcasted_iota(jnp.int32, (8, 128), 1)
    low = lane < 64

    def trade(first, second):
        middle_part = pltpu.roll(jnp.where(low, second, first), 64, 1)
        return jnp.where(low, first, middle_part), jnp.where(low, middle_part, second)

    @pl.loop(0, 32, unroll=4)
    def _(tile):
        rows = pl.ds(pl.multiple_of(tile * 8, 8), 8)
        values = [(u_ref[c, 0, rows, :], u_ref[c, 1, rows, :]) for c in range(16)]
        spectrum = transform_list(values)
        back = [None] * 16
        for index in range(8):
            g, r = index // 4, index % 4
            e = 8 * g + r
            grows = pl.ds(pl.multiple_of(tile * 8 + r * 256, 8), 8)
            lr = lane_ref[flip, 0, index : index + 1, :]
            li = lane_ref[flip, 1, index : index + 1, :]
            even_r, odd_r = trade(spectrum[e][0], spectrum[e + 4][0])
            even_i, odd_i = trade(spectrum[e][1], spectrum[e + 4][1])
            odd_r, odd_i = odd_r * lr - odd_i * li, odd_r * li + odd_i * lr
            products = []
            for h, (fr, fi) in enumerate(
                ((even_r + odd_r, even_i + odd_i), (even_r - odd_r, even_i - odd_i))
            ):
                gr = green_ref[g, h, 0, grows, :]
                gi = green_ref[g, h, 1, grows, :]
                products.append((gr * fr - gi * fi, gr * fi + gi * fr))
            (ar, ai), (br, bi) = products
            odd_r, odd_i = ar - br, ai - bi
            odd_r, odd_i = odd_r * lr + odd_i * li, odd_i * lr - odd_r * li
            first_r, second_r = trade(ar + br, odd_r)
            first_i, second_i = trade(ai + bi, odd_i)
            back[e] = (first_r, first_i)
            back[e + 4] = (second_r, second_i)
        for c, (re, im) in enumerate(inverse_list(back)):
            u_ref[c, 0, rows, :] = re
            u_ref[c, 1, rows, :] = im

    halves = []
    for cc in range(8):
        columns = []
        for half in range(2):
            ur = u_ref[2 * cc + half, 0, :256, :]
            ui = u_ref[2 * cc + half, 1, :256, :]
            nr = now_ref[2 * cc + half, 0]
            ni = now_ref[2 * cc + half, 1]
            columns.append(jnp.concatenate([ur * nr + ui * ni, ui * nr - ur * ni], 0))
        out = dot3(t4_ref[...], jnp.concatenate(columns, 1))
        for half in range(2):
            lanes = slice(128 * half, 128 * half + 128)
            row = line_row(2 * cc + half)
            out_ref[pl.ds(row, 128, stride=40), :] = out[:128, lanes]
            out_ref[pl.ds(row + 8, 128, stride=40), :] = out[128:, lanes]
        if cc % 4 == 3:
            rows = pl.ds(cc // 4 * 16, 16)
            halves.append(
                pltpu.make_async_copy(
                    out_ref.reshape(128, 40, 128).at[:, rows], out_hbm.at[:, rows], sent.at[cc // 4]
                )
            )
            halves[-1].start()
    for copy in halves:
        copy.wait()


def middle(a, greens):
    t = tables()
    return pl.pallas_call(
        middle_kernel,
        in_specs=[spec_vmem()] + [spec_hbm()] * 9,
        out_specs=spec_hbm(),
        out_shape=pltpu.HBM((128, 32, 128), f32),
        scratch_shapes=[
            pltpu.VMEM((512, 768), bf16),
            pltpu.VMEM((2, 256, 128), f32),
            pltpu.VMEM((2, 256, 128), f32),
            pltpu.VMEM((2, 2, 2, 1024, 128), f32),
            pltpu.VMEM((2, 2, 8, 128), f32),
            pltpu.VMEM((256, 1536), bf16),
            pltpu.VMEM((16, 2, 264, 128), f32),
            pltpu.VMEM((16, 2, 256, 128), f32),
            pltpu.VMEM((5120, 128), f32),
            pltpu.VMEM((5120, 128), f32),
            pltpu.SemaphoreType.DMA((9,)),
            pltpu.SemaphoreType.DMA((2,)),
            pltpu.SemaphoreType.DMA,
        ],
        compiler_params=params(32),
        cost_estimate=cost(2 * 8 * 2 * 512 * 65536 * 3, 10 << 20),
        name="middle",
    )(
        a, *in_hbm(t["t3"], t["tw3"], t["step3"], *greens, t["lane3"], t["t4"])
    )


def x_inverse_kernel(
    a_ref, t5_hbm, tw_hbm, t6_hbm, out_hbm, t5_ref, tw_ref, t6_ref, spread_ref, out_ref, arrived,
    sent, moved,
):
    spread = pltpu.make_async_copy(
        a_ref.reshape(128, 32, 128), spread_ref.reshape(128, 40, 128).at[:, pl.ds(0, 32)], moved
    )
    spread.start()
    for copy in fetch((t5_hbm, tw_hbm, t6_hbm), (t5_ref, tw_ref, t6_ref), arrived):
        copy.wait()
    spread.wait()

    blocks = []
    for cc in range(8):
        columns = []
        for half in range(2):
            row = line_row(2 * cc + half)
            re = spread_ref[pl.ds(row, 128, stride=40), :]
            im = spread_ref[pl.ds(row + 8, 128, stride=40), :]
            columns.append(jnp.concatenate([re, im], 0))
        u = dot3(t5_ref[...], jnp.concatenate(columns, 1))
        rows = []
        for half in range(2):
            ur = u[:128, 128 * half : 128 * half + 128]
            ui = u[128:, 128 * half : 128 * half + 128]
            rows.append(
                jnp.concatenate(
                    [ur * tw_ref[0] - ui * tw_ref[1], ur * tw_ref[1] + ui * tw_ref[0]], 1
                )
            )
        out = dot3_nt(t6_ref[...], jnp.concatenate(rows, 0))
        for half in range(2):
            lanes = slice(128 * half, 128 * half + 128)
            for b0 in range(2):
                row = line_row(4 * cc + 2 * half + b0)
                out_ref[pl.ds(row, 32, stride=72), :] = out[64 * b0 : 64 * b0 + 32, lanes]
                out_ref[pl.ds(row + 8, 32, stride=72), :] = out[64 * b0 + 32 : 64 * b0 + 64, lanes]
        if cc % 2 == 1:
            rows = pl.ds(cc // 2 * 16, 16)
            blocks.append(
                pltpu.make_async_copy(
                    out_ref.reshape(32, 72, 128).at[:, rows], out_hbm.at[:, rows], sent.at[cc // 2]
                )
            )
            blocks[-1].start()
    for copy in blocks:
        copy.wait()


def x_inverse(a):
    t = tables()
    return pl.pallas_call(
        x_inverse_kernel,
        in_specs=[spec_vmem()] + [spec_hbm()] * 3,
        out_specs=spec_hbm(),
        out_shape=pltpu.HBM((32, 64, 128), f32),
        scratch_shapes=[
            pltpu.VMEM((256, 768), bf16),
            pltpu.VMEM((2, 128, 128), f32),
            pltpu.VMEM((128, 768), bf16),
            pltpu.VMEM((5120, 128), f32),
            pltpu.VMEM((2304, 128), f32),
            pltpu.SemaphoreType.DMA((3,)),
            pltpu.SemaphoreType.DMA((4,)),
            pltpu.SemaphoreType.DMA,
        ],
        compiler_params=params(12),
        cost_estimate=cost(2 * 2048 * 65536 * 4, 4 << 20),
        name="x_inverse",
    )(a, *in_hbm(t["t5"], t["tw5"], t["t6"]))


def residual_kernel(a_ref, contrast_ref, known_ref, out_ref):
    for tile in range(4):
        lanes = slice(128 * tile, 128 * tile + 128)
        scattered = []
        for part in range(2):
            rows = []
            for block in range(16):
                first = 256 * tile + block * 16 + part * 8
                rows.append(a_ref[first : first + 8, :])
            scattered.append(jnp.concatenate(rows, 0).T)
        cr = contrast_ref[0, :, lanes]
        ci = contrast_ref[1, :, lanes]
        out_ref[0, :, lanes] = cr * scattered[0] - ci * scattered[1] + known_ref[0, :, lanes]
        out_ref[1, :, lanes] = cr * scattered[1] + ci * scattered[0] + known_ref[1, :, lanes]


def residual_of(a, contrast, known):
    tile = pl.BlockSpec((2, 128, 512), lambda t: (0, 0, t))
    return pl.pallas_call(
        residual_kernel,
        grid=(2,),
        in_specs=[pl.BlockSpec((1024, 128), lambda t: (t, 0)), tile, tile],
        out_specs=tile,
        out_shape=jax.ShapeDtypeStruct((2, 128, 1024), f32),
        compiler_params=params(),
        cost_estimate=cost(0, 4 << 20),
        name="residual",
    )(a, contrast, known)


def pack_kernel(across, green_hbm, *refs):
    out_hbms, (green_ref, out_ref, arrived, sent) = refs[:-4], refs[-4:]
    flip, upper = place()
    column = jnp.where(upper == 1, 1 - across, across)
    lanes = pl.ds(pl.multiple_of(column * 128, 128), 128)
    lane = lax.broadcasted_iota(jnp.int32, (512, 128), 1)
    low = lane < 64
    pick = low == (flip == 0)
    pieces = [(part, pl.ds(first, 512)) for first in (0, 512) for part in range(2)]
    copies = fetch(
        [green_hbm.at[part, :, rows, lanes] for part, rows in pieces],
        [green_ref.at[part, :, rows] for part, rows in pieces],
        arrived,
    )
    leaving = []
    for k, (part, rows) in enumerate(pieces):
        copies[k].wait()
        first = green_ref[part, 0, rows]
        second = green_ref[part, 1, rows]
        straight = jnp.where(low, first, second)
        crossed = pltpu.roll(jnp.where(low, second, first), 64, 1)
        for core, value in enumerate(
            (jnp.where(pick, straight, crossed), jnp.where(pick, crossed, straight))
        ):
            out_ref[core, part, rows] = value
            target = out_hbms[0].at[core] if across else out_hbms[core]
            leaving.append(
                pltpu.make_async_copy(
                    out_ref.at[core, part, rows], target.at[part, rows], sent.at[k, core]
                )
            )
            leaving[-1].start()
    for copy in leaving:
        copy.wait()


def pack_green(green, across):
    if across:
        out_shape = [pltpu.HBM((2, 2, 1024, 128), f32)]
    else:
        out_shape = [pltpu.HBM((2, 1024, 128), f32)] * 2
    out = pl.pallas_call(
        functools.partial(pack_kernel, across),
        in_specs=[spec_hbm()],
        out_specs=[spec_hbm()] * len(out_shape),
        out_shape=out_shape,
        scratch_shapes=[
            pltpu.VMEM((2, 2, 1024, 128), f32),
            pltpu.VMEM((2, 2, 1024, 128), f32),
            pltpu.SemaphoreType.DMA((4,)),
            pltpu.SemaphoreType.DMA((4, 2)),
        ],
        compiler_params=params(12),
        cost_estimate=cost(0, 4 << 20),
        name="pack_far" if across else "pack_near",
    )(*in_hbm(green.reshape(2, 2, 1024, 256)))
    return out[0] if across else out


def second_kernel(in_ref, out_ref):
    out_ref[...] = in_ref[0]


def second_of(values):
    return pl.pallas_call(
        second_kernel,
        grid=(2,),
        in_specs=[pl.BlockSpec((1, 1, 1024, 128), lambda t: (1, t, 0, 0))],
        out_specs=pl.BlockSpec((1, 1024, 128), lambda t: (t, 0, 0)),
        out_shape=pltpu.HBM(values.shape[1:], f32),
        compiler_params=params(8),
        cost_estimate=cost(0, 2 << 20),
        name="second",
    )(*in_hbm(values))


def project_kernel(source_ref, ea_ref, eb_ref, row_ref, out_ref, lhs_ref, rhs_ref):
    @pl.when(pl.program_id(0) == 0)
    def _():
        re = source_ref[0]
        im = source_ref[1]
        for rows, cols, value in (
            (0, 0, re), (0, 1024, -im), (128, 0, im), (128, 1024, re),
        ):
            high, low = split(value)
            lhs_ref[0, rows : rows + 128, cols : cols + 1024] = high
            lhs_ref[1, rows : rows + 128, cols : cols + 1024] = low

    br = eb_ref[0]
    bi = eb_ref[1]
    for a in range(32):
        ar = ea_ref[0, a : a + 1, :]
        ai = ea_ref[1, a : a + 1, :]
        for part, value in ((0, ar * br - ai * bi), (1, ar * bi + ai * br)):
            high, low = split(value)
            rhs_ref[0, part * 1024 + a * 32 : part * 1024 + a * 32 + 32, :] = high
            rhs_ref[1, part * 1024 + a * 32 : part * 1024 + a * 32 + 32, :] = low
    inner = dot(lhs_ref[0], rhs_ref[0]) + (dot(lhs_ref[0], rhs_ref[1]) + dot(lhs_ref[1], rhs_ref[0]))
    ir = inner[:128]
    ii = inner[128:]
    fr = row_ref[0]
    fi = row_ref[1]
    pr = jnp.sum(fr * ir - fi * ii, axis=0, keepdims=True)
    pi_ = jnp.sum(fr * ii + fi * ir, axis=0, keepdims=True)
    out_ref[...] = jnp.concatenate([pr, pi_, jnp.zeros((6, pr.shape[1]), f32)], 0)


def project(source, ea, eb, rows):
    tile = 256
    whole = pl.BlockSpec((2, 128, 1024), lambda t: (0, 0, 0))
    return pl.pallas_call(
        project_kernel,
        grid=(R // tile,),
        in_specs=[
            whole,
            pl.BlockSpec((2, 32, tile), lambda t: (0, 0, t)),
            pl.BlockSpec((2, 32, tile), lambda t: (0, 0, t)),
            pl.BlockSpec((2, 128, tile), lambda t: (0, 0, t)),
        ],
        out_specs=pl.BlockSpec((8, tile), lambda t: (0, t)),
        out_shape=jax.ShapeDtypeStruct((8, R), f32),
        scratch_shapes=[pltpu.VMEM((2, 256, 2048), bf16), pltpu.VMEM((2, 2048, tile), bf16)],
        compiler_params=params(),
        cost_estimate=cost(2 * 256 * 2048 * 1024 * 3, 4 << 20),
        name="project",
    )(source, ea, eb, rows)


def backproject_kernel(weight_ref, ea_ref, eb_ref, out_ref, lhs_ref, rhs_ref):
    @pl.when(pl.program_id(0) == 0)
    def _():
        wr = weight_ref[0]
        wi = weight_ref[1]
        for rows, cols, value in (
            (0, 0, wr), (0, 1024, wi), (128, 0, wi), (128, 1024, -wr),
        ):
            high, low = split(value)
            lhs_ref[0, rows : rows + 128, cols : cols + 1024] = high
            lhs_ref[1, rows : rows + 128, cols : cols + 1024] = low

    br = eb_ref[0]
    bi = eb_ref[1]
    for a in range(8):
        ar = ea_ref[0, a : a + 1, :]
        ai = ea_ref[1, a : a + 1, :]
        for part, value in ((0, ar * br - ai * bi), (1, ar * bi + ai * br)):
            high, low = split(value)
            rhs_ref[0, a * 32 : a * 32 + 32, part * 1024 : part * 1024 + 1024] = high
            rhs_ref[1, a * 32 : a * 32 + 32, part * 1024 : part * 1024 + 1024] = low
    out = dot_nt(lhs_ref[0], rhs_ref[0]) + (
        dot_nt(lhs_ref[0], rhs_ref[1]) + dot_nt(lhs_ref[1], rhs_ref[0])
    )
    out_ref[0] = out[:128]
    out_ref[1] = out[128:]


def backproject(weights, ea, eb):
    whole = pl.BlockSpec((2, 128, 1024), lambda t: (0, 0, 0))
    return pl.pallas_call(
        backproject_kernel,
        grid=(4,),
        in_specs=[
            whole,
            pl.BlockSpec((2, 8, 1024), lambda t: (0, t, 0)),
            pl.BlockSpec((2, 32, 1024), lambda t: (0, 0, 0)),
        ],
        out_specs=pl.BlockSpec((2, 128, 256), lambda t: (0, 0, t)),
        out_shape=jax.ShapeDtypeStruct((2, 128, 1024), f32),
        scratch_shapes=[pltpu.VMEM((2, 256, 2048), bf16), pltpu.VMEM((2, 256, 2048), bf16)],
        compiler_params=params(),
        cost_estimate=cost(2 * 256 * 2048 * 1024 * 3, 4 << 20),
        name="backproject",
    )(weights, ea, eb)


def phase_pair(position, direction):
    phase = (wave_step * position)[:, None] * direction[None, :]
    return jnp.stack([jnp.cos(phase), -jnp.sin(phase)])


def sum_over(value, steps):
    def exchange(value, axis, size, strides):
        parts = [value] + [
            lax.ppermute(value, axis, [(j, j ^ stride) for j in range(size)]) for stride in strides
        ]
        while len(parts) > 1:
            parts = [parts[j] + parts[j + 1] for j in range(0, len(parts), 2)]
        return parts[0]

    for axis, size, strides in steps:
        value = exchange(value, axis, size, strides)
    return value


def local(sources, incident, contrast, green, angles, measured):
    wide = lax.axis_index("wide")
    narrow = lax.axis_index("narrow")
    source = sources[0]

    def partner(value, k):
        return lax.ppermute(value, "narrow", [(j, j ^ k) for j in range(NARROW)])

    lines = columns_major(source)
    lines, green = lax.optimization_barrier((lines, green))
    far = partner(pack_green(green, 1), 2)
    lines = lax.all_to_all(lines.reshape(WIDE, 64, 128), "wide", 0, 0, tiled=True)

    row_position = (wide * 128 + jnp.arange(128, dtype=jnp.int32)).astype(f32) - N // 2 + 0.5
    block_position = (narrow * 1024 + 32 * jnp.arange(32, dtype=jnp.int32)).astype(f32) - N // 2 + 0.5
    cell_position = jnp.arange(32, dtype=jnp.int32).astype(f32)
    rows = phase_pair(row_position, jnp.cos(angles))
    sine = jnp.sin(angles)
    ea = phase_pair(block_position, sine)
    eb = phase_pair(cell_position, sine)
    partial_value = project(source, ea, eb, rows)
    lines, partial_value = lax.optimization_barrier((lines, partial_value))
    lines = x_forward(lines.reshape(2048, 128))
    lines, partial_value = lax.optimization_barrier((lines, partial_value))
    lines = lax.all_to_all(lines.reshape(128, 32, 128), ("wide", "narrow"), 0, 0, tiled=True)

    total = sum_over(partial_value, [("wide", WIDE, (1, 2, 3)), ("wide", WIDE, (8, 16, 24))])
    total, green = lax.optimization_barrier((total, green))
    near = pack_green(green, 0)
    near_partner = partner(near[1], 1)
    total, far, near_partner = lax.optimization_barrier((total, far, near_partner))
    total = sum_over(total, [("narrow", NARROW, (1,))])
    greens = [near[0], near_partner, far, partner(second_of(far), 1)]
    total, lines = lax.optimization_barrier((total, lines))
    lines = middle(lines.reshape(4096, 128), greens)
    total, lines = lax.optimization_barrier((total, lines))
    lines = lax.all_to_all(lines.reshape(128, 32, 128), ("wide", "narrow"), 0, 0, tiled=True)
    total = sum_over(
        total, [(("wide", "narrow"), WIDE * NARROW, (2, 4 * NARROW, 4 * NARROW + 2))]
    )[:2]
    lines = x_inverse(lines.reshape(4096, 128))
    lines, contrast = lax.optimization_barrier((lines, contrast))
    known = jnp.stack(
        [
            contrast[0] * incident[0, 0] - contrast[1] * incident[0, 1] - source[0],
            contrast[0] * incident[0, 1] + contrast[1] * incident[0, 0] - source[1],
        ]
    )
    lines = lax.all_to_all(lines.reshape(WIDE, 64, 128), "wide", 0, 0, tiled=True)
    residual = residual_of(lines.reshape(2048, 128), contrast, known)

    data_residual = measured - total[None] * (1.0 / N)
    rho_real = data_residual[0, 0][None, :]
    rho_imag = data_residual[0, 1][None, :]
    scale = 1.0 / math.sqrt(R)
    weights = jnp.stack(
        [
            (rows[0] * rho_real + rows[1] * rho_imag) * scale,
            (rows[0] * rho_imag - rows[1] * rho_real) * scale,
        ]
    )
    back = backproject(weights, ea, eb)
    return (residual[None], back[None], data_residual)


def solution(mesh):
    placed = (
        P(None, None, "wide", "narrow"),
        P(None, None, "wide", "narrow"),
        P(None, "wide", "narrow"),
        P(None, "narrow", "wide"),
        P(),
        P(),
    )
    return jax.shard_map(
        local,
        mesh=mesh,
        in_specs=placed,
        out_specs=(P(None, None, "wide", "narrow"), P(None, None, "wide", "narrow"), P()),
        check_vma=False,
    )
```

```python
import functools
import math

import jax
import jax.numpy as jnp
import ml_dtypes
import numpy as np
from jax import lax
from jax.experimental import pallas as pl
from jax.experimental.pallas import tpu as pltpu
from jax.sharding import PartitionSpec as P

N = 4096
R = 1024
M = 8192
WIDE = 32
NARROW = 4

wave_step = 0.2 * math.pi
f32 = jnp.float32
bf16 = jnp.bfloat16


def complex_block(table):
    return np.block([[table.real, -table.imag], [table.imag, table.real]])


def terms(table):
    high = table.astype(np.float32).astype(ml_dtypes.bfloat16)
    low = (table - high.astype(np.float64)).astype(np.float32).astype(ml_dtypes.bfloat16)
    return np.concatenate([high, high, low], 1)


def root(product, length, sign):
    return np.exp(sign * 2j * np.pi * (product % length) / length)


def pair(table):
    return np.stack([table.real, table.imag]).astype(np.float32)


@functools.lru_cache(None)
def tables():
    out = {}
    w = np.arange(32)
    k1 = np.arange(64)
    i = np.arange(128)
    m = np.arange(128)
    out["t1"] = terms(complex_block(root(np.outer(k1, w), 64, -1)))
    out["tw1"] = pair(root(np.outer(k1, i), M, -1))
    out["t2"] = terms(complex_block(root(np.outer(m, i), 128, -1)))
    d = np.arange(128)
    s = 32 * (d % 4) + d // 4
    c1 = np.arange(256)
    out["t3"] = terms(complex_block(root(np.outer(c1, s), 256, -1)))
    low_half = np.arange(128) < 64
    first = np.where(low_half[None, :], 1.0, root(c1, M, -1)[:, None])
    out["tw3"] = pair(first)
    out["step3"] = pair(root(2 * c1, M, -1)[:, None] * np.ones((1, 128)))
    lanes = []
    for flip in (0, 1):
        first_e = (np.array([0, 1, 2, 3, 8, 9, 10, 11]) + 8 * flip) % 16
        e = np.where(low_half[None, :], first_e[:, None], first_e[:, None] + 4)
        lanes.append(pair(root(e, 32, -1)))
    out["lane3"] = np.stack(lanes)
    out["t4"] = terms(complex_block(root(np.outer(s, c1), 256, 1)))
    out["t5"] = terms(complex_block(root(np.outer(i, m), 128, 1)))
    lane_k1 = np.arange(128) % 64
    out["tw5"] = pair(root(np.outer(i, lane_k1), M, 1))
    inner = root(np.outer(w, k1), 64, 1) / (M * M)
    block = np.zeros((2, 2, 32, 2, 2, 64))
    for b0 in (0, 1):
        block[b0, 0, :, 0, b0, :] = inner.real
        block[b0, 0, :, 1, b0, :] = -inner.imag
        block[b0, 1, :, 0, b0, :] = inner.imag
        block[b0, 1, :, 1, b0, :] = inner.real
    out["t6"] = terms(block.reshape(128, 256))
    return out


def split(values):
    high = values.astype(bf16)
    low = (values - high.astype(f32)).astype(bf16)
    return high, low


def dot(a, b):
    return lax.dot_general(a, b, (((1,), (0,)), ((), ())), preferred_element_type=f32)


def dot_nt(a, b):
    return lax.dot_general(a, b, (((1,), (1,)), ((), ())), preferred_element_type=f32)


def dot3(table, values):
    high, low = split(values)
    return dot(table, jnp.concatenate([high, low, high], 0))


def dot3_nt(table, values):
    high, low = split(values)
    return dot_nt(table, jnp.concatenate([high, low, high], 1))


def times_root(value, numerator, length):
    re, im = value
    numerator %= length
    if numerator == 0:
        return value
    if 4 * numerator == length:
        return im, -re
    if 2 * numerator == length:
        return -re, -im
    if 4 * numerator == 3 * length:
        return -im, re
    if 8 * numerator == length:
        half = math.sqrt(0.5)
        return (re + im) * half, (im - re) * half
    if 8 * numerator == 3 * length:
        half = math.sqrt(0.5)
        return (im - re) * half, (-re - im) * half
    cosine = math.cos(2 * math.pi * numerator / length)
    sine = -math.sin(2 * math.pi * numerator / length)
    return re * cosine - im * sine, re * sine + im * cosine


def transform_list(values):
    count = len(values)
    if count == 1:
        return values
    if count == 2:
        (ar, ai), (br, bi) = values
        return [(ar + br, ai + bi), (ar - br, ai - bi)]
    if count == 4:
        (ar, ai), (br, bi), (cr, ci), (dr, di) = values
        pr, pi_, qr, qi = ar + cr, ai + ci, ar - cr, ai - ci
        sr, si, tr, ti = br + dr, bi + di, br - dr, bi - di
        return [(pr + sr, pi_ + si), (qr + ti, qi - tr), (pr - sr, pi_ - si), (qr - ti, qi + tr)]
    parts = [transform_list(values[start::4]) for start in range(4)]
    quarter = count // 4
    out = [None] * count
    for k in range(quarter):
        column = [times_root(parts[j][k], j * k, count) for j in range(4)]
        for q, value in enumerate(transform_list(column)):
            out[k + q * quarter] = value
    return out


def inverse_list(values):
    swapped = transform_list([(im, re) for re, im in values])
    return [(re, im) for im, re in swapped]


def place():
    narrow = lax.axis_index("narrow")
    return lax.rem(narrow, 2), lax.div(narrow, 2)


def spec_vmem():
    return pl.BlockSpec(memory_space=pltpu.VMEM)


def spec_hbm():
    return pl.BlockSpec(memory_space=pltpu.HBM)


def in_hbm(*values):
    return [pltpu.with_memory_space_constraint(jnp.asarray(value), pltpu.HBM) for value in values]


def fetch(sources, targets, arrived):
    copies = [
        pltpu.make_async_copy(source, target, arrived.at[k])
        for k, (source, target) in enumerate(zip(sources, targets))
    ]
    for copy in copies:
        copy.start()
    return copies


def params(mebibytes=16):
    return pltpu.CompilerParams(vmem_limit_bytes=mebibytes << 20)


def cost(flops, bytes_accessed):
    return pl.CostEstimate(flops=flops, bytes_accessed=bytes_accessed, transcendentals=0)


def columns_kernel(source_ref, out_ref):
    for tile in range(4):
        for part in range(2):
            turned = source_ref[part, :, 128 * tile : 128 * tile + 128].T
            for block in range(4):
                first = 256 * tile + block * 64 + part * 32
                out_ref[first : first + 32, :] = turned[block * 32 : block * 32 + 32]


def columns_major(source):
    return pl.pallas_call(
        columns_kernel,
        grid=(2,),
        in_specs=[pl.BlockSpec((2, 128, 512), lambda t: (0, 0, t))],
        out_specs=pl.BlockSpec((1024, 128), lambda t: (t, 0)),
        out_shape=pltpu.HBM((2048, 128), f32),
        cost_estimate=cost(0, 2 << 20),
        name="columns_major",
    )(source)


def x_forward_kernel(
    a_ref, t1_hbm, tw_hbm, t2_hbm, out_hbm, t1_ref, tw_ref, t2_ref, out_ref, arrived, sent
):
    for copy in fetch((t1_hbm, tw_hbm, t2_hbm), (t1_ref, tw_ref, t2_ref), arrived):
        copy.wait()

    @pl.loop(0, 16, unroll=8)
    def _(c):
        columns = []
        for b0 in range(2):
            re = a_ref[pl.ds(2 * c + b0, 32, stride=64), :]
            im = a_ref[pl.ds(2 * c + b0 + 32, 32, stride=64), :]
            columns.append(jnp.concatenate([re, im], 0))
        u = dot3(t1_ref[...], jnp.concatenate(columns, 1))
        rows = []
        for b0 in range(2):
            ur = u[:64, 128 * b0 : 128 * b0 + 128]
            ui = u[64:, 128 * b0 : 128 * b0 + 128]
            rows.append(
                jnp.concatenate(
                    [ur * tw_ref[0] - ui * tw_ref[1], ur * tw_ref[1] + ui * tw_ref[0]], 1
                )
            )
        z = jnp.concatenate(rows, 0)
        out = dot3_nt(t2_ref[...], z)
        out_ref[pl.ds(c, 128, stride=32), :] = out[:128]
        out_ref[pl.ds(c + 16, 128, stride=32), :] = out[128:]

    last = pltpu.make_async_copy(out_ref, out_hbm, sent)
    last.start()
    last.wait()


def x_forward(a):
    t = tables()
    return pl.pallas_call(
        x_forward_kernel,
        in_specs=[spec_vmem()] + [spec_hbm()] * 3,
        out_specs=spec_hbm(),
        out_shape=pltpu.HBM((4096, 128), f32),
        scratch_shapes=[
            pltpu.VMEM((128, 192), bf16),
            pltpu.VMEM((2, 64, 128), f32),
            pltpu.VMEM((256, 768), bf16),
            pltpu.VMEM((4096, 128), f32),
            pltpu.SemaphoreType.DMA((3,)),
            pltpu.SemaphoreType.DMA,
        ],
        compiler_params=params(8),
        cost_estimate=cost(2 * 2048 * 65536 * 4, 4 << 20),
        name="x_forward",
    )(a, *in_hbm(t["t1"], t["tw1"], t["t2"]))


def line_row(c):
    return c // 8 * 16 + c % 8


def middle_kernel(
    a_ref, t3_hbm, tw_hbm, step_hbm, r0_hbm, r1_hbm, r2_hbm, r3_hbm, lane_hbm, t4_hbm,
    out_hbm, t3_ref, tw_ref, step_ref, green_ref, lane_ref, t4_ref, u_ref, now_ref, out_ref,
    spread_ref, arrived, sent, moved,
):
    flip, upper = place()
    spread = pltpu.make_async_copy(
        a_ref.reshape(128, 32, 128), spread_ref.reshape(128, 40, 128).at[:, pl.ds(0, 32)], moved
    )
    spread.start()
    copies = fetch(
        (t3_hbm, tw_hbm, step_hbm, r0_hbm, r1_hbm, r2_hbm.at[0], r3_hbm, lane_hbm, t4_hbm),
        (t3_ref, tw_ref, step_ref)
        + tuple(green_ref.at[g, h] for h in (upper, 1 - upper) for g in range(2))
        + (lane_ref, t4_ref),
        arrived,
    )
    for copy in copies[:3]:
        copy.wait()
    spread.wait()
    sign = 1.0 - 2.0 * flip.astype(f32)
    step_ref[...] = step_ref[...] * sign
    now_ref[0] = tw_ref[...]

    for cc in range(8):
        columns = []
        for half in range(2):
            re = spread_ref[pl.ds(2 * cc + half, 128, stride=40), :]
            im = spread_ref[pl.ds(2 * cc + half + 16, 128, stride=40), :]
            columns.append(jnp.concatenate([re, im], 0))
        u = dot3(t3_ref[...], jnp.concatenate(columns, 1))
        for half in range(2):
            ur = u[:256, 128 * half : 128 * half + 128]
            ui = u[256:, 128 * half : 128 * half + 128]
            c = 2 * cc + half
            nr = now_ref[c, 0]
            ni = now_ref[c, 1]
            u_ref[c, 0, :256, :] = ur * nr - ui * ni
            u_ref[c, 1, :256, :] = ur * ni + ui * nr
            if c < 15:
                now_ref[c + 1, 0] = nr * step_ref[0] - ni * step_ref[1]
                now_ref[c + 1, 1] = nr * step_ref[1] + ni * step_ref[0]

    for copy in copies[3:]:
        copy.wait()

    lane = lax.broadcasted_iota(jnp.int32, (8, 128), 1)
    low = lane < 64

    def trade(first, second):
        middle_part = pltpu.roll(jnp.where(low, second, first), 64, 1)
        return jnp.where(low, first, middle_part), jnp.where(low, middle_part, second)

    @pl.loop(0, 32, unroll=4)
    def _(tile):
        rows = pl.ds(pl.multiple_of(tile * 8, 8), 8)
        values = [(u_ref[c, 0, rows, :], u_ref[c, 1, rows, :]) for c in range(16)]
        spectrum = transform_list(values)
        back = [None] * 16
        for index in range(8):
            g, r = index // 4, index % 4
            e = 8 * g + r
            grows = pl.ds(pl.multiple_of(tile * 8 + r * 256, 8), 8)
            lr = lane_ref[flip, 0, index : index + 1, :]
            li = lane_ref[flip, 1, index : index + 1, :]
            even_r, odd_r = trade(spectrum[e][0], spectrum[e + 4][0])
            even_i, odd_i = trade(spectrum[e][1], spectrum[e + 4][1])
            odd_r, odd_i = odd_r * lr - odd_i * li, odd_r * li + odd_i * lr
            products = []
            for h, (fr, fi) in enumerate(
                ((even_r + odd_r, even_i + odd_i), (even_r - odd_r, even_i - odd_i))
            ):
                gr = green_ref[g, h, 0, grows, :]
                gi = green_ref[g, h, 1, grows, :]
                products.append((gr * fr - gi * fi, gr * fi + gi * fr))
            (ar, ai), (br, bi) = products
            odd_r, odd_i = ar - br, ai - bi
            odd_r, odd_i = odd_r * lr + odd_i * li, odd_i * lr - odd_r * li
            first_r, second_r = trade(ar + br, odd_r)
            first_i, second_i = trade(ai + bi, odd_i)
            back[e] = (first_r, first_i)
            back[e + 4] = (second_r, second_i)
        for c, (re, im) in enumerate(inverse_list(back)):
            u_ref[c, 0, rows, :] = re
            u_ref[c, 1, rows, :] = im

    halves = []
    for cc in range(8):
        columns = []
        for half in range(2):
            ur = u_ref[2 * cc + half, 0, :256, :]
            ui = u_ref[2 * cc + half, 1, :256, :]
            nr = now_ref[2 * cc + half, 0]
            ni = now_ref[2 * cc + half, 1]
            columns.append(jnp.concatenate([ur * nr + ui * ni, ui * nr - ur * ni], 0))
        out = dot3(t4_ref[...], jnp.concatenate(columns, 1))
        for half in range(2):
            lanes = slice(128 * half, 128 * half + 128)
            row = line_row(2 * cc + half)
            out_ref[pl.ds(row, 128, stride=40), :] = out[:128, lanes]
            out_ref[pl.ds(row + 8, 128, stride=40), :] = out[128:, lanes]
        if cc % 4 == 3:
            rows = pl.ds(cc // 4 * 16, 16)
            halves.append(
                pltpu.make_async_copy(
                    out_ref.reshape(128, 40, 128).at[:, rows], out_hbm.at[:, rows], sent.at[cc // 4]
                )
            )
            halves[-1].start()
    for copy in halves:
        copy.wait()


def middle(a, greens):
    t = tables()
    return pl.pallas_call(
        middle_kernel,
        in_specs=[spec_vmem()] + [spec_hbm()] * 9,
        out_specs=spec_hbm(),
        out_shape=pltpu.HBM((128, 32, 128), f32),
        scratch_shapes=[
            pltpu.VMEM((512, 768), bf16),
            pltpu.VMEM((2, 256, 128), f32),
            pltpu.VMEM((2, 256, 128), f32),
            pltpu.VMEM((2, 2, 2, 1024, 128), f32),
            pltpu.VMEM((2, 2, 8, 128), f32),
            pltpu.VMEM((256, 1536), bf16),
            pltpu.VMEM((16, 2, 264, 128), f32),
            pltpu.VMEM((16, 2, 256, 128), f32),
            pltpu.VMEM((5120, 128), f32),
            pltpu.VMEM((5120, 128), f32),
            pltpu.SemaphoreType.DMA((9,)),
            pltpu.SemaphoreType.DMA((2,)),
            pltpu.SemaphoreType.DMA,
        ],
        compiler_params=params(32),
        cost_estimate=cost(2 * 8 * 2 * 512 * 65536 * 3, 10 << 20),
        name="middle",
    )(
        a, *in_hbm(t["t3"], t["tw3"], t["step3"], *greens, t["lane3"], t["t4"])
    )


def x_inverse_kernel(
    a_ref, t5_hbm, tw_hbm, t6_hbm, out_hbm, t5_ref, tw_ref, t6_ref, spread_ref, out_ref, arrived,
    sent, moved,
):
    spread = pltpu.make_async_copy(
        a_ref.reshape(128, 32, 128), spread_ref.reshape(128, 40, 128).at[:, pl.ds(0, 32)], moved
    )
    spread.start()
    for copy in fetch((t5_hbm, tw_hbm, t6_hbm), (t5_ref, tw_ref, t6_ref), arrived):
        copy.wait()
    spread.wait()

    blocks = []
    for cc in range(8):
        columns = []
        for half in range(2):
            row = line_row(2 * cc + half)
            re = spread_ref[pl.ds(row, 128, stride=40), :]
            im = spread_ref[pl.ds(row + 8, 128, stride=40), :]
            columns.append(jnp.concatenate([re, im], 0))
        u = dot3(t5_ref[...], jnp.concatenate(columns, 1))
        rows = []
        for half in range(2):
            ur = u[:128, 128 * half : 128 * half + 128]
            ui = u[128:, 128 * half : 128 * half + 128]
            rows.append(
                jnp.concatenate(
                    [ur * tw_ref[0] - ui * tw_ref[1], ur * tw_ref[1] + ui * tw_ref[0]], 1
                )
            )
        out = dot3_nt(t6_ref[...], jnp.concatenate(rows, 0))
        for half in range(2):
            lanes = slice(128 * half, 128 * half + 128)
            for b0 in range(2):
                row = line_row(4 * cc + 2 * half + b0)
                out_ref[pl.ds(row, 32, stride=72), :] = out[64 * b0 : 64 * b0 + 32, lanes]
                out_ref[pl.ds(row + 8, 32, stride=72), :] = out[64 * b0 + 32 : 64 * b0 + 64, lanes]
        if cc % 2 == 1:
            rows = pl.ds(cc // 2 * 16, 16)
            blocks.append(
                pltpu.make_async_copy(
                    out_ref.reshape(32, 72, 128).at[:, rows], out_hbm.at[:, rows], sent.at[cc // 2]
                )
            )
            blocks[-1].start()
    for copy in blocks:
        copy.wait()


def x_inverse(a):
    t = tables()
    return pl.pallas_call(
        x_inverse_kernel,
        in_specs=[spec_vmem()] + [spec_hbm()] * 3,
        out_specs=spec_hbm(),
        out_shape=pltpu.HBM((32, 64, 128), f32),
        scratch_shapes=[
            pltpu.VMEM((256, 768), bf16),
            pltpu.VMEM((2, 128, 128), f32),
            pltpu.VMEM((128, 768), bf16),
            pltpu.VMEM((5120, 128), f32),
            pltpu.VMEM((2304, 128), f32),
            pltpu.SemaphoreType.DMA((3,)),
            pltpu.SemaphoreType.DMA((4,)),
            pltpu.SemaphoreType.DMA,
        ],
        compiler_params=params(12),
        cost_estimate=cost(2 * 2048 * 65536 * 4, 4 << 20),
        name="x_inverse",
    )(a, *in_hbm(t["t5"], t["tw5"], t["t6"]))


def residual_kernel(a_ref, contrast_ref, known_ref, out_ref):
    for tile in range(4):
        lanes = slice(128 * tile, 128 * tile + 128)
        scattered = []
        for part in range(2):
            rows = []
            for block in range(16):
                first = 256 * tile + block * 16 + part * 8
                rows.append(a_ref[first : first + 8, :])
            scattered.append(jnp.concatenate(rows, 0).T)
        cr = contrast_ref[0, :, lanes]
        ci = contrast_ref[1, :, lanes]
        out_ref[0, :, lanes] = cr * scattered[0] - ci * scattered[1] + known_ref[0, :, lanes]
        out_ref[1, :, lanes] = cr * scattered[1] + ci * scattered[0] + known_ref[1, :, lanes]


def residual_of(a, contrast, known):
    tile = pl.BlockSpec((2, 128, 512), lambda t: (0, 0, t))
    return pl.pallas_call(
        residual_kernel,
        grid=(2,),
        in_specs=[pl.BlockSpec((1024, 128), lambda t: (t, 0)), tile, tile],
        out_specs=tile,
        out_shape=jax.ShapeDtypeStruct((2, 128, 1024), f32),
        compiler_params=params(),
        cost_estimate=cost(0, 4 << 20),
        name="residual",
    )(a, contrast, known)


def pack_kernel(across, green_hbm, *refs):
    out_hbms, (green_ref, out_ref, arrived, sent) = refs[:-4], refs[-4:]
    flip, upper = place()
    column = jnp.where(upper == 1, 1 - across, across)
    lanes = pl.ds(pl.multiple_of(column * 128, 128), 128)
    lane = lax.broadcasted_iota(jnp.int32, (512, 128), 1)
    low = lane < 64
    pick = low == (flip == 0)
    pieces = [(part, pl.ds(first, 512)) for first in (0, 512) for part in range(2)]
    copies = fetch(
        [green_hbm.at[part, :, rows, lanes] for part, rows in pieces],
        [green_ref.at[part, :, rows] for part, rows in pieces],
        arrived,
    )
    leaving = []
    for k, (part, rows) in enumerate(pieces):
        copies[k].wait()
        first = green_ref[part, 0, rows]
        second = green_ref[part, 1, rows]
        straight = jnp.where(low, first, second)
        crossed = pltpu.roll(jnp.where(low, second, first), 64, 1)
        for core, value in enumerate(
            (jnp.where(pick, straight, crossed), jnp.where(pick, crossed, straight))
        ):
            out_ref[core, part, rows] = value
            target = out_hbms[0].at[core] if across else out_hbms[core]
            leaving.append(
                pltpu.make_async_copy(
                    out_ref.at[core, part, rows], target.at[part, rows], sent.at[k, core]
                )
            )
            leaving[-1].start()
    for copy in leaving:
        copy.wait()


def pack_green(green, across):
    if across:
        out_shape = [pltpu.HBM((2, 2, 1024, 128), f32)]
    else:
        out_shape = [pltpu.HBM((2, 1024, 128), f32)] * 2
    out = pl.pallas_call(
        functools.partial(pack_kernel, across),
        in_specs=[spec_hbm()],
        out_specs=[spec_hbm()] * len(out_shape),
        out_shape=out_shape,
        scratch_shapes=[
            pltpu.VMEM((2, 2, 1024, 128), f32),
            pltpu.VMEM((2, 2, 1024, 128), f32),
            pltpu.SemaphoreType.DMA((4,)),
            pltpu.SemaphoreType.DMA((4, 2)),
        ],
        compiler_params=params(12),
        cost_estimate=cost(0, 4 << 20),
        name="pack_far" if across else "pack_near",
    )(*in_hbm(green.reshape(2, 2, 1024, 256)))
    return out[0] if across else out


def second_kernel(pair_hbm, out_hbm, held_ref, arrived, sent):
    pieces = [(part, pl.ds(first, 512)) for part in range(2) for first in (0, 512)]
    copies = fetch(
        [pair_hbm.at[1, part, rows] for part, rows in pieces],
        [held_ref.at[part, rows] for part, rows in pieces],
        arrived,
    )
    leaving = []
    for k, (part, rows) in enumerate(pieces):
        copies[k].wait()
        leaving.append(
            pltpu.make_async_copy(held_ref.at[part, rows], out_hbm.at[part, rows], sent.at[k])
        )
        leaving[-1].start()
    for copy in leaving:
        copy.wait()


def second_of(values):
    return pl.pallas_call(
        second_kernel,
        in_specs=[spec_hbm()],
        out_specs=spec_hbm(),
        out_shape=pltpu.HBM(values.shape[1:], f32),
        scratch_shapes=[
            pltpu.VMEM((2, 1024, 128), f32),
            pltpu.SemaphoreType.DMA((4,)),
            pltpu.SemaphoreType.DMA((4,)),
        ],
        compiler_params=params(8),
        cost_estimate=cost(0, 2 << 20),
        name="second",
    )(*in_hbm(values))


def project_kernel(source_ref, ea_ref, eb_ref, row_ref, out_ref, lhs_ref, rhs_ref):
    @pl.when(pl.program_id(0) == 0)
    def _():
        re = source_ref[0]
        im = source_ref[1]
        for rows, cols, value in (
            (0, 0, re), (0, 1024, -im), (128, 0, im), (128, 1024, re),
        ):
            high, low = split(value)
            lhs_ref[0, rows : rows + 128, cols : cols + 1024] = high
            lhs_ref[1, rows : rows + 128, cols : cols + 1024] = low

    br = eb_ref[0]
    bi = eb_ref[1]
    for a in range(32):
        ar = ea_ref[0, a : a + 1, :]
        ai = ea_ref[1, a : a + 1, :]
        for part, value in ((0, ar * br - ai * bi), (1, ar * bi + ai * br)):
            high, low = split(value)
            rhs_ref[0, part * 1024 + a * 32 : part * 1024 + a * 32 + 32, :] = high
            rhs_ref[1, part * 1024 + a * 32 : part * 1024 + a * 32 + 32, :] = low
    inner = dot(lhs_ref[0], rhs_ref[0]) + (dot(lhs_ref[0], rhs_ref[1]) + dot(lhs_ref[1], rhs_ref[0]))
    ir = inner[:128]
    ii = inner[128:]
    fr = row_ref[0]
    fi = row_ref[1]
    pr = jnp.sum(fr * ir - fi * ii, axis=0, keepdims=True)
    pi_ = jnp.sum(fr * ii + fi * ir, axis=0, keepdims=True)
    out_ref[...] = jnp.concatenate([pr, pi_, jnp.zeros((6, pr.shape[1]), f32)], 0)


def project(source, ea, eb, rows):
    tile = 256
    whole = pl.BlockSpec((2, 128, 1024), lambda t: (0, 0, 0))
    return pl.pallas_call(
        project_kernel,
        grid=(R // tile,),
        in_specs=[
            whole,
            pl.BlockSpec((2, 32, tile), lambda t: (0, 0, t)),
            pl.BlockSpec((2, 32, tile), lambda t: (0, 0, t)),
            pl.BlockSpec((2, 128, tile), lambda t: (0, 0, t)),
        ],
        out_specs=pl.BlockSpec((8, tile), lambda t: (0, t)),
        out_shape=jax.ShapeDtypeStruct((8, R), f32),
        scratch_shapes=[pltpu.VMEM((2, 256, 2048), bf16), pltpu.VMEM((2, 2048, tile), bf16)],
        compiler_params=params(),
        cost_estimate=cost(2 * 256 * 2048 * 1024 * 3, 4 << 20),
        name="project",
    )(source, ea, eb, rows)


def backproject_kernel(weight_ref, ea_ref, eb_ref, out_ref, lhs_ref, rhs_ref):
    @pl.when(pl.program_id(0) == 0)
    def _():
        wr = weight_ref[0]
        wi = weight_ref[1]
        for rows, cols, value in (
            (0, 0, wr), (0, 1024, wi), (128, 0, wi), (128, 1024, -wr),
        ):
            high, low = split(value)
            lhs_ref[0, rows : rows + 128, cols : cols + 1024] = high
            lhs_ref[1, rows : rows + 128, cols : cols + 1024] = low

    br = eb_ref[0]
    bi = eb_ref[1]
    for a in range(8):
        ar = ea_ref[0, a : a + 1, :]
        ai = ea_ref[1, a : a + 1, :]
        for part, value in ((0, ar * br - ai * bi), (1, ar * bi + ai * br)):
            high, low = split(value)
            rhs_ref[0, a * 32 : a * 32 + 32, part * 1024 : part * 1024 + 1024] = high
            rhs_ref[1, a * 32 : a * 32 + 32, part * 1024 : part * 1024 + 1024] = low
    out = dot_nt(lhs_ref[0], rhs_ref[0]) + (
        dot_nt(lhs_ref[0], rhs_ref[1]) + dot_nt(lhs_ref[1], rhs_ref[0])
    )
    out_ref[0] = out[:128]
    out_ref[1] = out[128:]


def backproject(weights, ea, eb):
    whole = pl.BlockSpec((2, 128, 1024), lambda t: (0, 0, 0))
    return pl.pallas_call(
        backproject_kernel,
        grid=(4,),
        in_specs=[
            whole,
            pl.BlockSpec((2, 8, 1024), lambda t: (0, t, 0)),
            pl.BlockSpec((2, 32, 1024), lambda t: (0, 0, 0)),
        ],
        out_specs=pl.BlockSpec((2, 128, 256), lambda t: (0, 0, t)),
        out_shape=jax.ShapeDtypeStruct((2, 128, 1024), f32),
        scratch_shapes=[pltpu.VMEM((2, 256, 2048), bf16), pltpu.VMEM((2, 256, 2048), bf16)],
        compiler_params=params(),
        cost_estimate=cost(2 * 256 * 2048 * 1024 * 3, 4 << 20),
        name="backproject",
    )(weights, ea, eb)


def phase_pair(position, direction):
    phase = (wave_step * position)[:, None] * direction[None, :]
    return jnp.stack([jnp.cos(phase), -jnp.sin(phase)])


def sum_over(value, steps):
    def exchange(value, axis, size, strides):
        parts = [value] + [
            lax.ppermute(value, axis, [(j, j ^ stride) for j in range(size)]) for stride in strides
        ]
        while len(parts) > 1:
            parts = [parts[j] + parts[j + 1] for j in range(0, len(parts), 2)]
        return parts[0]

    for axis, size, strides in steps:
        value = exchange(value, axis, size, strides)
    return value


def local(sources, incident, contrast, green, angles, measured):
    wide = lax.axis_index("wide")
    narrow = lax.axis_index("narrow")
    source = sources[0]

    def partner(value, k):
        return lax.ppermute(value, "narrow", [(j, j ^ k) for j in range(NARROW)])

    lines = columns_major(source)
    lines, green = lax.optimization_barrier((lines, green))
    far = partner(pack_green(green, 1), 2)
    lines = lax.all_to_all(lines.reshape(WIDE, 64, 128), "wide", 0, 0, tiled=True)

    row_position = (wide * 128 + jnp.arange(128, dtype=jnp.int32)).astype(f32) - N // 2 + 0.5
    block_position = (narrow * 1024 + 32 * jnp.arange(32, dtype=jnp.int32)).astype(f32) - N // 2 + 0.5
    cell_position = jnp.arange(32, dtype=jnp.int32).astype(f32)
    rows = phase_pair(row_position, jnp.cos(angles))
    sine = jnp.sin(angles)
    ea = phase_pair(block_position, sine)
    eb = phase_pair(cell_position, sine)
    partial_value = project(source, ea, eb, rows)
    lines, partial_value = lax.optimization_barrier((lines, partial_value))
    lines = x_forward(lines.reshape(2048, 128))
    lines, partial_value = lax.optimization_barrier((lines, partial_value))
    lines = lax.all_to_all(lines.reshape(128, 32, 128), ("wide", "narrow"), 0, 0, tiled=True)

    total = sum_over(partial_value, [("wide", WIDE, (1, 2, 3)), ("wide", WIDE, (8, 16, 24))])
    total, green = lax.optimization_barrier((total, green))
    near = pack_green(green, 0)
    near_partner = partner(near[1], 1)
    total, far, near_partner = lax.optimization_barrier((total, far, near_partner))
    total = sum_over(total, [("narrow", NARROW, (1,))])
    greens = [near[0], near_partner, far, partner(second_of(far), 1)]
    total, lines = lax.optimization_barrier((total, lines))
    lines = middle(lines.reshape(4096, 128), greens)
    total, lines = lax.optimization_barrier((total, lines))
    lines = lax.all_to_all(lines.reshape(128, 32, 128), ("wide", "narrow"), 0, 0, tiled=True)
    total = sum_over(
        total, [(("wide", "narrow"), WIDE * NARROW, (2, 4 * NARROW, 4 * NARROW + 2))]
    )[:2]
    lines = x_inverse(lines.reshape(4096, 128))
    lines, contrast = lax.optimization_barrier((lines, contrast))
    known = jnp.stack(
        [
            contrast[0] * incident[0, 0] - contrast[1] * incident[0, 1] - source[0],
            contrast[0] * incident[0, 1] + contrast[1] * incident[0, 0] - source[1],
        ]
    )
    lines = lax.all_to_all(lines.reshape(WIDE, 64, 128), "wide", 0, 0, tiled=True)
    residual = residual_of(lines.reshape(2048, 128), contrast, known)

    data_residual = measured - total[None] * (1.0 / N)
    rho_real = data_residual[0, 0][None, :]
    rho_imag = data_residual[0, 1][None, :]
    scale = 1.0 / math.sqrt(R)
    weights = jnp.stack(
        [
            (rows[0] * rho_real + rows[1] * rho_imag) * scale,
            (rows[0] * rho_imag - rows[1] * rho_real) * scale,
        ]
    )
    back = backproject(weights, ea, eb)
    return (residual[None], back[None], data_residual)


def solution(mesh):
    placed = (
        P(None, None, "wide", "narrow"),
        P(None, None, "wide", "narrow"),
        P(None, "wide", "narrow"),
        P(None, "narrow", "wide"),
        P(),
        P(),
    )
    return jax.shard_map(
        local,
        mesh=mesh,
        in_specs=placed,
        out_specs=(P(None, None, "wide", "narrow"), P(None, None, "wide", "narrow"), P()),
        check_vma=False,
    )
```
